128 devices in a mesh: ctx: 16 (over x, z_lo, core), fsdp: 8 (over z_hi, y).
Axes of the slice: x: 4, y: 4, z: 4 (z_hi: 2, z_lo: 2; z = z_hi * 2 + z_lo), core: 2. Of those that a mesh axis runs over, the one named last changes fastest.
Arguments:
- tokens: bfloat16 [8, 2048, 768], P('fsdp', 'ctx'), may hold values from -6 to 6
- block_table: int32 [16, 2], replicated, may hold values from 0 to 31, as said below
- seq_ids: int32 [8, 2048], P('fsdp'), may hold values from 0 to 3, as said below
- w_query: bfloat16 [768, 768], P('fsdp'), may hold values from -0.21875 to 0.21875
- w_key: bfloat16 [768, 768], P('fsdp'), may hold values from -0.21875 to 0.21875
- w_value: bfloat16 [768, 768], P('fsdp'), may hold values from -0.21875 to 0.21875
- w_out: bfloat16 [768, 768], P('fsdp'), may hold values from -2.5 to 2.5
- w_gate: bfloat16 [768, 3072], P('fsdp'), may hold values from -0.21875 to 0.21875
- w_up: bfloat16 [768, 3072], P('fsdp'), may hold values from -0.21875 to 0.21875
- w_down: bfloat16 [3072, 768], P('fsdp'), may hold values from -0.109375 to 0.109375
- gain_attn: bfloat16 [768], P('fsdp'), may hold values from 0.25 to 1.75
- gain_mlp: bfloat16 [768], P('fsdp'), may hold values from 0.25 to 1.75
- cotangent: bfloat16 [8, 2048, 768], P('fsdp', 'ctx'), may hold values from -6 to 6
Outputs:
- result: bfloat16 [8, 2048, 768], P('fsdp', 'ctx')
- grad_tokens: bfloat16 [8, 2048, 768], P('fsdp', 'ctx')
- grad_query: float32 [768, 768], P('fsdp')
- grad_key: float32 [768, 768], P('fsdp')
- grad_value: float32 [768, 768], P('fsdp')
- grad_out: float32 [768, 768], P('fsdp')
- grad_gate: float32 [768, 3072], P('fsdp')
- grad_up: float32 [768, 3072], P('fsdp')
- grad_down: float32 [3072, 768], P('fsdp')
- grad_gain_attn: float32 [768], P('fsdp')
- grad_gain_mlp: float32 [768], P('fsdp')
The draws below stay inside these ranges and needn't reach their ends.
Inputs may be any that keep to these rules, and one draw needn't show every extreme that they name: `block_table`: row c holds b and 31 - b for some b below 16; every block number occurs once. `seq_ids`: read in the order of true positions, a stream's document numbers never fall; document 0 takes exactly the first 1024 positions, and every number up to 3 occurs.
All inputs are finite; a program needn't handle non-finite values.
Results may differ from the reference program's by a relative error of at most 0.025.
Values may be sent and summed in bfloat16 or wider, within the bound.
No kernel may reach another device: no remote copies, remote signals or barrier semaphores. Data moves between devices by JAX's collectives and lax.ppermute only.
A program may use at most 128 MiB of HBM per device.

```python
import math
import jax
import jax.numpy as jnp
from jax import lax

D = 768
HEADS = 12
FF = 3072
BLOCK = 64
DOCS = 4
NBLK = 32
SEQ = 2048
STREAMS = 8


def shared_order(key):
    return jax.random.permutation(key, NBLK // 2).astype(jnp.int32)


def draw_block_table(key, part):
    order = shared_order(key)
    return jnp.stack([order, NBLK - 1 - order], axis=1).astype(jnp.int32)


def draw_seq_ids(key, part):
    order = shared_order(key)
    key = jax.random.fold_in(key, 5)
    half_len = SEQ // 2

    def one_stream(stream_key):
        cuts = jax.random.permutation(stream_key, half_len - 1)[:DOCS - 2] + 1
        cuts = jnp.sort(cuts.astype(jnp.int32))
        places = jnp.arange(half_len, dtype=jnp.int32)
        later = 1 + jnp.sum((places[:, None] >= cuts[None, :]).astype(jnp.int32), axis=1)
        return jnp.concatenate([jnp.zeros((half_len,), jnp.int32), later.astype(jnp.int32)])
    true_ids = jax.vmap(one_stream)(jax.random.split(key, STREAMS))
    blocks = jnp.stack([order, NBLK - 1 - order], axis=1).reshape(-1)
    stored = (blocks[:, None] * BLOCK + jnp.arange(BLOCK, dtype=jnp.int32)[None, :]).reshape(-1)
    return true_ids[:, stored].astype(jnp.int32)


def block_levels(own_key, dims, shards, low, largest):
    loudness = 1.0
    for dim, shards_of in shards:
        steps = jax.random.uniform(jax.random.fold_in(jax.random.fold_in(own_key, 6), dim), (shards_of,), jnp.float32, low / len(shards), largest / len(shards))
        loudness = loudness * jnp.repeat(jnp.exp(steps), dims[dim] // shards_of).reshape((-1,) + (1,) * (len(dims) - 1 - dim))
    return loudness


def noise(key, extent, width, most, cuts=(), kind=jnp.bfloat16):
    factor_of = block_levels(key, extent, cuts, -0.22, 0.18) if cuts else 1.0
    entries = jax.random.normal(key, extent, jnp.float32) * width * factor_of
    return jnp.minimum(jnp.maximum(entries, -most), most).astype(kind)


def setup_inputs(seed: int = 0) -> dict:
    seeds = jax.random.split(jax.random.key(seed), 14)
    return {
        "tokens": noise(seeds[0], (STREAMS, SEQ, D), 1.0, 6.0, ((0, 8), (1, 16))),
        "block_table": draw_block_table(jax.random.fold_in(seeds[13], 71), 0),
        "seq_ids": draw_seq_ids(jax.random.fold_in(seeds[13], 71), 0),
        "w_query": noise(seeds[3], (D, D), D ** -0.5, 0.21875, ((0, 8),)),
        "w_key": noise(seeds[4], (D, D), D ** -0.5, 0.21875, ((0, 8),)),
        "w_value": noise(seeds[5], (D, D), D ** -0.5, 0.21875, ((0, 8),)),
        "w_out": noise(seeds[6], (D, D), (max(D * 16 // SEQ, 1)) ** -0.5, 2.5, ((0, 8),)),
        "w_gate": noise(seeds[7], (D, FF), D ** -0.5, 0.21875, ((0, 8),)),
        "w_up": noise(seeds[8], (D, FF), D ** -0.5, 0.21875, ((0, 8),)),
        "w_down": noise(seeds[9], (FF, D), FF ** -0.5, 0.109375, ((0, 8),)),
        "gain_attn": jnp.clip(1.0 + 0.15 * jax.random.normal(seeds[10], (D,), jnp.float32), 0.25, 1.75).astype(jnp.bfloat16),
        "gain_mlp": jnp.clip(1.0 + 0.15 * jax.random.normal(seeds[11], (D,), jnp.float32), 0.25, 1.75).astype(jnp.bfloat16),
        "cotangent": noise(seeds[12], (STREAMS, SEQ, D), 1.0, 6.0, ((0, 8), (1, 16))),
    }


EPS = 1e-05
THETA = 10000.0
HIGHEST = lax.Precision.HIGHEST

@jax.custom_vjp
def low(v):
    return lax.optimization_barrier(v.astype(jnp.bfloat16)).astype(jnp.float32)

@jax.custom_vjp
def low_back(v):
    return v

def low_keep(v):
    return (low(v), None)

def low_pass(kept, grad):
    return (grad,)

def back_keep(v):
    return (v, None)

def back_low(kept, grad):
    return (low(grad),)
low.defvjp(low_keep, low_pass)
low_back.defvjp(back_keep, back_low)

def matmul(left_side, right_side):
    return jnp.dot(left_side, right_side, precision=HIGHEST, preferred_element_type=jnp.float32)

def rms_norm(values, gains):
    inverse = lax.rsqrt(lax.optimization_barrier(jnp.mean(values * values, axis=-1, keepdims=True)) + EPS)
    return values * inverse * gains

def rotary(values, places):
    row_count = values.shape[0]
    head_dim = values.shape[1] // HEADS
    half_dim = head_dim // 2
    frequency = jnp.power(THETA, -(jnp.arange(half_dim, dtype=jnp.float32) * 2.0) / head_dim)
    angles = places.astype(jnp.float32)[:, None] * frequency[None, :]
    cosine = jnp.cos(angles)[:, None, :]
    sine = jnp.sin(angles)[:, None, :]
    by_head = values.reshape(row_count, HEADS, head_dim)
    first_half = by_head[..., :half_dim]
    second_half = by_head[..., half_dim:]
    turned = jnp.concatenate([first_half * cosine - second_half * sine, second_half * cosine + first_half * sine], axis=-1)
    return turned.reshape(row_count, HEADS * head_dim)

def stored_positions(block_table):
    blocks = block_table.reshape(-1).astype(jnp.int32)
    offsets = jnp.arange(BLOCK, dtype=jnp.int32)
    return (blocks[:, None] * BLOCK + offsets[None, :]).reshape(-1)

def attention(queries, keys_rot, values, places, doc_ids):
    length = queries.shape[0]
    head_dim = queries.shape[1] // HEADS
    query_block = math.gcd(length, 512)
    block_count = length // query_block
    key_heads = keys_rot.reshape(length, HEADS, head_dim)
    value_heads = values.reshape(length, HEADS, head_dim)

    def one_block(inputs):
        query_rows, query_places, query_ids = inputs
        query_heads = query_rows.reshape(query_block, HEADS, head_dim)
        scores = jnp.einsum('qhd,khd->hqk', query_heads, key_heads, precision=HIGHEST) * head_dim ** (-0.5)
        scores = low_back(scores)
        allowed = (places[None, :] <= query_places[:, None]) & (doc_ids[None, :] == query_ids[:, None])
        scores = jnp.where(allowed[None], scores, -1e+30)
        row_max = lax.optimization_barrier(jnp.max(scores, axis=-1, keepdims=True))
        powers = jnp.exp(scores - row_max)
        probs = low(powers / lax.optimization_barrier(jnp.sum(powers, axis=-1, keepdims=True)))
        combined = jnp.einsum('hqk,khd->qhd', probs, value_heads, precision=HIGHEST)
        return combined.reshape(query_block, HEADS * head_dim)
    outputs = lax.map(jax.checkpoint(one_block), (queries.reshape(block_count, query_block, -1), places.reshape(block_count, query_block), doc_ids.reshape(block_count, query_block)))
    return outputs.reshape(length, -1)

def layer(stream, doc_ids, places, w_query, w_key, w_value, w_out, w_gate, w_up, w_down, gain_attn, gain_mlp):
    normed = low(rms_norm(stream, gain_attn))
    queries = low(rotary(low_back(matmul(normed, w_query)), places))
    keys_rot = low(rotary(low_back(matmul(normed, w_key)), places))
    values = low(low_back(matmul(normed, w_value)))
    attended = low(low_back(attention(queries, keys_rot, values, places, doc_ids)))
    middle = stream + low_back(matmul(attended, w_out))
    normed_mlp = low(rms_norm(middle, gain_mlp))
    gate_pre = low_back(matmul(normed_mlp, w_gate))
    up_pre = low_back(matmul(normed_mlp, w_up))
    hidden = low(gate_pre * jax.nn.sigmoid(gate_pre) * up_pre)
    return middle + low_back(matmul(hidden, w_down))

def reference(tokens, block_table, seq_ids, w_query, w_key, w_value, w_out, w_gate, w_up, w_down, gain_attn, gain_mlp, cotangent):
    places = stored_positions(block_table)
    weights = tuple((weight_in.astype(jnp.float32) for weight_in in (w_query, w_key, w_value, w_out, w_gate, w_up, w_down, gain_attn, gain_mlp)))

    def forward(streams, params):

        def one_stream(inputs):
            rows_in, ids_in = inputs
            return layer(rows_in, ids_in, places, *params)
        return lax.map(jax.checkpoint(one_stream), (streams, seq_ids))
    result, pullback = jax.vjp(forward, tokens.astype(jnp.float32), weights)
    grad_tokens, grad_weights = pullback(cotangent.astype(jnp.float32))
    return (result.astype(jnp.bfloat16), grad_tokens.astype(jnp.bfloat16), grad_weights[0], grad_weights[1], grad_weights[2], grad_weights[3], grad_weights[4], grad_weights[5], grad_weights[6], grad_weights[7], grad_weights[8])
```

```python
import functools

import jax
import jax.numpy as jnp
from jax import lax
from jax.experimental import pallas as pl
from jax.experimental.pallas import tpu as pltpu
from jax.sharding import PartitionSpec as P

HEADS = 12
EPS = 1e-05
THETA = 10000.0
WIDTH = 768
HEAD = 64
HALF = 32
SEQ = 2048
BLOCK = 64
CHUNK = 256
HALF_SEQ = 1024
F32 = jnp.float32
BF16 = jnp.bfloat16

QUADS = [[4 * i + j for j in range(4)] for i in range(4)]
COLUMNS = [[j + 4 * i for i in range(4)] for j in range(4)]


def dot(left, right, left_dim=1, right_dim=0):
    return lax.dot_general(
        left, right, (((left_dim,), (right_dim,)), ((), ())), preferred_element_type=F32
    )


def turn(block, cosine, sine, backward):
    first, second = block[:HALF], block[HALF:]
    if backward:
        return jnp.concatenate([first * cosine + second * sine, second * cosine - first * sine], 0)
    return jnp.concatenate([first * cosine - second * sine, second * cosine + first * sine], 0)


def masked(scores, half, part, id_row, id_column, other):
    keys = scores.shape[0]
    base = keys - CHUNK
    row = lax.broadcasted_iota(jnp.int32, (CHUNK, CHUNK), 0)
    column = lax.broadcasted_iota(jnp.int32, (CHUNK, CHUNK), 1)
    if half == 1:
        same = id_column[:keys] == id_row[:, part * CHUNK : (part + 1) * CHUNK]
        scores = jnp.where(same, scores, other)
    last = jnp.where(row <= column, scores[base:], other)
    return last if base == 0 else jnp.concatenate([scores[:base], last], 0)


def forward_kernel(
    inverse, x_ref, w_ref, gain_ref, cos_ref, sin_ref, id_row, id_column,
    out_ref, h_ref, q_ref, k_ref, v_ref, krow_ref, o_ref, lse_ref, wt_ref,
):
    wt_ref[...] = w_ref[...].T

    def prepare(i, _):
        rows = [
            x_ref[pl.ds(pl.multiple_of(inverse[4 * i + j] * BLOCK, BLOCK), BLOCK), :]
            for j in range(4)
        ]
        x = jnp.concatenate(rows, 0).astype(F32)
        scale = lax.rsqrt(jnp.mean(x * x, axis=-1, keepdims=True) + EPS)
        h = (x * scale * gain_ref[...]).astype(BF16)
        h_ref[i] = h
        qkv = dot(wt_ref[...], h, 1, 1)
        cosine, sine = cos_ref[i], sin_ref[i]
        q_ref[i] = (turn(qkv[:HEAD], cosine, sine, False).astype(BF16) * 0.125).astype(BF16)
        k = turn(qkv[HEAD : 2 * HEAD], cosine, sine, False).astype(BF16)
        k_ref[i] = k
        krow_ref[i] = k.T
        v_ref[i] = qkv[2 * HEAD :].astype(BF16)
        return 0

    lax.fori_loop(0, SEQ // CHUNK, prepare, 0)
    for half in range(2):
        for part in range(4):
            at = 4 * half + part
            keys = (part + 1) * CHUNK
            k = krow_ref[4 * half : 4 * half + part + 1].reshape(keys, HEAD)
            s = dot(k, q_ref[at])
            s = masked(s, half, part, id_row[...], id_column[...], -1e30)
            top = jnp.max(s, axis=0, keepdims=True)
            p = jnp.exp(s - top)
            total = jnp.sum(p, axis=0, keepdims=True)
            low = p.astype(BF16)
            o = dot(v_ref[4 * half], low[:CHUNK])
            for j in range(1, part + 1):
                o += dot(v_ref[4 * half + j], low[j * CHUNK : (j + 1) * CHUNK])
            o_ref[at] = o / total
            lse_ref[at] = top + jnp.log(total)
    for b in range(16):
        flat = inverse[b]
        upper = 15 - b
        lo = o_ref[b // 4, :, (b % 4) * BLOCK : (b % 4 + 1) * BLOCK]
        up = o_ref[4 + upper // 4, :, (upper % 4) * BLOCK : (upper % 4 + 1) * BLOCK]
        tile = jnp.concatenate([lo, up], 1)
        turned = jnp.concatenate([up, lo], 1)
        out_ref[flat // 2] = jnp.where(flat % 2 == 0, tile, turned).astype(BF16)


def backward_kernel(
    inverse, do_ref, h_ref, q_ref, k_ref, v_ref, krow_ref, o_ref, lse_ref, cos_ref, sin_ref,
    id_row, id_column, out_ref, grad_ref, d_ref, dk_ref, dv_ref, dot_ref, vrow_ref, wt_ref,
):
    for b in range(16):
        flat = inverse[b]
        upper = 15 - b
        tile = do_ref[flat // 2].astype(F32)
        swapped = jnp.concatenate([tile[:, BLOCK:], tile[:, :BLOCK]], 1)
        tile = jnp.where(flat % 2 == 0, tile, swapped).astype(BF16)
        dot_ref[b // 4, :, (b % 4) * BLOCK : (b % 4 + 1) * BLOCK] = tile[:, :BLOCK]
        dot_ref[4 + upper // 4, :, (upper % 4) * BLOCK : (upper % 4 + 1) * BLOCK] = tile[:, BLOCK:]
    for half in range(2):
        for part in range(4):
            at = 4 * half + part
            vrow_ref[at] = v_ref[at].T
            keys = (part + 1) * CHUNK
            first = 4 * half
            k = krow_ref[first : first + part + 1].reshape(keys, HEAD)
            v = vrow_ref[first : first + part + 1].reshape(keys, HEAD)
            q = q_ref[at]
            do = dot_ref[at]
            delta = jnp.sum(do.astype(F32) * o_ref[at], axis=0, keepdims=True)
            s = dot(k, q) - lse_ref[at]
            p = jnp.exp(masked(s, half, part, id_row[...], id_column[...], -1e30))
            ds = (p * (dot(v, do) - delta)).astype(BF16)
            dv = dot(p.astype(BF16), do.T).reshape(part + 1, CHUNK, HEAD)
            dk = dot(ds, q.T).reshape(part + 1, CHUNK, HEAD)
            if part:
                dv_ref[first : first + part] += dv[:part]
                dk_ref[first : first + part] += dk[:part]
            dv_ref[at] = dv[part]
            dk_ref[at] = dk[part]
            dq = dot(k_ref[first], ds[:CHUNK])
            for j in range(1, part + 1):
                dq += dot(k_ref[first + j], ds[j * CHUNK : (j + 1) * CHUNK])
            d_ref[at, :HEAD] = turn(dq * 0.125, cos_ref[at], sin_ref[at], True).astype(BF16)
    for at in range(8):
        dk = turn(dk_ref[at].T, cos_ref[at], sin_ref[at], True)
        d_ref[at, HEAD : 2 * HEAD] = dk.astype(BF16)
        d_ref[at, 2 * HEAD :] = dv_ref[at].T.astype(BF16)
        part = dot(d_ref[at], h_ref[at])
        wt_ref[...] = part if at == 0 else wt_ref[...] + part
    grad_ref[...] = wt_ref[...].T.astype(BF16)
    for b in range(16):
        flat = inverse[b]
        upper = 15 - b
        lo = d_ref[b // 4, :, (b % 4) * BLOCK : (b % 4 + 1) * BLOCK].astype(F32)
        up = d_ref[4 + upper // 4, :, (upper % 4) * BLOCK : (upper % 4 + 1) * BLOCK].astype(F32)
        tile = jnp.concatenate([lo, up], 1)
        turned = jnp.concatenate([up, lo], 1)
        out_ref[flat // 2] = jnp.where(flat % 2 == 0, tile, turned).astype(BF16)


VMEM = pl.BlockSpec(memory_space=pltpu.VMEM)
SMEM = pl.BlockSpec(memory_space=pltpu.SMEM)
CHUNKS = SEQ // CHUNK


def run_forward(inverse, x, w, gain, cosine, sine, id_row, id_column):
    shape = jax.ShapeDtypeStruct
    return pl.pallas_call(
        forward_kernel,
        out_shape=(
            shape((16, HEAD, 2 * BLOCK), BF16),
            shape((CHUNKS, CHUNK, WIDTH), BF16),
            shape((CHUNKS, HEAD, CHUNK), BF16),
            shape((CHUNKS, HEAD, CHUNK), BF16),
            shape((CHUNKS, HEAD, CHUNK), BF16),
            shape((CHUNKS, CHUNK, HEAD), BF16),
            shape((CHUNKS, HEAD, CHUNK), F32),
            shape((CHUNKS, 1, CHUNK), F32),
        ),
        in_specs=[SMEM] + [VMEM] * 7,
        out_specs=(VMEM,) * 8,
        scratch_shapes=[pltpu.VMEM((3 * HEAD, WIDTH), BF16)],
        compiler_params=pltpu.CompilerParams(vmem_limit_bytes=48 << 20),
        name="attention_forward",
    )(inverse, x, w, gain, cosine, sine, id_row, id_column)


def run_backward(inverse, do, kept, cosine, sine, id_row, id_column):
    shape = jax.ShapeDtypeStruct
    return pl.pallas_call(
        backward_kernel,
        out_shape=(
            shape((16, 3 * HEAD, 2 * BLOCK), BF16),
            shape((WIDTH, 3 * HEAD), BF16),
        ),
        in_specs=[SMEM] + [VMEM] * 12,
        out_specs=(VMEM,) * 2,
        scratch_shapes=[
            pltpu.VMEM((CHUNKS, 3 * HEAD, CHUNK), BF16),
            pltpu.VMEM((CHUNKS, CHUNK, HEAD), F32),
            pltpu.VMEM((CHUNKS, CHUNK, HEAD), F32),
            pltpu.VMEM((CHUNKS, HEAD, CHUNK), BF16),
            pltpu.VMEM((CHUNKS, CHUNK, HEAD), BF16),
            pltpu.VMEM((3 * HEAD, WIDTH), F32),
        ],
        compiler_params=pltpu.CompilerParams(vmem_limit_bytes=48 << 20),
        name="attention_backward",
    )(inverse, do, *kept, cosine, sine, id_row, id_column)


def spread(part, axis, count):
    whole = jnp.broadcast_to(part[None], (count,) + part.shape)
    return lax.all_to_all(whole, axis, 0, 0)


def quad_sum(partial, rank):
    core, low = rank % 2, rank // 2
    by_rank = partial.reshape(2, 2, *partial.shape[1:])
    keep = lax.dynamic_index_in_dim(by_rank, core, 1, keepdims=False)
    send = lax.dynamic_index_in_dim(by_rank, 1 - core, 1, keepdims=False)
    got = lax.ppermute(send, "ctx", [(i, i ^ 1) for i in range(16)])
    both = keep.astype(F32) + got.astype(F32)
    keep = lax.dynamic_index_in_dim(both, low, 0, keepdims=False)
    send = lax.dynamic_index_in_dim(both, 1 - low, 0, keepdims=False).astype(BF16)
    got = lax.ppermute(send, "ctx", [(i, i ^ 2) for i in range(16)])
    return keep + got.astype(F32)


def norm_back(grad_normed, normal_rows, inverse, gains):
    scaled = grad_normed * gains
    return inverse * (scaled - normal_rows * jnp.mean(scaled * normal_rows, axis=-1, keepdims=True))


def local(
    tokens, block_table, seq_ids, w_query, w_key, w_value, w_out, w_gate, w_up, w_down,
    gain_attn, gain_mlp, cotangent,
):
    index = lax.axis_index("ctx")
    rank = index % 4
    column = index // 4
    head = 3 * rank + jnp.minimum(column, 2)

    x_all = lax.all_gather(tokens[0], "ctx", axis=0, tiled=True)
    heads = [
        lax.dynamic_slice_in_dim(w, head * HEAD, HEAD, 1) for w in (w_query, w_key, w_value)
    ]
    gains_own = jnp.stack([gain_attn, gain_mlp])
    unit = jnp.concatenate(
        [
            jnp.concatenate(heads[:2], 1),
            jnp.concatenate([heads[2][:48], heads[2][48:]], 1),
            jnp.pad(gains_own, ((0, 14), (0, 32))),
        ],
        0,
    )
    first = spread(unit, "fsdp", 8)
    w_head = jnp.concatenate(
        [
            first[:, :96],
            jnp.concatenate([first[:, 96:144, :HEAD], first[:, 96:144, HEAD:]], 1),
        ],
        2,
    ).reshape(WIDTH, 3 * HEAD)
    gains = first[:, 144:146, :96].transpose(1, 0, 2).reshape(2, WIDTH).astype(F32)
    gain_one, gain_two = gains[:1], gains[1:]

    def own_units(w):
        return lax.dynamic_index_in_dim(w.reshape(96, 8, 4, 96), rank, 2, keepdims=False).reshape(
            96, WIDTH
        )

    unit = jnp.concatenate(
        [
            own_units(w_gate),
            own_units(w_up),
            lax.dynamic_slice_in_dim(w_down, rank * 96, 96, 0),
            lax.dynamic_slice_in_dim(w_out, rank * 24, 24, 0),
        ],
        0,
    )
    second = spread(unit, "fsdp", 8)
    gate = second[:, :96].reshape(WIDTH, WIDTH)
    up = second[:, 96:192].reshape(WIDTH, WIDTH)
    down = second[:, 192:288].reshape(WIDTH, WIDTH)
    out_full = lax.all_gather(second[:, 288:], "ctx", axis=0, axis_index_groups=QUADS)
    out_full = out_full.transpose(1, 0, 2, 3).reshape(WIDTH, WIDTH)
    w_heads = lax.all_gather(w_head, "ctx", axis=0, axis_index_groups=COLUMNS)[:3]
    grad_quad = lax.all_gather(cotangent[0], "ctx", axis=0, tiled=True, axis_index_groups=QUADS)

    blocks = block_table.reshape(-1)
    numbers = jnp.arange(32, dtype=jnp.int32)
    inverse = jnp.sum(
        jnp.where(blocks[None, :] == numbers[:, None], numbers[None, :], 0), axis=1
    ).astype(jnp.int32)
    ids = seq_ids[0].reshape(32, BLOCK)
    hits = (inverse[16:, None] == numbers[None, :]).astype(jnp.int32)
    ids = jnp.sum(hits[:, :, None] * ids[None], axis=1).reshape(HALF_SEQ)
    id_row, id_column = ids.reshape(1, HALF_SEQ), ids.reshape(HALF_SEQ, 1)
    frequency = jnp.power(THETA, -(jnp.arange(HALF, dtype=F32) * 2.0) / HEAD)
    angles = (
        jnp.arange(SEQ, dtype=F32).reshape(CHUNKS, 1, CHUNK) * frequency[None, :, None]
    )
    cosine, sine = jnp.cos(angles), jnp.sin(angles)

    o_packed, *kept = run_forward(
        inverse, x_all, w_head, gain_one, cosine, sine, id_row, id_column
    )
    o_rows = lax.all_to_all(
        o_packed.reshape(4, 4, HEAD, 128), "ctx", 0, 0, axis_index_groups=COLUMNS
    )[:3]
    o_quad = lax.all_gather(o_rows, "ctx", axis=0, axis_index_groups=QUADS)
    ob = o_quad.transpose(2, 0, 1, 3, 4).reshape(4, WIDTH, 128)

    x_quad = lax.dynamic_slice_in_dim(x_all, column * 512, 512, 0).astype(F32)
    middle = x_quad + jnp.einsum("cfr,fd->crd", ob, out_full, preferred_element_type=F32).reshape(
        512, WIDTH
    )
    inverse_two = lax.rsqrt(jnp.mean(middle * middle, axis=-1, keepdims=True) + EPS)
    normal_two = middle * inverse_two
    h2 = (normal_two * gain_two).astype(BF16)
    g = dot(h2, gate)
    u = dot(h2, up)
    sigma = jax.nn.sigmoid(g)
    swish = g * sigma
    a = (swish * u).astype(BF16)
    da = dot(grad_quad, down, 1, 1)
    dg = (da * u * (sigma + swish * (1.0 - sigma))).astype(BF16)
    du = (da * swish).astype(BF16)
    dh2 = (dot(dg, gate, 1, 1) + dot(du, up, 1, 1)).astype(BF16)
    dh2 = quad_sum(dh2.reshape(4, 128, WIDTH), rank)
    z = dot(a, down).astype(BF16)

    def own_rows(values):
        return lax.dynamic_slice_in_dim(values, rank * 128, 128, 0)

    middle_own = own_rows(middle)
    dy1 = cotangent[0].astype(F32) + norm_back(
        dh2, own_rows(normal_two), own_rows(inverse_two), gain_two
    )
    dyb = dy1.astype(BF16)
    do = dot(out_full, dyb, 1, 1).astype(BF16).reshape(4, 3, HEAD, 128).transpose(1, 0, 2, 3)
    do = jnp.concatenate([do, do[:1]], 0).reshape(16, HEAD, 128)
    do = lax.all_to_all(do, "ctx", 0, 0)

    d_packed, grad_head = run_backward(inverse, do, kept, cosine, sine, id_row, id_column)

    grad_gate = dot(h2, dg, 0, 0).astype(BF16).reshape(8, 96, WIDTH)
    grad_up = dot(h2, du, 0, 0).astype(BF16).reshape(8, 96, WIDTH)
    grad_down = dot(a, grad_quad, 0, 0).astype(BF16).reshape(8, 96, WIDTH)
    ff = jnp.concatenate([grad_gate, grad_up, grad_down], 1)
    ff = ff.reshape(8, 4, 72, WIDTH).transpose(1, 0, 2, 3)
    ff = lax.psum_scatter(
        ff, "ctx", scatter_dimension=0, tiled=True, axis_index_groups=COLUMNS
    )[0]
    ff = jnp.sum(lax.all_to_all(ff, "fsdp", 0, 0).astype(F32), axis=0).astype(BF16)
    ff = lax.all_gather(ff, "ctx", axis=0).reshape(4, 4, 72, WIDTH)
    ff = ff.transpose(1, 0, 2, 3).reshape(4, 288, WIDTH).astype(F32)

    def spread_units(part):
        return part.reshape(4, 96, 8, 96).transpose(1, 2, 0, 3).reshape(96, 4 * WIDTH)

    total_gate = spread_units(ff[:, :96])
    total_up = spread_units(ff[:, 96:192])
    total_down = ff[:, 192:].reshape(384, WIDTH)

    dyb_columns = lax.all_to_all(
        dyb.reshape(128, 4, 192).transpose(1, 0, 2), "ctx", 0, 0, axis_index_groups=QUADS
    )
    grad_out = jnp.einsum("cfr,crk->fk", ob, dyb_columns, preferred_element_type=F32).astype(BF16)
    small = jnp.concatenate([grad_head, grad_out], 1).reshape(8, 96, 384)
    small = jnp.sum(lax.all_to_all(small, "fsdp", 0, 0).astype(F32), axis=0).astype(BF16)
    small = lax.all_gather(small, "ctx", axis=0).reshape(4, 4, 96, 384).astype(F32)
    by_head = small[:3, :, :, :192].reshape(3, 4, 96, 3, HEAD).transpose(3, 2, 1, 0, 4)
    total_query, total_key, total_value = by_head.reshape(3, 96, WIDTH)
    total_out = jnp.sum(small[..., 192:], axis=0).transpose(1, 0, 2).reshape(96, WIDTH)

    d_rows = lax.all_to_all(
        d_packed.reshape(4, 4, 192, 128), "ctx", 0, 0, axis_index_groups=COLUMNS
    )[:3]
    dh1 = jnp.einsum("xcfr,xdf->crd", d_rows, w_heads, preferred_element_type=F32).astype(BF16)
    dh1 = quad_sum(dh1, rank)
    stream = tokens[0].astype(F32)
    inverse_one = lax.rsqrt(jnp.mean(stream * stream, axis=-1, keepdims=True) + EPS)
    grad_stream = dy1 + norm_back(dh1, stream * inverse_one, inverse_one, gain_one)

    result = middle_own + quad_sum(z.reshape(4, 128, WIDTH), rank)

    def along(w, grad):
        return jnp.sum(w.astype(F32) * grad, axis=1)

    total_gain_one = (
        along(w_query, total_query) + along(w_key, total_key) + along(w_value, total_value)
    ) / gain_attn.astype(F32)
    total_gain_two = (along(w_gate, total_gate) + along(w_up, total_up)) / gain_mlp.astype(F32)
    return (
        result[None].astype(BF16),
        grad_stream[None].astype(BF16),
        total_query,
        total_key,
        total_value,
        total_out,
        total_gate,
        total_up,
        total_down,
        total_gain_one,
        total_gain_two,
    )


def solution(mesh):
    rows = P("fsdp", "ctx", None)
    weight = P("fsdp", None)
    return jax.shard_map(
        local,
        mesh=mesh,
        in_specs=(rows, P(), weight) + (weight,) * 7 + (P("fsdp"), P("fsdp"), rows),
        out_specs=(rows, rows) + (weight,) * 7 + (P("fsdp"), P("fsdp")),
        check_vma=False,
    )
```

```python
import jax
import jax.numpy as jnp
from jax import lax
from jax.experimental import pallas as pl
from jax.experimental.pallas import tpu as pltpu
from jax.sharding import PartitionSpec as P

EPS = 1e-05
THETA = 10000.0
WIDTH = 768
HEAD = 64
HALF = 32
SEQ = 2048
BLOCK = 64
CHUNK = 256
CHUNKS = SEQ // CHUNK
HALF_SEQ = SEQ // 2
F32 = jnp.float32
BF16 = jnp.bfloat16

QUADS = [[4 * i + j for j in range(4)] for i in range(4)]
COLUMNS = [[j + 4 * i for i in range(4)] for j in range(4)]
SAME_CORE = [[j + 2 * i for i in range(8)] for j in range(2)]
FOUR_CHIPS = [[8 * g + j + 2 * i for i in range(4)] for g in range(2) for j in range(2)]
RING = [(0, 0), (1, 0), (0, 3), (0, 1), (1, 3), (1, 1), (0, 2), (1, 2)]

VMEM = pl.BlockSpec(memory_space=pltpu.VMEM)
SMEM = pl.BlockSpec(memory_space=pltpu.SMEM)
ANY = pl.BlockSpec(memory_space=pl.ANY)
SHAPE = jax.ShapeDtypeStruct


def cost(microseconds):
    return pl.CostEstimate(
        flops=int(microseconds * 1.1e9), bytes_accessed=int(microseconds * 3.6e6), transcendentals=0
    )


def after(value, *others):
    return lax.optimization_barrier((value, others))[0]


def dot(left, right, left_dim=1, right_dim=0):
    return lax.dot_general(
        left, right, (((left_dim,), (right_dim,)), ((), ())), preferred_element_type=F32
    )


def turn(block, cosine, sine, backward):
    first, second = block[:HALF], block[HALF:]
    if backward:
        return jnp.concatenate([first * cosine + second * sine, second * cosine - first * sine], 0)
    return jnp.concatenate([first * cosine - second * sine, second * cosine + first * sine], 0)


def normalise(x):
    scale = lax.rsqrt(jnp.mean(x * x, axis=-1, keepdims=True) + EPS)
    return x * scale, scale


def masked(scores, half, part, id_row, id_column, other):
    keys = scores.shape[0]
    base = keys - CHUNK
    row = lax.broadcasted_iota(jnp.int32, (CHUNK, CHUNK), 0)
    column = lax.broadcasted_iota(jnp.int32, (CHUNK, CHUNK), 1)
    if half == 1:
        same = id_column[:keys] == id_row[:, part * CHUNK : (part + 1) * CHUNK]
        scores = jnp.where(same, scores, other)
    last = jnp.where(row <= column, scores[base:], other)
    return last if base == 0 else jnp.concatenate([scores[:base], last], 0)


def swap_lanes(tile):
    return jnp.concatenate([tile[:, BLOCK:], tile[:, :BLOCK]], 1)


def sort_tiles(inverse, in_ref, out_ref):
    for b in range(16):
        flat = inverse[b]
        upper = 15 - b
        tile = in_ref[flat // 2].astype(F32)
        tile = jnp.where(flat % 2 == 0, tile, swap_lanes(tile)).astype(BF16)
        out_ref[b // 4, :, (b % 4) * BLOCK : (b % 4 + 1) * BLOCK] = tile[:, :BLOCK]
        out_ref[4 + upper // 4, :, (upper % 4) * BLOCK : (upper % 4 + 1) * BLOCK] = tile[:, BLOCK:]


def pack_heads_kernel(q_ref, k_ref, v_ref, one_ref, two_ref, out_ref):
    rank = lax.axis_index("ctx") & 3
    column = lax.broadcasted_iota(jnp.int32, (96, 64), 1)
    one = jnp.broadcast_to(one_ref[...].astype(F32), (128, 96)).T[:, :64]
    two = jnp.broadcast_to(two_ref[...].astype(F32), (128, 96)).T[:, :64]
    gains = jnp.where(column == 0, one, jnp.where(column == 1, two, 0.0)).astype(BF16)
    for r in range(4):

        @pl.when(rank == r)
        def _():
            lanes = slice(192 * r, 192 * (r + 1))
            unit = jnp.concatenate([q_ref[:, lanes], k_ref[:, lanes], v_ref[:, lanes], gains], 1)
            for f in range(8):
                out_ref[f] = unit


def run_pack_heads(query, key, value, gain_one, gain_two):
    return pl.pallas_call(
        pack_heads_kernel,
        out_shape=SHAPE((8, 96, 640), BF16),
        in_specs=[VMEM] * 5,
        out_specs=VMEM,
        compiler_params=pltpu.CompilerParams(vmem_limit_bytes=60 << 20),
        cost_estimate=cost(2),
        name="pack_heads",
    )(query, key, value, gain_one.reshape(1, 96), gain_two.reshape(1, 96))


def pack_units_kernel(gate_ref, up_ref, down_ref, wout_ref, _, out_ref):
    index = lax.axis_index("ctx")
    member = index & 7
    for m in range(8):

        @pl.when(member == m)
        def _():
            parts = [
                ref[:, 384 * f + 48 * m : 384 * f + 48 * (m + 1)]
                for ref in (gate_ref, up_ref)
                for f in range(8)
            ]
            out_ref[:96] = jnp.concatenate(parts, 1)

    out_ref[96:144] = down_ref[pl.ds(pl.multiple_of(member * 48, 16), 48), :]
    out_ref[144:] = wout_ref[...]


def run_pack_units(gate, up, down, wout, after):
    return pl.pallas_call(
        pack_units_kernel,
        out_shape=SHAPE((240, WIDTH), BF16),
        in_specs=[VMEM] * 4 + [ANY],
        out_specs=VMEM,
        compiler_params=pltpu.CompilerParams(vmem_limit_bytes=60 << 20),
        cost_estimate=cost(2.4),
        name="pack_units",
    )(gate, up, down, wout, after)


def project_kernel(
    place, w_ref, x0_ref, x1_ref, x2_ref, x3_ref, cos_ref, sin_ref,
    out0_ref, out1_ref, out2_ref, out3_ref, wt_ref, out_ref,
):
    wt_ref[...] = w_ref[...].T
    gain = wt_ref[576:592].astype(F32)[:1]
    for d, block in enumerate((x0_ref, x1_ref, x2_ref, x3_ref)):
        c = place[11] ^ d
        normal, _ = normalise(block[...].astype(F32))
        h = (normal * gain).astype(BF16)
        qkv = dot(wt_ref[:576], h, 1, 1)
        cosine, sine = cos_ref[c], sin_ref[c]
        for j in range(3):
            at = HEAD * j
            q = (turn(qkv[at : at + HEAD], cosine, sine, False).astype(BF16) * 0.125).astype(BF16)
            k = turn(qkv[192 + at : 192 + at + HEAD], cosine, sine, False).astype(BF16)
            v = qkv[384 + at : 384 + at + HEAD].astype(BF16)
            for target in (2, 3) if j == 2 else (j,):
                away = (target - place[12]) & 3
                out_ref[away, c, :HEAD] = q
                out_ref[away, c, HEAD : 2 * HEAD] = k
                out_ref[away, c, 2 * HEAD :] = v
    for k, ref in enumerate((out0_ref, out1_ref, out2_ref, out3_ref)):
        ref[...] = out_ref[k]


def run_project(place, w, blocks, cosine, sine):
    return pl.pallas_call(
        project_kernel,
        out_shape=(SHAPE((4, 3 * HEAD, 128), BF16),) * 4 + (SHAPE((640, WIDTH), BF16),),
        in_specs=[SMEM] + [VMEM] * 7,
        out_specs=(VMEM,) * 5,
        scratch_shapes=[pltpu.VMEM((4, 4, 3 * HEAD, 128), BF16)],
        compiler_params=pltpu.CompilerParams(vmem_limit_bytes=60 << 20),
        cost_estimate=cost(40),
        name="project",
    )(place, w, *blocks, cosine, sine)


def hidden_kernel(inverse, place, *refs):
    gain_ref, h_ref, x_ref = refs[8:]
    for k, ref in enumerate(refs[:8]):
        base = k % 2 + 2 * (k // 2 % 2) + 8 * (k // 4)
        x_ref[place[14] ^ base] = ref[0]
        x_ref[place[14] ^ (base + 4)] = ref[1]

    def chunk(i, _):
        rows = []
        for j in range(4):
            flat = inverse[4 * i + j]
            start = pl.multiple_of((flat & 1) * BLOCK, BLOCK)
            rows.append(x_ref[flat // 2, pl.ds(start, BLOCK), :])
        normal, _ = normalise(jnp.concatenate(rows, 0).astype(F32))
        h_ref[i] = (normal * gain_ref[...]).astype(BF16)
        return 0

    lax.fori_loop(0, CHUNKS, chunk, 0)


def run_hidden(inverse, place, blocks, gain):
    two = pl.BlockSpec((2, 128, WIDTH), lambda i: (0, 0, 0))
    return pl.pallas_call(
        hidden_kernel,
        grid=(1,),
        out_shape=SHAPE((CHUNKS, CHUNK, WIDTH), BF16),
        in_specs=[SMEM, SMEM] + [two] * 8 + [pl.BlockSpec((1, WIDTH), lambda i: (0, 0))],
        out_specs=pl.BlockSpec((CHUNKS, CHUNK, WIDTH), lambda i: (0, 0, 0)),
        scratch_shapes=[pltpu.VMEM((16, 128, WIDTH), BF16)],
        compiler_params=pltpu.CompilerParams(vmem_limit_bytes=60 << 20),
        cost_estimate=cost(5),
        name="hidden",
    )(inverse, place, *blocks, gain)


def forward_kernel(
    inverse, place, in0_ref, in1_ref, in2_ref, in3_ref, id_row, id_column,
    out_ref, q_ref, k_ref, v_ref, krow_ref, o_ref, lse_ref, all_ref, orow_ref, in_ref,
):
    for k, ref in enumerate((in0_ref, in1_ref, in2_ref, in3_ref)):
        in_ref[pl.ds(4 * ((place[12] - k) & 3), 4)] = ref[...]
    sort_tiles(inverse, in_ref, all_ref)
    for at in range(CHUNKS):
        q_ref[at] = all_ref[at, :HEAD]
        k_ref[at] = all_ref[at, HEAD : 2 * HEAD]
        v_ref[at] = all_ref[at, 2 * HEAD :]
        krow_ref[at] = all_ref[at, HEAD : 2 * HEAD].T
    for half in range(2):
        for part in range(4):
            at = 4 * half + part
            keys = (part + 1) * CHUNK
            k = krow_ref[4 * half : 4 * half + part + 1].reshape(keys, HEAD)
            s = dot(k, q_ref[at])
            s = masked(s, half, part, id_row[...], id_column[...], -1e30)
            top = jnp.max(s, axis=0, keepdims=True)
            p = jnp.exp(s - top)
            total = jnp.sum(p, axis=0, keepdims=True)
            low = p.astype(BF16)
            o = dot(v_ref[4 * half], low[:CHUNK])
            for j in range(1, part + 1):
                o += dot(v_ref[4 * half + j], low[j * CHUNK : (j + 1) * CHUNK])
            o = o / total
            o_ref[at] = o
            orow_ref[at] = o.T
            lse_ref[at] = top + jnp.log(total)
    for b in range(16):
        flat = inverse[b]
        upper = 15 - b
        lo = orow_ref[b // 4, (b % 4) * BLOCK : (b % 4 + 1) * BLOCK, :]
        up = orow_ref[4 + upper // 4, (upper % 4) * BLOCK : (upper % 4 + 1) * BLOCK, :]
        tile = jnp.concatenate([lo, up], 1)
        turned = jnp.concatenate([up, lo], 1)
        tile = jnp.where(flat % 2 == 0, tile, turned).astype(BF16)
        group = flat // 16
        for chip in range(4):
            out_ref[4 * group + chip, (flat // 2) % 8] = tile


def run_forward(inverse, place, tiles, id_row, id_column):
    return pl.pallas_call(
        forward_kernel,
        out_shape=(
            SHAPE((8, 8, BLOCK, 128), BF16),
            SHAPE((CHUNKS, HEAD, CHUNK), BF16),
            SHAPE((CHUNKS, HEAD, CHUNK), BF16),
            SHAPE((CHUNKS, HEAD, CHUNK), BF16),
            SHAPE((CHUNKS, CHUNK, HEAD), BF16),
            SHAPE((CHUNKS, HEAD, CHUNK), F32),
            SHAPE((CHUNKS, 1, CHUNK), F32),
        ),
        in_specs=[SMEM] * 2 + [VMEM] * 6,
        out_specs=(VMEM,) * 7,
        scratch_shapes=[
            pltpu.VMEM((CHUNKS, 3 * HEAD, CHUNK), BF16),
            pltpu.VMEM((CHUNKS, CHUNK, HEAD), F32),
            pltpu.VMEM((16, 3 * HEAD, 128), BF16),
        ],
        compiler_params=pltpu.CompilerParams(vmem_limit_bytes=60 << 20),
        cost_estimate=cost(40),
        name="attention_forward",
    )(inverse, place, *tiles, id_row, id_column)


def backward_kernel(
    inverse, place, do_ref, h_ref, q_ref, k_ref, v_ref, krow_ref, o_ref, lse_ref, cos_ref, sin_ref,
    id_row, id_column, ob_ref, near_ref, far_ref,
    out0_ref, out1_ref, out2_ref, out3_ref, grad_ref,
    d_ref, dk_ref, dv_ref, dot_ref, vrow_ref, wt_ref, all_ref,
):
    sort_tiles(inverse, do_ref, dot_ref)
    for half in range(2):
        for part in range(4):
            at = 4 * half + part
            vrow_ref[at] = v_ref[at].T
            keys = (part + 1) * CHUNK
            first = 4 * half
            k = krow_ref[first : first + part + 1].reshape(keys, HEAD)
            v = vrow_ref[first : first + part + 1].reshape(keys, HEAD)
            q = q_ref[at]
            do = dot_ref[at]
            delta = jnp.sum(do.astype(F32) * o_ref[at], axis=0, keepdims=True)
            s = dot(k, q) - lse_ref[at]
            p = jnp.exp(masked(s, half, part, id_row[...], id_column[...], -1e30))
            ds = (p * (dot(v, do) - delta)).astype(BF16)
            dv = dot(p.astype(BF16), do.T).reshape(part + 1, CHUNK, HEAD)
            dk = dot(ds, q.T).reshape(part + 1, CHUNK, HEAD)
            if part:
                dv_ref[first : first + part] += dv[:part]
                dk_ref[first : first + part] += dk[:part]
            dv_ref[at] = dv[part]
            dk_ref[at] = dk[part]
            dq = dot(k_ref[first], ds[:CHUNK])
            for j in range(1, part + 1):
                dq += dot(k_ref[first + j], ds[j * CHUNK : (j + 1) * CHUNK])
            d_ref[at, :HEAD] = turn(dq * 0.125, cos_ref[at], sin_ref[at], True).astype(BF16)
    for at in range(8):
        dk = turn(dk_ref[at].T, cos_ref[at], sin_ref[at], True)
        d_ref[at, HEAD : 2 * HEAD] = dk.astype(BF16)
        d_ref[at, 2 * HEAD :] = dv_ref[at].T.astype(BF16)
        part = dot(d_ref[at], h_ref[at])
        wt_ref[:192] = part if at == 0 else wt_ref[:192] + part
    for d in range(4):
        start = pl.multiple_of((d // 2) * 256 + ((place[9] ^ d) & 1) * 128, 128)
        columns = (near_ref if d % 2 == 0 else far_ref)[d // 2]
        part = dot(columns.T, ob_ref[pl.ds(start, 128), :])
        wt_ref[192:] = part if d == 0 else wt_ref[192:] + part
    grad_ref[...] = wt_ref[...].T.astype(BF16).reshape(8, 96, 384)
    for b in range(16):
        flat = inverse[b]
        upper = 15 - b
        lo = d_ref[b // 4, :, (b % 4) * BLOCK : (b % 4 + 1) * BLOCK].astype(F32)
        up = d_ref[4 + upper // 4, :, (upper % 4) * BLOCK : (upper % 4 + 1) * BLOCK].astype(F32)
        tile = jnp.concatenate([lo, up], 1)
        turned = jnp.concatenate([up, lo], 1)
        away = (flat // 8 - place[12]) & 3
        all_ref[away, (flat // 2) % 4] = jnp.where(flat % 2 == 0, tile, turned).astype(BF16)
    for k, ref in enumerate((out0_ref, out1_ref, out2_ref, out3_ref)):
        ref[...] = all_ref[k]


def run_backward(inverse, place, do, h, kept, cosine, sine, id_row, id_column, ob, columns):
    return pl.pallas_call(
        backward_kernel,
        out_shape=(
            *(SHAPE((4, 3 * HEAD, 2 * BLOCK), BF16),) * 4,
            SHAPE((8, 96, 384), BF16),
        ),
        in_specs=[SMEM] * 2 + [VMEM] * 15,
        out_specs=(VMEM,) * 5,
        scratch_shapes=[
            pltpu.VMEM((CHUNKS, 3 * HEAD, CHUNK), BF16),
            pltpu.VMEM((CHUNKS, CHUNK, HEAD), F32),
            pltpu.VMEM((CHUNKS, CHUNK, HEAD), F32),
            pltpu.VMEM((CHUNKS, HEAD, CHUNK), BF16),
            pltpu.VMEM((CHUNKS, CHUNK, HEAD), BF16),
            pltpu.VMEM((384, WIDTH), F32),
            pltpu.VMEM((4, 4, 3 * HEAD, 2 * BLOCK), BF16),
        ],
        compiler_params=pltpu.CompilerParams(vmem_limit_bytes=60 << 20),
        cost_estimate=cost(22.0),
        name="attention_backward",
    )(inverse, place, do, h, *kept, cosine, sine, id_row, id_column, ob, *columns)


def pick(core, same, other):
    first = jnp.where(core == 0, same, other)
    return jnp.concatenate([first, jnp.where(core == 0, other, same)], 0)


def assemble(place, units_ref, sems, gu_ref=None, down_ref=None, wout_ref=None):
    copies = []
    parts = ((wout_ref, 144, 96), (gu_ref, 0, 96), (down_ref, 96, 48))
    for target, first, size in parts:
        if target is not None:
            for k in range(8):
                start = ((place[13] ^ (k % 2)) * 4 + k // 2) * size
                rows = target.at[pl.ds(pl.multiple_of(start, 16), size)]
                source = units_ref.at[k // 2, k % 2, first : first + size]
                copies.append(pltpu.make_async_copy(source, rows, sems.at[len(copies)]))
    for copy in copies:
        copy.start()

    def wait(first, last):
        for copy in copies[first:last]:
            copy.wait()

    return wait


def feed_kernel(
    place, own_ref, other_ref, x0_ref, x1_ref, x2_ref, x3_ref, z0_ref, z1_ref, z2_ref, z3_ref,
    gain_ref, units_ref,
    keep_ref, send_ref, h_ref, d_ref, a_ref, quad_ref, y_ref, ob_ref, mid_ref,
    gu_ref, down_ref, wout_ref, sems,
):
    step = pl.program_id(0)

    @pl.when(step == 0)
    def _():
        assemble(place, units_ref, sems, gu_ref, down_ref, wout_ref)(0, 24)

    core, member = place[8], place[9]
    swap = (member // 2) & 1
    for i in range(2):
        at = i ^ swap
        for c in range(2):
            base = 256 * i + 128 * c
            for z in range(2):
                tiles = []
                for k in range(2):
                    for x in range(3):
                        mine = own_ref[2 * x + z, 2 * at + c]
                        theirs = other_ref[2 * x + z, 2 * at + c]
                        tiles.append(jnp.where(core == k, mine, theirs))
                for pair in range(3):
                    left, right = tiles[2 * pair], tiles[2 * pair + 1]
                    lanes = slice(384 * z + 128 * pair, 384 * z + 128 * (pair + 1))
                    ob_ref[base : base + BLOCK, lanes] = jnp.concatenate(
                        [left[:, :BLOCK], right[:, :BLOCK]], 1
                    )
                    ob_ref[base + BLOCK : base + 128, lanes] = jnp.concatenate(
                        [left[:, BLOCK:], right[:, BLOCK:]], 1
                    )
    xs = [pick(core, x0_ref[0], x1_ref[0]), pick(core, x2_ref[0], x3_ref[0])]
    middle = jnp.concatenate(xs, 0).astype(F32) + dot(ob_ref[...], wout_ref[...])
    mid_ref[...] = middle

    @pl.when(step == 0)
    def _():
        y_ref[...] = mid_ref[pl.ds(pl.multiple_of(core * 128, 128), 128), :]
        quad_ref[...] = ob_ref[...]

    normal, _ = normalise(middle)
    h = (normal * gain_ref[...]).astype(BF16)
    h_ref[...] = h
    gu = dot(h, gu_ref[...])
    g, u = gu[:, :384], gu[:, 384:]
    sigma = jax.nn.sigmoid(g)
    swish = g * sigma
    a_ref[...] = (swish * u).astype(BF16)
    dz = [pick(core, z0_ref[0], z1_ref[0]), pick(core, z2_ref[0], z3_ref[0])]
    dz = jnp.concatenate(dz, 0)
    da = dot(dz, down_ref[...], 1, 1)
    d_ref[:, :384] = (da * u * (sigma + swish * (1.0 - sigma))).astype(BF16)
    d_ref[:, 384:] = (da * swish).astype(BF16)
    mid_ref[...] = dot(d_ref[...], gu_ref[...], 1, 1)
    for i in range(2):
        at = i ^ swap
        keep = pl.multiple_of(256 * i + core * 128, 128)
        send = pl.multiple_of(256 * i + 128 - core * 128, 128)
        keep_ref[at] = mid_ref[pl.ds(keep, 128), :].astype(BF16)
        send_ref[at] = mid_ref[pl.ds(send, 128), :].astype(BF16)


def run_feed(place, own, other, blocks, gain, units):
    rows = 4 * CHUNK
    return pl.pallas_call(
        feed_kernel,
        grid_spec=pltpu.PrefetchScalarGridSpec(
            num_scalar_prefetch=1,
            grid=(2,),
            in_specs=[
                pl.BlockSpec((6, 4, BLOCK, 128), lambda i, s: (0, s[9] // 4 ^ i, 0, 0)),
                pl.BlockSpec((6, 4, BLOCK, 128), lambda i, s: (0, s[9] // 4 ^ i, 0, 0)),
                *[pl.BlockSpec((1, 128, WIDTH), lambda i, s: (i, 0, 0))] * 4,
                *[pl.BlockSpec((1, 128, WIDTH), lambda i, s: (2 + i, 0, 0))] * 4,
                pl.BlockSpec((1, WIDTH), lambda i, s: (0, 0)),
                ANY,
            ],
            out_specs=[
                pl.BlockSpec((2, 128, WIDTH), lambda i, s: (s[9] // 4 ^ i, 0, 0)),
                pl.BlockSpec((2, 128, WIDTH), lambda i, s: (s[9] // 4 ^ i, 0, 0)),
                pl.BlockSpec((2 * CHUNK, WIDTH), lambda i, s: (i, 0)),
                pl.BlockSpec((2 * CHUNK, WIDTH), lambda i, s: (i, 0)),
                pl.BlockSpec((2 * CHUNK, WIDTH // 2), lambda i, s: (i, 0)),
                pl.BlockSpec((2 * CHUNK, WIDTH), lambda i, s: (0, 0)),
                pl.BlockSpec((128, WIDTH), lambda i, s: (0, 0)),
            ],
            scratch_shapes=[
                pltpu.VMEM((2 * CHUNK, WIDTH), BF16),
                pltpu.VMEM((2 * CHUNK, WIDTH), F32),
                pltpu.VMEM((WIDTH, WIDTH), BF16),
                pltpu.VMEM((WIDTH // 2, WIDTH), BF16),
                pltpu.VMEM((WIDTH, WIDTH), BF16),
                pltpu.SemaphoreType.DMA((24,)),
            ],
        ),
        out_shape=(
            SHAPE((4, 128, WIDTH), BF16),
            SHAPE((4, 128, WIDTH), BF16),
            SHAPE((rows, WIDTH), BF16),
            SHAPE((rows, WIDTH), BF16),
            SHAPE((rows, WIDTH // 2), BF16),
            SHAPE((2 * CHUNK, WIDTH), BF16),
            SHAPE((128, WIDTH), F32),
        ),
        compiler_params=pltpu.CompilerParams(vmem_limit_bytes=60 << 20),
        cost_estimate=cost(40),
        name="feed",
    )(place, own, other, *blocks, *blocks, gain, units)


def weights_kernel(
    place, h_ref, d_ref, a_ref, z0_ref, z1_ref, z2_ref, z3_ref, units_ref,
    out_ref, all_ref, gu_ref, gd_ref, down_ref, sems,
):
    step = pl.program_id(0)

    @pl.when(step == 0)
    def _():
        assemble(place, units_ref, sems, down_ref=down_ref)(0, 8)

    core, swap = place[8], (place[9] // 2) & 1
    dz = [pick(core, z0_ref[0], z1_ref[0]), pick(core, z2_ref[0], z3_ref[0])]
    gu = dot(h_ref[...], d_ref[...], 0, 0)
    gd = dot(a_ref[...], jnp.concatenate(dz, 0), 0, 0)

    @pl.when(step == 0)
    def _():
        gu_ref[...] = gu
        gd_ref[...] = gd

    @pl.when(step > 0)
    def _():
        gu_ref[...] += gu
        gd_ref[...] += gd

    z = dot(a_ref[...], down_ref[...]).astype(BF16)
    for i in range(2):
        start = pl.multiple_of((i ^ swap) * CHUNK, CHUNK)
        all_ref[pl.ds(start, CHUNK), :] = z[CHUNK * i : CHUNK * (i + 1)]

    @pl.when(step == 1)
    def _():
        for f in range(8):
            base = (2 * (f % 4) + f // 4) * 144
            out_ref[base : base + 96] = gu_ref[96 * f : 96 * (f + 1)].astype(BF16)
            out_ref[base + 96 : base + 144] = gd_ref[48 * f : 48 * (f + 1)].astype(BF16)


def run_weights(place, h, d, a, blocks, units):
    return pl.pallas_call(
        weights_kernel,
        grid_spec=pltpu.PrefetchScalarGridSpec(
            num_scalar_prefetch=1,
            grid=(2,),
            in_specs=[
                pl.BlockSpec((2 * CHUNK, WIDTH), lambda i, s: (i, 0)),
                pl.BlockSpec((2 * CHUNK, WIDTH), lambda i, s: (i, 0)),
                pl.BlockSpec((2 * CHUNK, WIDTH // 2), lambda i, s: (i, 0)),
                *[pl.BlockSpec((1, 128, WIDTH), lambda i, s: (2 + i, 0, 0))] * 4,
                ANY,
            ],
            out_specs=[
                pl.BlockSpec((8 * 144, WIDTH), lambda i, s: (0, 0)),
                pl.BlockSpec((2 * CHUNK, WIDTH), lambda i, s: (s[9] // 4 ^ i, 0)),
            ],
            scratch_shapes=[
                pltpu.VMEM((WIDTH, WIDTH), F32),
                pltpu.VMEM((WIDTH // 2, WIDTH), F32),
                pltpu.VMEM((WIDTH // 2, WIDTH), BF16),
                pltpu.SemaphoreType.DMA((8,)),
            ],
        ),
        out_shape=(SHAPE((8 * 144, WIDTH), BF16), SHAPE((4 * CHUNK, WIDTH), BF16)),
        compiler_params=pltpu.CompilerParams(vmem_limit_bytes=60 << 20),
        cost_estimate=cost(9),
        name="weights",
    )(place, h, d, a, *blocks, units)


def middle_kernel(
    place, parts_ref, y_ref, cot_ref, gain_ref, units_ref,
    dy_ref, keep_ref, send_ref, do_ref, columns_ref, wout_ref, sems,
):
    wait = assemble(place, units_ref, sems, wout_ref=wout_ref)
    dh = jnp.sum(parts_ref[...].astype(F32), axis=0)
    normal, scale = normalise(y_ref[...])
    dy = cot_ref[...].astype(F32) + norm_back(dh, normal, scale, gain_ref[...])
    dy_ref[...] = dy
    low = dy.astype(BF16)
    wait(0, 8)
    do = dot(wout_ref[...], low, 1, 1).astype(BF16)
    for t in range(4):
        for x in range(4):
            h = 3 * t + min(x, 2)
            do_ref[4 * x + t] = do[HEAD * h : HEAD * (h + 1)]
    for r in range(4):
        columns_ref[place[11] ^ r] = low[:, 192 * r : 192 * (r + 1)]
    keep_ref[...] = columns_ref[:2]
    send_ref[...] = columns_ref[2:]


def run_middle(place, parts, y, cotangent, gain, units):
    return pl.pallas_call(
        middle_kernel,
        out_shape=(
            SHAPE((128, WIDTH), F32),
            *(SHAPE((2, 128, 192), BF16),) * 2,
            SHAPE((16, HEAD, 128), BF16),
        ),
        in_specs=[SMEM] + [VMEM] * 4 + [ANY],
        out_specs=(VMEM,) * 4,
        scratch_shapes=[
            pltpu.VMEM((4, 128, 192), BF16),
            pltpu.VMEM((WIDTH, WIDTH), BF16),
            pltpu.SemaphoreType.DMA((8,)),
        ],
        compiler_params=pltpu.CompilerParams(vmem_limit_bytes=60 << 20),
        cost_estimate=cost(12.0),
        name="middle",
    )(place, parts, y, cotangent, gain, units)


def inputs_kernel(place, d0_ref, d1_ref, d2_ref, d3_ref, w_ref, keep_ref, send_ref, sum_ref):
    core, column = place[8], place[12]
    for c in range(4):
        for k, ref in enumerate((d0_ref, d1_ref, d2_ref, d3_ref)):
            x = (column - k) & 3
            at = jnp.minimum(x, 2) * HEAD
            w = jnp.concatenate(
                [w_ref[pl.ds(pl.multiple_of(base + at, HEAD), HEAD), :] for base in (0, 192, 384)],
                0,
            )
            part = jnp.where(x < 3, dot(ref[c], w, 0, 0), 0.0)
            sum_ref[c] = part if k == 0 else sum_ref[c] + part
    for z in range(2):
        keep_ref[z] = sum_ref[2 * z + core].astype(BF16)
        send_ref[z] = sum_ref[2 * z + 1 - core].astype(BF16)


def run_inputs(place, parts, w_rows):
    return pl.pallas_call(
        inputs_kernel,
        out_shape=(SHAPE((2, 128, WIDTH), BF16),) * 2,
        in_specs=[SMEM] + [VMEM] * 5,
        out_specs=(VMEM,) * 2,
        scratch_shapes=[pltpu.VMEM((4, 128, WIDTH), F32)],
        compiler_params=pltpu.CompilerParams(vmem_limit_bytes=60 << 20),
        cost_estimate=cost(3),
        name="inputs",
    )(place, *parts, w_rows)


def finish_kernel(
    place, *refs
):
    pieces = refs[:16]
    wq_ref, wk_ref, wv_ref, gate_ref, up_ref, one_ref, two_ref = refs[16:23]
    q_ref, k_ref, v_ref, o_ref, g_ref, u_ref, d_ref, n_ref, m_ref, all_ref = refs[23:]
    for d, ref in enumerate(pieces):
        all_ref[place[14] ^ d] = ref[...]

    def tile(chip, k, rows):
        return all_ref[2 * chip + k, rows]

    total = jnp.zeros((96, 1), F32)
    for half, (w_ref, out_ref) in enumerate(((gate_ref, g_ref), (up_ref, u_ref))):
        tiles = []
        for m in range(8):
            part = tile(4 * half + m // 2, m % 2, slice(96, 240))
            d_ref[48 * m : 48 * (m + 1), 384 * half : 384 * (half + 1)] = part[96:].astype(F32)
            tiles.append(part[:96])
        for f in range(8):
            block = jnp.concatenate([t[:, 48 * f : 48 * (f + 1)] for t in tiles], 1).astype(F32)
            lanes = slice(384 * f, 384 * (f + 1))
            out_ref[:, lanes] = block
            total += jnp.sum(w_ref[:, lanes].astype(F32) * block, axis=1, keepdims=True)
    m_ref[...] = jnp.broadcast_to(total, (96, 128)).T[:1] / two_ref[...].astype(F32)
    total = jnp.zeros((96, 1), F32)
    tiles = {
        (x, 2 * z + k): tile(2 * x + z, k, slice(0, 96)).astype(F32)
        for x in range(4)
        for z in range(2)
        for k in range(2)
    }
    for j, (w_ref, out_ref) in enumerate(((wq_ref, q_ref), (wk_ref, k_ref), (wv_ref, v_ref))):
        lanes = slice(HEAD * j, HEAD * (j + 1))
        whole = jnp.concatenate([tiles[h % 3, h // 3][:, lanes] for h in range(12)], 1)
        out_ref[...] = whole
        total += jnp.sum(w_ref[...].astype(F32) * whole, axis=1, keepdims=True)
    n_ref[...] = jnp.broadcast_to(total, (96, 128)).T[:1] / one_ref[...].astype(F32)
    o_ref[...] = jnp.concatenate(
        [sum(tiles[x, t][:, 192:] for x in range(4)) for t in range(4)], 1
    )


def run_finish(place, pieces, query, key, value, gate, up, one, two):
    return pl.pallas_call(
        finish_kernel,
        out_shape=(
            *(SHAPE((96, WIDTH), F32),) * 4,
            SHAPE((96, 3072), F32),
            SHAPE((96, 3072), F32),
            SHAPE((384, WIDTH), F32),
            SHAPE((1, 96), F32),
            SHAPE((1, 96), F32),
        ),
        in_specs=[SMEM] + [VMEM] * 23,
        out_specs=(VMEM,) * 9,
        scratch_shapes=[pltpu.VMEM((16, 240, 384), BF16)],
        compiler_params=pltpu.CompilerParams(vmem_limit_bytes=60 << 20),
        cost_estimate=cost(7),
        name="finish",
    )(place, *pieces, query, key, value, gate, up, one.reshape(1, 96), two.reshape(1, 96))


def fold_kernel(in_ref, out_ref):
    out_ref[...] = jnp.sum(in_ref[...].astype(F32), axis=0).astype(BF16)


def run_fold(parts):
    return pl.pallas_call(
        fold_kernel,
        out_shape=SHAPE(parts.shape[1:], BF16),
        in_specs=[VMEM],
        out_specs=VMEM,
        compiler_params=pltpu.CompilerParams(vmem_limit_bytes=60 << 20),
        cost_estimate=cost(2),
        name="fold",
    )(parts)


def trade(value, distance):
    return lax.ppermute(value, "ctx", [(i, i ^ distance) for i in range(16)])


def pair_sum(keep, send):
    return (keep.astype(F32) + trade(send, 1).astype(F32)).astype(BF16)


def norm_back(grad_normed, normal_rows, inverse, gains):
    scaled = grad_normed * gains
    return inverse * (scaled - normal_rows * jnp.mean(scaled * normal_rows, axis=-1, keepdims=True))


def local(
    tokens, block_table, seq_ids, w_query, w_key, w_value, w_out, w_gate, w_up, w_down,
    gain_attn, gain_mlp, cotangent,
):
    index = lax.axis_index("ctx")
    shard = lax.axis_index("fsdp")
    rank, column = index % 4, index // 4
    core, member, group = index % 2, index % 8, index // 8

    rings = [[0, 1, 2, 3], [4, 5, 6, 7]]

    blocks = block_table.reshape(-1)
    numbers = jnp.arange(32, dtype=jnp.int32)
    inverse = jnp.sum(
        jnp.where(blocks[None, :] == numbers[:, None], numbers[None, :], 0), axis=1
    ).astype(jnp.int32)
    ids = seq_ids[0].reshape(32, BLOCK)
    hits = (inverse[16:, None] == numbers[None, :]).astype(jnp.int32)
    ids = jnp.sum(hits[:, :, None] * ids[None], axis=1).reshape(HALF_SEQ)
    id_row, id_column = ids.reshape(1, HALF_SEQ), ids.reshape(HALF_SEQ, 1)
    frequency = jnp.power(THETA, -(jnp.arange(HALF, dtype=F32) * 2.0) / HEAD)
    angles = jnp.arange(SEQ, dtype=F32).reshape(CHUNKS, 1, CHUNK) * frequency[None, :, None]
    cosine, sine = jnp.cos(angles), jnp.sin(angles)
    own_blocks = lax.dynamic_slice_in_dim(blocks, 8 * column, 8)
    places = (own_blocks[:, None] * BLOCK + jnp.arange(BLOCK, dtype=jnp.int32)).reshape(4, 1, 128)
    angles = places.astype(F32) * frequency[None, :, None]
    place = jnp.stack(
        [(shard // 4 ^ dz) * 4 + (shard + dy) % 4 for dz, dy in RING]
        + [core, member, group, rank, column, shard // 4, index]
    ).astype(jnp.int32)

    units = run_pack_heads(w_query, w_key, w_value, gain_attn, gain_mlp)
    w_heads = lax.all_to_all(units, "fsdp", 0, 0).reshape(WIDTH, 640)
    x_own = after(tokens[0], units)
    x_blocks = [tokens[0], trade(x_own, 1)]
    unit = run_pack_units(w_gate, w_up, w_down, w_out, x_blocks[1])
    x_blocks.append(trade(x_own, 2))
    across = lax.ppermute(after(unit, x_blocks[2]), "fsdp", [(i, i ^ 4) for i in range(8)])
    own = after(jnp.stack([x_own, cotangent[0]]), x_blocks[1])
    own = [own, trade(own, 4), trade(own[0], 8), trade(own[0], 12)]
    x_blocks.append(trade(after(x_blocks[2], own, unit), 1))
    w_heads, cosine, sine, angles = lax.optimization_barrier(
        (w_heads, cosine, sine, (jnp.cos(angles), jnp.sin(angles)))
    )
    *tiles, w_rows = run_project(place, w_heads, x_blocks, *angles)
    gains = w_rows[576:578].astype(F32)
    gain_one, gain_two = gains[:1], gains[1:]

    for k in range(1, 4):
        tiles[k] = lax.ppermute(
            tiles[k], "ctx", [(i, (i + 4 * k) % 16) for i in range(16)]
        )
    units = lax.all_gather(
        jnp.stack([unit, after(across, w_rows)]), "fsdp", axis=0, axis_index_groups=rings
    )
    near = jnp.stack([own[0][0], own[1][0], own[0][1], own[1][1]])
    rest = jnp.stack(own[2:])
    far = trade(after(near, w_rows), 2)
    o_tiles, *kept = run_forward(inverse, place, tiles, id_row, id_column)
    o_tiles, far = lax.optimization_barrier((o_tiles, far))
    o_own = lax.all_to_all(o_tiles, "ctx", 0, 0, axis_index_groups=SAME_CORE)
    blocks = [near, trade(near, 1), far, trade(far, 1)]
    o_other = trade(after(o_own, blocks), 1)
    far = trade(after(rest, o_own), 2)

    keep, send, h2, dgu, a, ob, middle = run_feed(
        place, o_own, o_other, blocks, gain_two, units
    )
    pair = pair_sum(keep, send)
    parts = lax.all_to_all(pair, "ctx", 0, 0, axis_index_groups=FOUR_CHIPS)

    ff, z = run_weights(place, after(h2, pair), dgu, a, blocks, units)
    far = after(far, ff)
    hidden = run_hidden(
        inverse, place, blocks + [rest, trade(rest, 1), far, trade(far, 1)], gain_one
    )
    dy1, *columns, do = run_middle(place, after(parts, ff), middle, cotangent[0], gain_two, units)
    ff = lax.psum_scatter(
        ff, "fsdp", scatter_dimension=0, tiled=True, axis_index_groups=rings
    )
    do_tiles = do
    do = lax.all_to_all(do, "ctx", 0, 0)
    columns = jnp.stack([columns[0], trade(columns[1], 2)], 1)
    columns = [columns[0], trade(columns[1], 1)]
    *d_parts, small = run_backward(
        inverse, place, do, hidden, kept, cosine, sine, id_row, id_column, ob, columns
    )
    small, ff = lax.optimization_barrier((small, ff))
    eights = [list(range(8)), list(range(8, 16))]
    z = lax.psum_scatter(
        after(z, ff), "ctx", scatter_dimension=0, tiled=True, axis_index_groups=eights
    )
    result = middle + z.astype(F32)
    d_parts = after(d_parts, ff)
    for k in range(1, 4):
        d_parts[k] = lax.ppermute(
            d_parts[k], "ctx", [(i, (i + 4 * k) % 16) for i in range(16)]
        )
    far = shard // 4 == 1
    away = jnp.where(far, ff[:144], ff[144:])
    ff = jnp.where(far, ff[144:], ff[:144])

    def half(value, flip):
        return jnp.where((group == 1) ^ flip, value[:, 384:], value[:, :384])

    def across(value, flip, shift):
        pairs = [(8 * c + f, 8 * (c ^ shift) + (f ^ flip)) for f in range(8) for c in range(16)]
        return lax.ppermute(value, ("ctx", "fsdp"), pairs)

    parts = [
        half(ff, False),
        across(half(ff, True), 0, 8),
        across(half(away, False), 4, 0),
        across(half(away, True), 4, 8),
    ]
    ff = sum(part.astype(F32) for part in parts).astype(BF16)

    small = run_fold(lax.all_to_all(small, "fsdp", 0, 0))
    small, *d_parts = lax.optimization_barrier((small, *d_parts))
    last = jnp.concatenate([small, ff], 0)
    pieces = []
    for d in range(0, 16, 2):
        piece = trade(last, d) if d else last
        pieces += [piece, trade(piece, 1)]
    (
        total_query, total_key, total_value, total_out, total_gate, total_up, total_down,
        total_gain_one, total_gain_two,
    ) = run_finish(
        place, pieces, w_query, w_key, w_value, w_gate, w_up, gain_attn, gain_mlp
    )

    keep, send = run_inputs(place, d_parts, w_rows)
    summed = keep.astype(F32) + trade(send, 1).astype(F32)
    low = rank // 2 == 0
    keep = jnp.where(low, summed[0], summed[1])
    send = jnp.where(low, summed[1], summed[0]).astype(BF16)
    dh1 = keep + trade(send, 2).astype(F32)
    normal_one, inverse_one = normalise(tokens[0].astype(F32))
    grad_stream = dy1 + norm_back(dh1, normal_one, inverse_one, gain_one)

    eights = [list(range(8)), list(range(8, 16))]
    return (
        result[None].astype(BF16),
        grad_stream[None].astype(BF16),
        total_query,
        total_key,
        total_value,
        total_out,
        total_gate,
        total_up,
        total_down,
        total_gain_one.reshape(96),
        total_gain_two.reshape(96),
    )


def solution(mesh):
    rows = P("fsdp", "ctx", None)
    weight = P("fsdp", None)
    return jax.shard_map(
        local,
        mesh=mesh,
        in_specs=(rows, P(), weight) + (weight,) * 7 + (P("fsdp"), P("fsdp"), rows),
        out_specs=(rows, rows) + (weight,) * 7 + (P("fsdp"), P("fsdp")),
        check_vma=False,
    )
```

```python
import jax
import jax.numpy as jnp
from jax import lax
from jax.experimental import pallas as pl
from jax.experimental.pallas import tpu as pltpu
from jax.sharding import PartitionSpec as P

EPS = 1e-05
THETA = 10000.0
WIDTH = 768
HEAD = 64
HALF = 32
SEQ = 2048
BLOCK = 64
CHUNK = 256
CHUNKS = SEQ // CHUNK
HALF_SEQ = SEQ // 2
F32 = jnp.float32
BF16 = jnp.bfloat16

QUADS = [[4 * i + j for j in range(4)] for i in range(4)]
COLUMNS = [[j + 4 * i for i in range(4)] for j in range(4)]
SAME_CORE = [[j + 2 * i for i in range(8)] for j in range(2)]
FOUR_CHIPS = [[8 * g + j + 2 * i for i in range(4)] for g in range(2) for j in range(2)]
RING = [(0, 0), (1, 0), (0, 3), (0, 1), (1, 3), (1, 1), (0, 2), (1, 2)]

VMEM = pl.BlockSpec(memory_space=pltpu.VMEM)
SMEM = pl.BlockSpec(memory_space=pltpu.SMEM)
ANY = pl.BlockSpec(memory_space=pl.ANY)
SHAPE = jax.ShapeDtypeStruct


def cost(microseconds):
    return pl.CostEstimate(
        flops=int(microseconds * 1.1e9), bytes_accessed=int(microseconds * 3.6e6), transcendentals=0
    )


def after(value, *others):
    return lax.optimization_barrier((value, others))[0]


def dot(left, right, left_dim=1, right_dim=0):
    return lax.dot_general(
        left, right, (((left_dim,), (right_dim,)), ((), ())), preferred_element_type=F32
    )


def turn(block, cosine, sine, backward):
    first, second = block[:HALF], block[HALF:]
    if backward:
        return jnp.concatenate([first * cosine + second * sine, second * cosine - first * sine], 0)
    return jnp.concatenate([first * cosine - second * sine, second * cosine + first * sine], 0)


def normalise(x):
    scale = lax.rsqrt(jnp.mean(x * x, axis=-1, keepdims=True) + EPS)
    return x * scale, scale


def masked(scores, half, part, id_row, id_column, other):
    keys = scores.shape[0]
    base = keys - CHUNK
    row = lax.broadcasted_iota(jnp.int32, (CHUNK, CHUNK), 0)
    column = lax.broadcasted_iota(jnp.int32, (CHUNK, CHUNK), 1)
    if half == 1:
        same = id_column[:keys] == id_row[:, part * CHUNK : (part + 1) * CHUNK]
        scores = jnp.where(same, scores, other)
    last = jnp.where(row <= column, scores[base:], other)
    return last if base == 0 else jnp.concatenate([scores[:base], last], 0)


def swap_lanes(tile):
    return jnp.concatenate([tile[:, BLOCK:], tile[:, :BLOCK]], 1)


def sort_tiles(inverse, in_ref, out_ref):
    for b in range(16):
        flat = inverse[b]
        upper = 15 - b
        tile = in_ref[flat // 2].astype(F32)
        tile = jnp.where(flat % 2 == 0, tile, swap_lanes(tile)).astype(BF16)
        out_ref[b // 4, :, (b % 4) * BLOCK : (b % 4 + 1) * BLOCK] = tile[:, :BLOCK]
        out_ref[4 + upper // 4, :, (upper % 4) * BLOCK : (upper % 4 + 1) * BLOCK] = tile[:, BLOCK:]


def pack_heads_kernel(q_ref, k_ref, v_ref, one_ref, two_ref, out_ref):
    rank = lax.axis_index("ctx") & 3
    column = lax.broadcasted_iota(jnp.int32, (96, 64), 1)
    one = jnp.broadcast_to(one_ref[...].astype(F32), (128, 96)).T[:, :64]
    two = jnp.broadcast_to(two_ref[...].astype(F32), (128, 96)).T[:, :64]
    gains = jnp.where(column == 0, one, jnp.where(column == 1, two, 0.0)).astype(BF16)
    for r in range(4):

        @pl.when(rank == r)
        def _():
            lanes = slice(192 * r, 192 * (r + 1))
            unit = jnp.concatenate([q_ref[:, lanes], k_ref[:, lanes], v_ref[:, lanes], gains], 1)
            for f in range(8):
                out_ref[f] = unit


def run_pack_heads(query, key, value, gain_one, gain_two):
    return pl.pallas_call(
        pack_heads_kernel,
        out_shape=SHAPE((8, 96, 640), BF16),
        in_specs=[VMEM] * 5,
        out_specs=VMEM,
        compiler_params=pltpu.CompilerParams(vmem_limit_bytes=60 << 20),
        cost_estimate=cost(2),
        name="pack_heads",
    )(query, key, value, gain_one.reshape(1, 96), gain_two.reshape(1, 96))


def pack_units_kernel(gate_ref, up_ref, down_ref, wout_ref, _, out_ref):
    index = lax.axis_index("ctx")
    member = index & 7
    for m in range(8):

        @pl.when(member == m)
        def _():
            parts = [
                ref[:, 384 * f + 48 * m : 384 * f + 48 * (m + 1)]
                for ref in (gate_ref, up_ref)
                for f in range(8)
            ]
            out_ref[:96] = jnp.concatenate(parts, 1)

    out_ref[96:144] = down_ref[pl.ds(pl.multiple_of(member * 48, 16), 48), :]
    out_ref[144:] = wout_ref[...]


def run_pack_units(gate, up, down, wout, after):
    return pl.pallas_call(
        pack_units_kernel,
        out_shape=SHAPE((240, WIDTH), BF16),
        in_specs=[VMEM] * 4 + [ANY],
        out_specs=VMEM,
        compiler_params=pltpu.CompilerParams(vmem_limit_bytes=60 << 20),
        cost_estimate=cost(2.4),
        name="pack_units",
    )(gate, up, down, wout, after)


def project_kernel(
    place, w_ref, x0_ref, x1_ref, x2_ref, x3_ref, cos_ref, sin_ref,
    out0_ref, out1_ref, out2_ref, out3_ref, wt_ref, out_ref,
):
    wt_ref[...] = w_ref[...].T
    gain = wt_ref[576:592].astype(F32)[:1]
    for d, block in enumerate((x0_ref, x1_ref, x2_ref, x3_ref)):
        c = place[11] ^ d
        normal, _ = normalise(block[...].astype(F32))
        h = (normal * gain).astype(BF16)
        qkv = dot(wt_ref[:576], h, 1, 1)
        cosine, sine = cos_ref[c], sin_ref[c]
        for j in range(3):
            at = HEAD * j
            q = (turn(qkv[at : at + HEAD], cosine, sine, False).astype(BF16) * 0.125).astype(BF16)
            k = turn(qkv[192 + at : 192 + at + HEAD], cosine, sine, False).astype(BF16)
            v = qkv[384 + at : 384 + at + HEAD].astype(BF16)
            for target in (2, 3) if j == 2 else (j,):
                away = (target - place[12]) & 3
                out_ref[away, c, :HEAD] = q
                out_ref[away, c, HEAD : 2 * HEAD] = k
                out_ref[away, c, 2 * HEAD :] = v
    for k, ref in enumerate((out0_ref, out1_ref, out2_ref, out3_ref)):
        ref[...] = out_ref[k]


def run_project(place, w, blocks, cosine, sine):
    return pl.pallas_call(
        project_kernel,
        out_shape=(SHAPE((4, 3 * HEAD, 128), BF16),) * 4 + (SHAPE((640, WIDTH), BF16),),
        in_specs=[SMEM] + [VMEM] * 7,
        out_specs=(VMEM,) * 5,
        scratch_shapes=[pltpu.VMEM((4, 4, 3 * HEAD, 128), BF16)],
        compiler_params=pltpu.CompilerParams(vmem_limit_bytes=14 << 20),
        cost_estimate=cost(40),
        name="project",
    )(place, w, *blocks, cosine, sine)


def forward_kernel(
    inverse, place, in0_ref, in1_ref, in2_ref, in3_ref, id_row, id_column,
    out_ref, q_ref, k_ref, v_ref, krow_ref, o_ref, lse_ref, all_ref, orow_ref, in_ref,
):
    for k, ref in enumerate((in0_ref, in1_ref, in2_ref, in3_ref)):
        in_ref[pl.ds(4 * ((place[12] - k) & 3), 4)] = ref[...]
    sort_tiles(inverse, in_ref, all_ref)
    for at in range(CHUNKS):
        q_ref[at] = all_ref[at, :HEAD]
        k_ref[at] = all_ref[at, HEAD : 2 * HEAD]
        v_ref[at] = all_ref[at, 2 * HEAD :]
        krow_ref[at] = all_ref[at, HEAD : 2 * HEAD].T
    for half in range(2):
        for part in range(4):
            at = 4 * half + part
            keys = (part + 1) * CHUNK
            k = krow_ref[4 * half : 4 * half + part + 1].reshape(keys, HEAD)
            s = dot(k, q_ref[at])
            s = masked(s, half, part, id_row[...], id_column[...], -1e30)
            top = jnp.max(s, axis=0, keepdims=True)
            p = jnp.exp(s - top)
            total = jnp.sum(p, axis=0, keepdims=True)
            low = p.astype(BF16)
            o = dot(v_ref[4 * half], low[:CHUNK])
            for j in range(1, part + 1):
                o += dot(v_ref[4 * half + j], low[j * CHUNK : (j + 1) * CHUNK])
            o = o / total
            o_ref[at] = o
            orow_ref[at] = o.T
            lse_ref[at] = top + jnp.log(total)
    for b in range(16):
        flat = inverse[b]
        upper = 15 - b
        lo = orow_ref[b // 4, (b % 4) * BLOCK : (b % 4 + 1) * BLOCK, :]
        up = orow_ref[4 + upper // 4, (upper % 4) * BLOCK : (upper % 4 + 1) * BLOCK, :]
        tile = jnp.concatenate([lo, up], 1)
        turned = jnp.concatenate([up, lo], 1)
        tile = jnp.where(flat % 2 == 0, tile, turned).astype(BF16)
        group = flat // 16
        for chip in range(4):
            out_ref[4 * group + chip, (flat // 2) % 8] = tile


def run_forward(inverse, place, tiles, id_row, id_column):
    return pl.pallas_call(
        forward_kernel,
        out_shape=(
            SHAPE((8, 8, BLOCK, 128), BF16),
            SHAPE((CHUNKS, HEAD, CHUNK), BF16),
            SHAPE((CHUNKS, HEAD, CHUNK), BF16),
            SHAPE((CHUNKS, HEAD, CHUNK), BF16),
            SHAPE((CHUNKS, CHUNK, HEAD), BF16),
            SHAPE((CHUNKS, HEAD, CHUNK), F32),
            SHAPE((CHUNKS, 1, CHUNK), F32),
        ),
        in_specs=[SMEM] * 2 + [VMEM] * 6,
        out_specs=(VMEM,) * 7,
        scratch_shapes=[
            pltpu.VMEM((CHUNKS, 3 * HEAD, CHUNK), BF16),
            pltpu.VMEM((CHUNKS, CHUNK, HEAD), F32),
            pltpu.VMEM((16, 3 * HEAD, 128), BF16),
        ],
        compiler_params=pltpu.CompilerParams(vmem_limit_bytes=60 << 20),
        cost_estimate=cost(40),
        name="attention_forward",
    )(inverse, place, *tiles, id_row, id_column)


def backward_kernel(
    inverse, place, do_ref, b0_ref, b1_ref, b2_ref, b3_ref, wide_ref, gain_ref,
    q_ref, k_ref, v_ref, krow_ref, o_ref, lse_ref, cos_ref, sin_ref,
    id_row, id_column, ob_ref, near_ref, far_ref,
    out0_ref, out1_ref, out2_ref, out3_ref, grad_ref,
    d_ref, dk_ref, dv_ref, dot_ref, vrow_ref, wt_ref, all_ref, xv_ref, obv_ref, xsem,
):
    other = xv_ref.at[pl.ds(8 - 8 * place[10], 8)]
    copies = [
        pltpu.make_async_copy(ob_ref, obv_ref, xsem.at[8]),
        pltpu.make_async_copy(wide_ref, other, xsem.at[9]),
    ]
    for k, ref in enumerate((b0_ref, b1_ref, b2_ref, b3_ref)):
        for j in range(2):
            at = place[14] ^ (k + 4 * j)
            copies.append(pltpu.make_async_copy(ref.at[j], xv_ref.at[at], xsem.at[2 * k + j]))
    for copy in copies:
        copy.start()
    sort_tiles(inverse, do_ref, dot_ref)
    for half in range(2):
        for part in range(4):
            at = 4 * half + part
            vrow_ref[at] = v_ref[at].T
            keys = (part + 1) * CHUNK
            first = 4 * half
            k = krow_ref[first : first + part + 1].reshape(keys, HEAD)
            v = vrow_ref[first : first + part + 1].reshape(keys, HEAD)
            q = q_ref[at]
            do = dot_ref[at]
            delta = jnp.sum(do.astype(F32) * o_ref[at], axis=0, keepdims=True)
            s = dot(k, q) - lse_ref[at]
            p = jnp.exp(masked(s, half, part, id_row[...], id_column[...], -1e30))
            ds = (p * (dot(v, do) - delta)).astype(BF16)
            dv = dot(p.astype(BF16), do.T).reshape(part + 1, CHUNK, HEAD)
            dk = dot(ds, q.T).reshape(part + 1, CHUNK, HEAD)
            if part:
                dv_ref[first : first + part] += dv[:part]
                dk_ref[first : first + part] += dk[:part]
            dv_ref[at] = dv[part]
            dk_ref[at] = dk[part]
            dq = dot(k_ref[first], ds[:CHUNK])
            for j in range(1, part + 1):
                dq += dot(k_ref[first + j], ds[j * CHUNK : (j + 1) * CHUNK])
            d_ref[at, :HEAD] = turn(dq * 0.125, cos_ref[at], sin_ref[at], True).astype(BF16)
    for copy in copies:
        copy.wait()
    for at in range(8):
        dk = turn(dk_ref[at].T, cos_ref[at], sin_ref[at], True)
        d_ref[at, HEAD : 2 * HEAD] = dk.astype(BF16)
        d_ref[at, 2 * HEAD :] = dv_ref[at].T.astype(BF16)
        rows = []
        for j in range(4):
            flat = inverse[4 * at + j]
            start = pl.multiple_of((flat & 1) * BLOCK, BLOCK)
            rows.append(xv_ref[flat // 2, pl.ds(start, BLOCK), :])
        normal, _ = normalise(jnp.concatenate(rows, 0).astype(F32))
        part = dot(d_ref[at], (normal * gain_ref[...]).astype(BF16))
        wt_ref[:192] = part if at == 0 else wt_ref[:192] + part
    for d in range(4):
        start = pl.multiple_of((d // 2) * 256 + ((place[9] ^ d) & 1) * 128, 128)
        columns = (near_ref if d % 2 == 0 else far_ref)[d // 2]
        part = dot(columns.T, obv_ref[pl.ds(start, 128), :])
        wt_ref[192:] = part if d == 0 else wt_ref[192:] + part
    grad_ref[...] = wt_ref[...].T.astype(BF16).reshape(8, 96, 384)
    for b in range(16):
        flat = inverse[b]
        upper = 15 - b
        lo = d_ref[b // 4, :, (b % 4) * BLOCK : (b % 4 + 1) * BLOCK].astype(F32)
        up = d_ref[4 + upper // 4, :, (upper % 4) * BLOCK : (upper % 4 + 1) * BLOCK].astype(F32)
        tile = jnp.concatenate([lo, up], 1)
        turned = jnp.concatenate([up, lo], 1)
        away = (flat // 8 - place[12]) & 3
        all_ref[away, (flat // 2) % 4] = jnp.where(flat % 2 == 0, tile, turned).astype(BF16)
    for k, ref in enumerate((out0_ref, out1_ref, out2_ref, out3_ref)):
        ref[...] = all_ref[k]


def run_backward(
    inverse, place, do, blocks, wide, gain, kept, cosine, sine, id_row, id_column, ob, columns
):
    return pl.pallas_call(
        backward_kernel,
        out_shape=(
            *(SHAPE((4, 3 * HEAD, 2 * BLOCK), BF16),) * 4,
            SHAPE((8, 96, 384), BF16),
        ),
        in_specs=[SMEM] * 2 + [VMEM] + [ANY] * 5 + [VMEM] * 11 + [ANY] + [VMEM] * 2,
        out_specs=(VMEM,) * 5,
        scratch_shapes=[
            pltpu.VMEM((CHUNKS, 3 * HEAD, CHUNK), BF16),
            pltpu.VMEM((CHUNKS, CHUNK, HEAD), F32),
            pltpu.VMEM((CHUNKS, CHUNK, HEAD), F32),
            pltpu.VMEM((CHUNKS, HEAD, CHUNK), BF16),
            pltpu.VMEM((CHUNKS, CHUNK, HEAD), BF16),
            pltpu.VMEM((384, WIDTH), F32),
            pltpu.VMEM((4, 4, 3 * HEAD, 2 * BLOCK), BF16),
            pltpu.VMEM((16, 128, WIDTH), BF16),
            pltpu.VMEM((2 * CHUNK, WIDTH), BF16),
            pltpu.SemaphoreType.DMA((10,)),
        ],
        compiler_params=pltpu.CompilerParams(vmem_limit_bytes=60 << 20),
        cost_estimate=cost(22.0),
        name="attention_backward",
    )(inverse, place, do, *blocks, wide, gain, *kept, cosine, sine, id_row, id_column, ob, *columns)


def pick(core, same, other):
    first = jnp.where(core == 0, same, other)
    return jnp.concatenate([first, jnp.where(core == 0, other, same)], 0)


def assemble(place, units_ref, sems, gu_ref=None, down_ref=None, wout_ref=None):
    copies = []
    parts = ((wout_ref, 144, 96), (gu_ref, 0, 96), (down_ref, 96, 48))
    for target, first, size in parts:
        if target is not None:
            for k in range(8):
                start = ((place[13] ^ (k % 2)) * 4 + k // 2) * size
                rows = target.at[pl.ds(pl.multiple_of(start, 16), size)]
                source = units_ref.at[k // 2, k % 2, first : first + size]
                copies.append(pltpu.make_async_copy(source, rows, sems.at[len(copies)]))
    for copy in copies:
        copy.start()

    def wait(first, last):
        for copy in copies[first:last]:
            copy.wait()

    return wait


def feed_kernel(
    place, own_ref, other_ref, n0_ref, n1_ref, f0_ref, f1_ref, gain_ref, units_ref,
    keep_ref, send_ref, h_ref, d_ref, a_ref, quad_ref, y_ref,
    own_v, other_v, x_v, z_v, gu_v, down_v, wout_v, ob_v, mid_v, h_v, d_v, a_v, keep_v, send_v, y_v,
    sems, unit_sems,
):
    core, member = place[8], place[9]
    started = []

    def copy(source, target):
        started.append(pltpu.make_async_copy(source, target, sems.at[len(started)]))
        started[-1].start()
        return started[-1]

    tiles_in = [copy(own_ref.at[:6], own_v), copy(other_ref.at[:6], other_v)]
    arrays = (n0_ref, n1_ref, f0_ref, f1_ref)
    x_in = [copy(ref.at[:2], x_v.at[k]) for k, ref in enumerate(arrays)]
    units_in = assemble(place, units_ref, unit_sems, gu_v, down_v, wout_v)
    z_in = [copy(ref.at[2:], z_v.at[k]) for k, ref in enumerate(arrays)]

    def rows(i):
        return slice(CHUNK * i, CHUNK * (i + 1))

    def block(ref, i):
        return pick(core, ref[2 * (i % 2), i // 2], ref[2 * (i % 2) + 1, i // 2])

    for part in tiles_in:
        part.wait()
    for i in range(4):
        at = (member // 2) ^ i
        for c in range(2):
            base = CHUNK * i + 128 * c
            for z in range(2):
                tiles = []
                for k in range(2):
                    for x in range(3):
                        mine, theirs = own_v[2 * x + z, 2 * at + c], other_v[2 * x + z, 2 * at + c]
                        tiles.append(jnp.where(core == k, mine, theirs))
                for pair in range(3):
                    left, right = tiles[2 * pair], tiles[2 * pair + 1]
                    lanes = slice(384 * z + 128 * pair, 384 * z + 128 * (pair + 1))
                    ob_v[base : base + BLOCK, lanes] = jnp.concatenate(
                        [left[:, :BLOCK], right[:, :BLOCK]], 1
                    )
                    ob_v[base + BLOCK : base + 128, lanes] = jnp.concatenate(
                        [left[:, BLOCK:], right[:, BLOCK:]], 1
                    )
    out = [copy(ob_v.at[: 2 * CHUNK], quad_ref)]
    for part in x_in:
        part.wait()
    units_in(0, 8)
    for i in range(4):
        middle = block(x_v, i).astype(F32) + dot(ob_v[rows(i)], wout_v[...])
        mid_v[rows(i)] = middle
        normal, _ = normalise(middle)
        h_v[rows(i)] = (normal * gain_ref[...]).astype(BF16)
        out.append(copy(h_v.at[rows(i)], h_ref.at[rows(i)]))
    y_v[...] = mid_v[pl.ds(pl.multiple_of(core * 128, 128), 128), :]
    out.append(copy(y_v, y_ref))
    for part in z_in:
        part.wait()
    units_in(8, 24)
    for i in range(4):
        gu = dot(h_v[rows(i)], gu_v[...])
        g, u = gu[:, :384], gu[:, 384:]
        da = dot(block(z_v, i), down_v[...], 1, 1)
        sigma = jax.nn.sigmoid(g)
        swish = g * sigma
        a_v[rows(i)] = (swish * u).astype(BF16)
        d_v[rows(i), :384] = (da * u * (sigma + swish * (1.0 - sigma))).astype(BF16)
        d_v[rows(i), 384:] = (da * swish).astype(BF16)
        out.append(copy(a_v.at[rows(i)], a_ref.at[rows(i)]))
        out.append(copy(d_v.at[rows(i)], d_ref.at[rows(i)]))
    for i in range(4):
        mid_v[rows(i)] = dot(d_v[rows(i)], gu_v[...], 1, 1)
        keep = pl.multiple_of(CHUNK * i + core * 128, 128)
        send = pl.multiple_of(CHUNK * i + 128 - core * 128, 128)
        keep_v[i] = mid_v[pl.ds(keep, 128), :].astype(BF16)
        send_v[i] = mid_v[pl.ds(send, 128), :].astype(BF16)
        out.append(copy(send_v.at[i], send_ref.at[i]))
        out.append(copy(keep_v.at[i], keep_ref.at[i]))
    for part in out:
        part.wait()


def run_feed(place, own, other, blocks, gain, units):
    rows = 4 * CHUNK
    scratch = [
        ((6, 8, BLOCK, 128), BF16),
        ((6, 8, BLOCK, 128), BF16),
        ((4, 2, 128, WIDTH), BF16),
        ((4, 2, 128, WIDTH), BF16),
        ((WIDTH, WIDTH), BF16),
        ((WIDTH // 2, WIDTH), BF16),
        ((WIDTH, WIDTH), BF16),
        ((rows, WIDTH), BF16),
        ((rows, WIDTH), F32),
        ((rows, WIDTH), BF16),
        ((rows, WIDTH), BF16),
        ((rows, WIDTH // 2), BF16),
        ((4, 128, WIDTH), BF16),
        ((4, 128, WIDTH), BF16),
        ((128, WIDTH), F32),
    ]
    return pl.pallas_call(
        feed_kernel,
        out_shape=(
            SHAPE((4, 128, WIDTH), BF16),
            SHAPE((4, 128, WIDTH), BF16),
            SHAPE((rows, WIDTH), BF16),
            SHAPE((rows, WIDTH), BF16),
            SHAPE((rows, WIDTH // 2), BF16),
            SHAPE((2 * CHUNK, WIDTH), BF16),
            SHAPE((128, WIDTH), F32),
        ),
        in_specs=[SMEM] + [ANY] * 6 + [VMEM, ANY],
        out_specs=(ANY,) * 7,
        scratch_shapes=[pltpu.VMEM(*shape) for shape in scratch]
        + [pltpu.SemaphoreType.DMA((40,)), pltpu.SemaphoreType.DMA((24,))],
        compiler_params=pltpu.CompilerParams(vmem_limit_bytes=60 << 20),
        cost_estimate=cost(40),
        name="feed",
    )(place, own, other, *blocks, gain, units)


def weights_kernel(
    place, h_ref, d_ref, a_ref, z0_ref, z1_ref, z2_ref, z3_ref, units_ref,
    out_ref, keep_ref, send_ref, gu_ref, gd_ref, z_ref, down_ref, sems,
):
    step = pl.program_id(0)

    @pl.when(step == 0)
    def _():
        assemble(place, units_ref, sems, down_ref=down_ref)(0, 8)

    core = place[8]
    dz = [pick(core, z0_ref[0], z1_ref[0]), pick(core, z2_ref[0], z3_ref[0])]
    gu = dot(h_ref[...], d_ref[...], 0, 0)
    gd = dot(a_ref[...], jnp.concatenate(dz, 0), 0, 0)

    @pl.when(step == 0)
    def _():
        gu_ref[...] = gu
        gd_ref[...] = gd

    @pl.when(step > 0)
    def _():
        gu_ref[...] += gu
        gd_ref[...] += gd

    z_ref[...] = dot(a_ref[...], down_ref[...])
    for i in range(2):
        keep = pl.multiple_of(256 * i + core * 128, 128)
        send = pl.multiple_of(256 * i + 128 - core * 128, 128)
        keep_ref[i] = z_ref[pl.ds(keep, 128), :].astype(BF16)
        send_ref[i] = z_ref[pl.ds(send, 128), :].astype(BF16)

    @pl.when(step == 1)
    def _():
        for f in range(8):
            base = (2 * (f % 4) + f // 4) * 144
            out_ref[base : base + 96] = gu_ref[96 * f : 96 * (f + 1)].astype(BF16)
            out_ref[base + 96 : base + 144] = gd_ref[48 * f : 48 * (f + 1)].astype(BF16)


def run_weights(place, h, d, a, blocks, units):
    return pl.pallas_call(
        weights_kernel,
        grid_spec=pltpu.PrefetchScalarGridSpec(
            num_scalar_prefetch=1,
            grid=(2,),
            in_specs=[
                pl.BlockSpec((2 * CHUNK, WIDTH), lambda i, s: (i, 0)),
                pl.BlockSpec((2 * CHUNK, WIDTH), lambda i, s: (i, 0)),
                pl.BlockSpec((2 * CHUNK, WIDTH // 2), lambda i, s: (i, 0)),
                *[pl.BlockSpec((1, 128, WIDTH), lambda i, s: (2 + i, 0, 0))] * 4,
                ANY,
            ],
            out_specs=[
                pl.BlockSpec((8 * 144, WIDTH), lambda i, s: (0, 0)),
                pl.BlockSpec((2, 128, WIDTH), lambda i, s: (i, 0, 0)),
                pl.BlockSpec((2, 128, WIDTH), lambda i, s: (i, 0, 0)),
            ],
            scratch_shapes=[
                pltpu.VMEM((WIDTH, WIDTH), F32),
                pltpu.VMEM((WIDTH // 2, WIDTH), F32),
                pltpu.VMEM((2 * CHUNK, WIDTH), F32),
                pltpu.VMEM((WIDTH // 2, WIDTH), BF16),
                pltpu.SemaphoreType.DMA((8,)),
            ],
        ),
        out_shape=(SHAPE((8 * 144, WIDTH), BF16),) + (SHAPE((4, 128, WIDTH), BF16),) * 2,
        compiler_params=pltpu.CompilerParams(vmem_limit_bytes=60 << 20),
        cost_estimate=cost(9),
        name="weights",
    )(place, h, d, a, *blocks, units)


def middle_kernel(
    place, p0_ref, p1_ref, p2_ref, p3_ref, y_ref, cot_ref, gain_ref, units_ref,
    dy_ref, keep_ref, send_ref, do_ref, columns_ref, wout_ref, sems,
):
    wait = assemble(place, units_ref, sems, wout_ref=wout_ref)
    dh = sum(ref[...].astype(F32) for ref in (p0_ref, p1_ref, p2_ref, p3_ref))
    normal, scale = normalise(y_ref[...])
    dy = cot_ref[...].astype(F32) + norm_back(dh, normal, scale, gain_ref[...])
    dy_ref[...] = dy
    low = dy.astype(BF16)
    wait(0, 8)
    do = dot(wout_ref[...], low, 1, 1).astype(BF16)
    for t in range(4):
        for x in range(4):
            h = 3 * t + min(x, 2)
            do_ref[4 * x + t] = do[HEAD * h : HEAD * (h + 1)]
    for r in range(4):
        columns_ref[place[11] ^ r] = low[:, 192 * r : 192 * (r + 1)]
    keep_ref[...] = columns_ref[:2]
    send_ref[...] = columns_ref[2:]


def run_middle(place, parts, y, cotangent, gain, units):
    return pl.pallas_call(
        middle_kernel,
        out_shape=(
            SHAPE((128, WIDTH), F32),
            *(SHAPE((2, 128, 192), BF16),) * 2,
            SHAPE((16, HEAD, 128), BF16),
        ),
        in_specs=[SMEM] + [VMEM] * 7 + [ANY],
        out_specs=(VMEM,) * 4,
        scratch_shapes=[
            pltpu.VMEM((4, 128, 192), BF16),
            pltpu.VMEM((WIDTH, WIDTH), BF16),
            pltpu.SemaphoreType.DMA((8,)),
        ],
        compiler_params=pltpu.CompilerParams(vmem_limit_bytes=10 << 20),
        cost_estimate=cost(12.0),
        name="middle",
    )(place, *parts, y, cotangent, gain, units)


def inputs_kernel(place, d0_ref, d1_ref, d2_ref, d3_ref, w_ref, keep_ref, send_ref, sum_ref):
    core, column = place[8], place[12]
    for c in range(4):
        for k, ref in enumerate((d0_ref, d1_ref, d2_ref, d3_ref)):
            x = (column - k) & 3
            at = jnp.minimum(x, 2) * HEAD
            w = jnp.concatenate(
                [w_ref[pl.ds(pl.multiple_of(base + at, HEAD), HEAD), :] for base in (0, 192, 384)],
                0,
            )
            part = jnp.where(x < 3, dot(ref[c], w, 0, 0), 0.0)
            sum_ref[c] = part if k == 0 else sum_ref[c] + part
    for z in range(2):
        keep_ref[z] = sum_ref[2 * z + core].astype(BF16)
        send_ref[z] = sum_ref[2 * z + 1 - core].astype(BF16)


def run_inputs(place, parts, w_rows):
    return pl.pallas_call(
        inputs_kernel,
        out_shape=(SHAPE((2, 128, WIDTH), BF16),) * 2,
        in_specs=[SMEM] + [VMEM] * 5,
        out_specs=(VMEM,) * 2,
        scratch_shapes=[pltpu.VMEM((4, 128, WIDTH), F32)],
        compiler_params=pltpu.CompilerParams(vmem_limit_bytes=12 << 20),
        cost_estimate=cost(3),
        name="inputs",
    )(place, *parts, w_rows)


def finish_feed_kernel(
    all_ref, gate_ref, up_ref, gain_ref, g_ref, u_ref, d_ref, n_ref
):
    total = jnp.zeros((96, 1), F32)
    for half, (w_ref, out_ref) in enumerate(((gate_ref, g_ref), (up_ref, u_ref))):
        tiles = []
        for m in range(8):
            part = all_ref[8 * half + m]
            d_ref[48 * m : 48 * (m + 1), 384 * half : 384 * (half + 1)] = part[96:].astype(F32)
            tiles.append(part[:96])
        for f in range(8):
            block = jnp.concatenate([t[:, 48 * f : 48 * (f + 1)] for t in tiles], 1).astype(F32)
            lanes = slice(384 * f, 384 * (f + 1))
            out_ref[:, lanes] = block
            total += jnp.sum(w_ref[:, lanes].astype(F32) * block, axis=1, keepdims=True)
    n_ref[...] = jnp.broadcast_to(total, (96, 128)).T[:1] / gain_ref[...].astype(F32)


def run_finish_feed(whole, gate, up, gain):
    return pl.pallas_call(
        finish_feed_kernel,
        out_shape=(
            SHAPE((96, 3072), F32),
            SHAPE((96, 3072), F32),
            SHAPE((384, WIDTH), F32),
            SHAPE((1, 96), F32),
        ),
        in_specs=[VMEM] * 4,
        out_specs=(VMEM,) * 4,
        compiler_params=pltpu.CompilerParams(vmem_limit_bytes=60 << 20),
        cost_estimate=cost(6),
        name="finish_feed",
    )(whole, gate, up, gain.reshape(1, 96))


def finish_heads_kernel(place, *refs):
    own_ref, other_ref = refs[:2]
    wq_ref, wk_ref, wv_ref, gain_ref, q_ref, k_ref, v_ref, o_ref, n_ref = refs[2:]
    core = place[8]
    tiles = {}
    for x in range(4):
        for z in range(2):
            mine, theirs = own_ref[2 * x + z], other_ref[2 * x + z]
            for k in range(2):
                tiles[x, 2 * z + k] = jnp.where(core == k, mine, theirs).astype(F32)
    total = jnp.zeros((96, 1), F32)
    for j, (w_ref, out_ref) in enumerate(((wq_ref, q_ref), (wk_ref, k_ref), (wv_ref, v_ref))):
        lanes = slice(HEAD * j, HEAD * (j + 1))
        whole = jnp.concatenate([tiles[h % 3, h // 3][:, lanes] for h in range(12)], 1)
        out_ref[...] = whole
        total += jnp.sum(w_ref[...].astype(F32) * whole, axis=1, keepdims=True)
    n_ref[...] = jnp.broadcast_to(total, (96, 128)).T[:1] / gain_ref[...].astype(F32)
    o_ref[...] = jnp.concatenate(
        [sum(tiles[x, t][:, 192:] for x in range(4)) for t in range(4)], 1
    )


def run_finish_heads(place, own, other, query, key, value, gain):
    return pl.pallas_call(
        finish_heads_kernel,
        out_shape=(SHAPE((96, WIDTH), F32),) * 4 + (SHAPE((1, 96), F32),),
        in_specs=[SMEM] + [VMEM] * 6,
        out_specs=(VMEM,) * 5,
        compiler_params=pltpu.CompilerParams(vmem_limit_bytes=12 << 20),
        cost_estimate=cost(8),
        name="finish_heads",
    )(place, own, other, query, key, value, gain.reshape(1, 96))


def fold_kernel(in_ref, out_ref):
    total = jnp.sum(in_ref[...].astype(F32), axis=0).astype(BF16)
    for k in range(8):
        out_ref[k] = total


def run_fold(parts):
    return pl.pallas_call(
        fold_kernel,
        out_shape=SHAPE(parts.shape, BF16),
        in_specs=[VMEM],
        out_specs=VMEM,
        compiler_params=pltpu.CompilerParams(vmem_limit_bytes=6 << 20),
        cost_estimate=cost(0.3),
        name="fold",
    )(parts)


def trade(value, distance):
    return lax.ppermute(value, "ctx", [(i, i ^ distance) for i in range(16)])


def pair_kernel(keep_ref, got_ref, *outs):
    for k, ref in enumerate(outs):
        ref[...] = (keep_ref[k].astype(F32) + got_ref[k].astype(F32)).astype(BF16)


def run_pair(keep, got):
    return pl.pallas_call(
        pair_kernel,
        out_shape=(SHAPE((128, WIDTH), BF16),) * 4,
        in_specs=[VMEM] * 2,
        out_specs=(VMEM,) * 4,
        compiler_params=pltpu.CompilerParams(vmem_limit_bytes=8 << 20),
        cost_estimate=cost(2),
        name="pair",
    )(keep, got)


def norm_back(grad_normed, normal_rows, inverse, gains):
    scaled = grad_normed * gains
    return inverse * (scaled - normal_rows * jnp.mean(scaled * normal_rows, axis=-1, keepdims=True))


def local(
    tokens, block_table, seq_ids, w_query, w_key, w_value, w_out, w_gate, w_up, w_down,
    gain_attn, gain_mlp, cotangent,
):
    index = lax.axis_index("ctx")
    shard = lax.axis_index("fsdp")
    rank, column = index % 4, index // 4
    core, member, group = index % 2, index % 8, index // 8

    rings = [[0, 1, 2, 3], [4, 5, 6, 7]]

    blocks = block_table.reshape(-1)
    numbers = jnp.arange(32, dtype=jnp.int32)
    inverse = jnp.sum(
        jnp.where(blocks[None, :] == numbers[:, None], numbers[None, :], 0), axis=1
    ).astype(jnp.int32)
    frequency = jnp.power(THETA, -(jnp.arange(HALF, dtype=F32) * 2.0) / HEAD)
    own_blocks = lax.dynamic_slice_in_dim(blocks, 8 * column, 8)
    places = (own_blocks[:, None] * BLOCK + jnp.arange(BLOCK, dtype=jnp.int32)).reshape(4, 1, 128)
    angles = places.astype(F32) * frequency[None, :, None]
    place = jnp.stack(
        [(shard // 4 ^ dz) * 4 + (shard + dy) % 4 for dz, dy in RING]
        + [core, member, group, rank, column, shard // 4, index]
    ).astype(jnp.int32)

    units = run_pack_heads(w_query, w_key, w_value, gain_attn, gain_mlp)
    w_heads = lax.all_to_all(units, "fsdp", 0, 0).reshape(WIDTH, 640)
    x_own = after(tokens[0], units)
    x_blocks = [tokens[0], trade(x_own, 1)]
    unit = run_pack_units(w_gate, w_up, w_down, w_out, x_blocks[1])
    x_blocks.append(trade(x_own, 2))
    across = lax.ppermute(after(unit, x_blocks[2]), "fsdp", [(i, i ^ 4) for i in range(8)])
    own = after(jnp.stack([x_own, cotangent[0]]), x_blocks[1])
    own = [own, trade(own, 4), trade(own[0], 8)]
    x_blocks.append(trade(after(x_blocks[2], own, unit), 1))
    w_heads, angles = lax.optimization_barrier((w_heads, (jnp.cos(angles), jnp.sin(angles))))
    *tiles, w_rows = run_project(place, w_heads, x_blocks, *angles)
    gains = w_rows[576:578].astype(F32)
    gain_one, gain_two = gains[:1], gains[1:]

    ids = after(seq_ids[0], w_rows).reshape(32, BLOCK)
    hits = (inverse[16:, None] == numbers[None, :]).astype(jnp.int32)
    ids = jnp.sum(hits[:, :, None] * ids[None], axis=1).reshape(HALF_SEQ)
    id_row, id_column = ids.reshape(1, HALF_SEQ), ids.reshape(HALF_SEQ, 1)
    angles = after(jnp.arange(SEQ, dtype=F32), w_rows).reshape(CHUNKS, 1, CHUNK)
    angles = angles * frequency[None, :, None]
    cosine, sine = jnp.cos(angles), jnp.sin(angles)

    for k in range(1, 4):
        tiles[k] = lax.ppermute(
            tiles[k], "ctx", [(i, (i + 4 * k) % 16) for i in range(16)]
        )
    units = lax.all_gather(
        jnp.stack([unit, after(across, w_rows)]), "fsdp", axis=0, axis_index_groups=rings
    )
    near = jnp.stack([own[0][0], own[1][0], own[0][1], own[1][1]])
    far = trade(after(near, w_rows), 2)
    tiles, cosine, sine = lax.optimization_barrier((tiles, cosine, sine))
    o_tiles, *kept = run_forward(inverse, place, tiles, id_row, id_column)
    o_own = lax.all_to_all(o_tiles, "ctx", 0, 0, axis_index_groups=SAME_CORE)
    blocks = [near, trade(near, 1), far, trade(far, 1)]
    o_other = trade(after(o_own, blocks), 1)
    eights = [list(range(8)), list(range(8, 16))]
    wide = lax.all_gather(after(own[2], o_tiles), "ctx", axis=0, axis_index_groups=eights)

    keep, send, h2, dgu, a, ob, middle = run_feed(
        place, o_own, o_other, blocks, gain_two, units
    )
    pair = run_pair(keep, trade(send, 1))
    parts = [pair[0]] + [trade(pair[k], 2 * k) for k in (1, 2, 3)]

    ff, z_keep, z_send = run_weights(place, after(h2, pair), dgu, a, blocks, units)
    dy1, *columns, do = run_middle(place, after(parts, ff), middle, cotangent[0], gain_two, units)
    ff = lax.psum_scatter(
        ff, "fsdp", scatter_dimension=0, tiled=True, axis_index_groups=rings
    )
    z = run_pair(z_keep, trade(after(z_send, do), 1))
    z = [z[0]] + [trade(z[k], 2 * k) for k in (1, 2, 3)]
    do = lax.all_to_all(do, "ctx", 0, 0)
    columns = jnp.stack([columns[0], trade(columns[1], 2)], 1)
    columns = [columns[0], trade(columns[1], 1)]
    *d_parts, small = run_backward(
        inverse, place, do, blocks, wide, gain_one, kept, cosine, sine, id_row, id_column, ob, columns
    )
    small, ff, z = lax.optimization_barrier((small, ff, z))
    small = lax.all_to_all(small, "fsdp", 0, 0)
    far = shard // 4 == 1
    away = jnp.where(far, ff[:144], ff[144:])
    ff = jnp.where(far, ff[144:], ff[:144])

    def half(value, flip):
        return jnp.where((group == 1) ^ flip, value[:, 384:], value[:, :384])

    def across(value, flip, shift):
        pairs = [(8 * c + f, 8 * (c ^ shift) + (f ^ flip)) for f in range(8) for c in range(16)]
        return lax.ppermute(value, ("ctx", "fsdp"), pairs)

    halves = half(ff, False), half(ff, True), half(away, False), half(away, True)
    parts = [
        halves[0], across(halves[1], 0, 8), across(halves[2], 4, 0), across(halves[3], 4, 8)
    ]
    ff = sum(part.astype(F32) for part in parts).astype(BF16)
    ff = lax.all_gather(ff, "ctx", axis=0)

    folded = run_fold(small)
    for k in range(1, 4):
        d_parts[k] = lax.ppermute(
            after(d_parts[k], folded), "ctx", [(i, (i + 4 * k) % 16) for i in range(16)]
        )
    small = lax.all_to_all(folded, "ctx", 0, 0, axis_index_groups=SAME_CORE)
    total_query, total_key, total_value, total_out, total_gain_one = run_finish_heads(
        place, small, trade(small, 1), w_query, w_key, w_value, gain_attn
    )

    keep, send = run_inputs(place, d_parts, w_rows)
    summed = keep.astype(F32) + trade(send, 1).astype(F32)
    low = rank // 2 == 0
    keep = jnp.where(low, summed[0], summed[1])
    send = jnp.where(low, summed[1], summed[0]).astype(BF16)
    dh1 = keep + trade(send, 2).astype(F32)
    normal_one, inverse_one = normalise(tokens[0].astype(F32))
    grad_stream = dy1 + norm_back(dh1, normal_one, inverse_one, gain_one)
    result = middle + sum(part.astype(F32) for part in z)
    grad_stream, result = grad_stream.astype(BF16), result.astype(BF16)
    ff, grad_stream, result, total_query = lax.optimization_barrier(
        (ff, grad_stream, result, total_query)
    )
    total_gate, total_up, total_down, total_gain_two = run_finish_feed(
        ff, w_gate, w_up, gain_mlp
    )

    return (
        result[None],
        grad_stream[None],
        total_query,
        total_key,
        total_value,
        total_out,
        total_gate,
        total_up,
        total_down,
        total_gain_one.reshape(96),
        total_gain_two.reshape(96),
    )


def solution(mesh):
    rows = P("fsdp", "ctx", None)
    weight = P("fsdp", None)
    return jax.shard_map(
        local,
        mesh=mesh,
        in_specs=(rows, P(), weight) + (weight,) * 7 + (P("fsdp"), P("fsdp"), rows),
        out_specs=(rows, rows) + (weight,) * 7 + (P("fsdp"), P("fsdp")),
        check_vma=False,
    )
```

```python
import jax
import jax.numpy as jnp
from jax import lax
from jax.experimental import pallas as pl
from jax.experimental.pallas import tpu as pltpu
from jax.sharding import PartitionSpec as P

EPS = 1e-05
THETA = 10000.0
WIDTH = 768
HEAD = 64
HALF = 32
SEQ = 2048
BLOCK = 64
CHUNK = 256
CHUNKS = SEQ // CHUNK
HALF_SEQ = SEQ // 2
F32 = jnp.float32
BF16 = jnp.bfloat16

QUADS = [[4 * i + j for j in range(4)] for i in range(4)]
COLUMNS = [[j + 4 * i for i in range(4)] for j in range(4)]
SAME_CORE = [[j + 2 * i for i in range(8)] for j in range(2)]
FOUR_CHIPS = [[8 * g + j + 2 * i for i in range(4)] for g in range(2) for j in range(2)]
RING = [(0, 0), (1, 0), (0, 3), (0, 1), (1, 3), (1, 1), (0, 2), (1, 2)]

VMEM = pl.BlockSpec(memory_space=pltpu.VMEM)
SMEM = pl.BlockSpec(memory_space=pltpu.SMEM)
ANY = pl.BlockSpec(memory_space=pl.ANY)
SHAPE = jax.ShapeDtypeStruct


def cost(microseconds):
    return pl.CostEstimate(
        flops=int(microseconds * 1.1e9), bytes_accessed=int(microseconds * 3.6e6), transcendentals=0
    )


def after(value, *others):
    return lax.optimization_barrier((value, others))[0]


def dot(left, right, left_dim=1, right_dim=0):
    return lax.dot_general(
        left, right, (((left_dim,), (right_dim,)), ((), ())), preferred_element_type=F32
    )


def turn(block, cosine, sine, backward):
    first, second = block[:HALF], block[HALF:]
    if backward:
        return jnp.concatenate([first * cosine + second * sine, second * cosine - first * sine], 0)
    return jnp.concatenate([first * cosine - second * sine, second * cosine + first * sine], 0)


def normalise(x):
    scale = lax.rsqrt(jnp.mean(x * x, axis=-1, keepdims=True) + EPS)
    return x * scale, scale


def document_starts(id_row):
    start = jnp.zeros_like(id_row)
    for number in (1, 2, 3):
        before = jnp.sum((id_row < number).astype(F32), axis=1, keepdims=True).astype(jnp.int32)
        start = jnp.where(id_row >= number, before, start)
    return start


def masked(scores, half, part, starts, other):
    keys = scores.shape[0]
    base = keys - CHUNK
    row = lax.broadcasted_iota(jnp.int32, (CHUNK, CHUNK), 0)
    column = lax.broadcasted_iota(jnp.int32, (CHUNK, CHUNK), 1)
    if half == 1:
        place = lax.broadcasted_iota(jnp.int32, scores.shape, 0)
        inside = place >= starts[:, part * CHUNK : (part + 1) * CHUNK]
        scores = jnp.where(inside, scores, other)
    last = jnp.where(row <= column, scores[base:], other)
    return last if base == 0 else jnp.concatenate([scores[:base], last], 0)


def swap_lanes(tile):
    return jnp.concatenate([tile[:, BLOCK:], tile[:, :BLOCK]], 1)


def sort_tiles(inverse, in_ref, out_ref):
    for b in range(16):
        flat = inverse[b]
        upper = 15 - b
        tile = in_ref[flat // 2].astype(F32)
        tile = jnp.where(flat % 2 == 0, tile, swap_lanes(tile)).astype(BF16)
        out_ref[b // 4, :, (b % 4) * BLOCK : (b % 4 + 1) * BLOCK] = tile[:, :BLOCK]
        out_ref[4 + upper // 4, :, (upper % 4) * BLOCK : (upper % 4 + 1) * BLOCK] = tile[:, BLOCK:]


def pack_heads_kernel(q_ref, k_ref, v_ref, one_ref, two_ref, out_ref):
    rank = lax.axis_index("ctx") & 3
    column = lax.broadcasted_iota(jnp.int32, (96, 64), 1)
    one = jnp.broadcast_to(one_ref[...].astype(F32), (128, 96)).T[:, :64]
    two = jnp.broadcast_to(two_ref[...].astype(F32), (128, 96)).T[:, :64]
    gains = jnp.where(column == 0, one, jnp.where(column == 1, two, 0.0)).astype(BF16)
    for r in range(4):

        @pl.when(rank == r)
        def _():
            lanes = slice(192 * r, 192 * (r + 1))
            unit = jnp.concatenate([q_ref[:, lanes], k_ref[:, lanes], v_ref[:, lanes], gains], 1)
            for f in range(8):
                out_ref[f] = unit


def run_pack_heads(query, key, value, gain_one, gain_two):
    return pl.pallas_call(
        pack_heads_kernel,
        out_shape=SHAPE((8, 96, 640), BF16),
        in_specs=[VMEM] * 5,
        out_specs=VMEM,
        compiler_params=pltpu.CompilerParams(vmem_limit_bytes=60 << 20),
        cost_estimate=cost(2),
        name="pack_heads",
    )(query, key, value, gain_one.reshape(1, 96), gain_two.reshape(1, 96))


def pack_units_kernel(gate_ref, up_ref, down_ref, wout_ref, _, out_ref, both_ref):
    index = lax.axis_index("ctx")
    member = index & 7
    for m in range(8):

        @pl.when(member == m)
        def _():
            parts = [
                ref[:, 384 * f + 48 * m : 384 * f + 48 * (m + 1)]
                for ref in (gate_ref, up_ref)
                for f in range(8)
            ]
            out_ref[:96] = jnp.concatenate(parts, 1)

    out_ref[96:144] = down_ref[pl.ds(pl.multiple_of(member * 48, 16), 48), :]
    out_ref[144:] = wout_ref[...]
    both_ref[0] = out_ref[...]


def run_pack_units(gate, up, down, wout, after):
    return pl.pallas_call(
        pack_units_kernel,
        out_shape=(SHAPE((240, WIDTH), BF16), SHAPE((2, 240, WIDTH), BF16)),
        in_specs=[VMEM] * 4 + [ANY],
        out_specs=(VMEM, VMEM),
        compiler_params=pltpu.CompilerParams(vmem_limit_bytes=60 << 20),
        cost_estimate=cost(2.4),
        name="pack_units",
    )(gate, up, down, wout, after)


def project_kernel(
    place, w_ref, x0_ref, x1_ref, x2_ref, x3_ref, cos_ref, sin_ref,
    out0_ref, out1_ref, out2_ref, out3_ref, wt_ref, out_ref,
):
    wt_ref[...] = w_ref[...].T
    gain = wt_ref[576:592].astype(F32)[:1]
    for d, block in enumerate((x0_ref, x1_ref, x2_ref, x3_ref)):
        c = place[11] ^ d
        normal, _ = normalise(block[...].astype(F32))
        h = (normal * gain).astype(BF16)
        qkv = dot(wt_ref[:576], h, 1, 1)
        cosine, sine = cos_ref[c], sin_ref[c]
        for j in range(3):
            at = HEAD * j
            q = (turn(qkv[at : at + HEAD], cosine, sine, False).astype(BF16) * 0.125).astype(BF16)
            k = turn(qkv[192 + at : 192 + at + HEAD], cosine, sine, False).astype(BF16)
            v = qkv[384 + at : 384 + at + HEAD].astype(BF16)
            for target in (2, 3) if j == 2 else (j,):
                away = (target - place[12]) & 3
                out_ref[away, c, :HEAD] = q
                out_ref[away, c, HEAD : 2 * HEAD] = k
                out_ref[away, c, 2 * HEAD :] = v
    for k, ref in enumerate((out0_ref, out1_ref, out2_ref, out3_ref)):
        ref[...] = out_ref[k]


def run_project(place, w, blocks, cosine, sine):
    return pl.pallas_call(
        project_kernel,
        out_shape=(SHAPE((4, 3 * HEAD, 128), BF16),) * 4 + (SHAPE((640, WIDTH), BF16),),
        in_specs=[SMEM] + [VMEM] * 7,
        out_specs=(VMEM,) * 5,
        scratch_shapes=[pltpu.VMEM((4, 4, 3 * HEAD, 128), BF16)],
        compiler_params=pltpu.CompilerParams(vmem_limit_bytes=14 << 20),
        cost_estimate=cost(40),
        name="project",
    )(place, w, *blocks, cosine, sine)


def forward_kernel(
    inverse, place, in0_ref, in1_ref, in2_ref, in3_ref, id_row,
    out_ref, q_ref, k_ref, v_ref, krow_ref, o_ref, lse_ref, all_ref, orow_ref, in_ref,
):
    for k, ref in enumerate((in0_ref, in1_ref, in2_ref, in3_ref)):
        in_ref[pl.ds(4 * ((place[12] - k) & 3), 4)] = ref[...]
    sort_tiles(inverse, in_ref, all_ref)
    starts = document_starts(id_row[...])
    for at in range(CHUNKS):
        q_ref[at] = all_ref[at, :HEAD]
        k_ref[at] = all_ref[at, HEAD : 2 * HEAD]
        v_ref[at] = all_ref[at, 2 * HEAD :]
        krow_ref[at] = all_ref[at, HEAD : 2 * HEAD].T
    for half in range(2):
        for part in range(4):
            at = 4 * half + part
            keys = (part + 1) * CHUNK
            k = krow_ref[4 * half : 4 * half + part + 1].reshape(keys, HEAD)
            s = dot(k, q_ref[at])
            s = masked(s, half, part, starts, -1e30)
            top = jnp.max(s, axis=0, keepdims=True)
            p = jnp.exp(s - top)
            total = jnp.sum(p, axis=0, keepdims=True)
            low = p.astype(BF16)
            o = dot(v_ref[4 * half], low[:CHUNK])
            for j in range(1, part + 1):
                o += dot(v_ref[4 * half + j], low[j * CHUNK : (j + 1) * CHUNK])
            o = o / total
            o_ref[at] = o
            orow_ref[at] = o.T
            lse_ref[at] = top + jnp.log(total)
    for b in range(16):
        flat = inverse[b]
        upper = 15 - b
        lo = orow_ref[b // 4, (b % 4) * BLOCK : (b % 4 + 1) * BLOCK, :]
        up = orow_ref[4 + upper // 4, (upper % 4) * BLOCK : (upper % 4 + 1) * BLOCK, :]
        tile = jnp.concatenate([lo, up], 1)
        turned = jnp.concatenate([up, lo], 1)
        tile = jnp.where(flat % 2 == 0, tile, turned).astype(BF16)
        group = flat // 16
        for chip in range(4):
            out_ref[4 * group + chip, (flat // 2) % 8] = tile


def run_forward(inverse, place, tiles, id_row):
    return pl.pallas_call(
        forward_kernel,
        out_shape=(
            SHAPE((8, 8, BLOCK, 128), BF16),
            SHAPE((CHUNKS, HEAD, CHUNK), BF16),
            SHAPE((CHUNKS, HEAD, CHUNK), BF16),
            SHAPE((CHUNKS, HEAD, CHUNK), BF16),
            SHAPE((CHUNKS, CHUNK, HEAD), BF16),
            SHAPE((CHUNKS, HEAD, CHUNK), F32),
            SHAPE((CHUNKS, 1, CHUNK), F32),
        ),
        in_specs=[SMEM] * 2 + [VMEM] * 5,
        out_specs=(VMEM,) * 7,
        scratch_shapes=[
            pltpu.VMEM((CHUNKS, 3 * HEAD, CHUNK), BF16),
            pltpu.VMEM((CHUNKS, CHUNK, HEAD), F32),
            pltpu.VMEM((16, 3 * HEAD, 128), BF16),
        ],
        compiler_params=pltpu.CompilerParams(vmem_limit_bytes=60 << 20),
        cost_estimate=cost(40),
        name="attention_forward",
    )(inverse, place, *tiles, id_row)


def backward_kernel(
    inverse, place, do_ref, b0_ref, b1_ref, b2_ref, b3_ref, wide_ref, gain_ref,
    q_ref, k_ref, v_ref, krow_ref, o_ref, lse_ref, cos_ref, sin_ref,
    id_row, ob_ref, near_ref, far_ref,
    out0_ref, out1_ref, out2_ref, out3_ref, grad_ref,
    d_ref, dk_ref, dv_ref, dot_ref, vrow_ref, wt_ref, all_ref, xv_ref, obv_ref, xsem,
):
    other = xv_ref.at[pl.ds(8 - 8 * place[10], 8)]
    copies = [
        pltpu.make_async_copy(ob_ref, obv_ref, xsem.at[8]),
        pltpu.make_async_copy(wide_ref, other, xsem.at[9]),
    ]
    for k, ref in enumerate((b0_ref, b1_ref, b2_ref, b3_ref)):
        for j in range(2):
            at = place[14] ^ (k + 4 * j)
            copies.append(pltpu.make_async_copy(ref.at[j], xv_ref.at[at], xsem.at[2 * k + j]))
    for copy in copies:
        copy.start()
    sort_tiles(inverse, do_ref, dot_ref)
    starts = document_starts(id_row[...])
    for half in range(2):
        for part in range(4):
            at = 4 * half + part
            vrow_ref[at] = v_ref[at].T
            keys = (part + 1) * CHUNK
            first = 4 * half
            k = krow_ref[first : first + part + 1].reshape(keys, HEAD)
            v = vrow_ref[first : first + part + 1].reshape(keys, HEAD)
            q = q_ref[at]
            do = dot_ref[at]
            delta = jnp.sum(do.astype(F32) * o_ref[at], axis=0, keepdims=True)
            s = dot(k, q) - lse_ref[at]
            p = jnp.exp(masked(s, half, part, starts, -1e30))
            ds = (p * (dot(v, do) - delta)).astype(BF16)
            dv = dot(p.astype(BF16), do.T).reshape(part + 1, CHUNK, HEAD)
            dk = dot(ds, q.T).reshape(part + 1, CHUNK, HEAD)
            if part:
                dv_ref[first : first + part] += dv[:part]
                dk_ref[first : first + part] += dk[:part]
            dv_ref[at] = dv[part]
            dk_ref[at] = dk[part]
            dq = dot(k_ref[first], ds[:CHUNK])
            for j in range(1, part + 1):
                dq += dot(k_ref[first + j], ds[j * CHUNK : (j + 1) * CHUNK])
            d_ref[at, :HEAD] = turn(dq * 0.125, cos_ref[at], sin_ref[at], True).astype(BF16)
    for copy in copies:
        copy.wait()
    for at in range(8):
        dk = turn(dk_ref[at].T, cos_ref[at], sin_ref[at], True)
        d_ref[at, HEAD : 2 * HEAD] = dk.astype(BF16)
        d_ref[at, 2 * HEAD :] = dv_ref[at].T.astype(BF16)
        rows = []
        for j in range(4):
            flat = inverse[4 * at + j]
            start = pl.multiple_of((flat & 1) * BLOCK, BLOCK)
            rows.append(xv_ref[flat // 2, pl.ds(start, BLOCK), :])
        normal, _ = normalise(jnp.concatenate(rows, 0).astype(F32))
        part = dot(d_ref[at], (normal * gain_ref[...]).astype(BF16))
        wt_ref[:192] = part if at == 0 else wt_ref[:192] + part
    for d in range(4):
        start = pl.multiple_of((d // 2) * 256 + ((place[9] ^ d) & 1) * 128, 128)
        columns = (near_ref if d % 2 == 0 else far_ref)[d // 2]
        part = dot(columns.T, obv_ref[pl.ds(start, 128), :])
        wt_ref[192:] = part if d == 0 else wt_ref[192:] + part
    grad_ref[...] = wt_ref[...].T.astype(BF16).reshape(8, 96, 384)
    for b in range(16):
        flat = inverse[b]
        upper = 15 - b
        lo = d_ref[b // 4, :, (b % 4) * BLOCK : (b % 4 + 1) * BLOCK].astype(F32)
        up = d_ref[4 + upper // 4, :, (upper % 4) * BLOCK : (upper % 4 + 1) * BLOCK].astype(F32)
        tile = jnp.concatenate([lo, up], 1)
        turned = jnp.concatenate([up, lo], 1)
        away = (flat // 8 - place[12]) & 3
        all_ref[away, (flat // 2) % 4] = jnp.where(flat % 2 == 0, tile, turned).astype(BF16)
    for k, ref in enumerate((out0_ref, out1_ref, out2_ref, out3_ref)):
        ref[...] = all_ref[k]


def run_backward(
    inverse, place, do, blocks, wide, gain, kept, cosine, sine, id_row, ob, columns
):
    return pl.pallas_call(
        backward_kernel,
        out_shape=(
            *(SHAPE((4, 3 * HEAD, 2 * BLOCK), BF16),) * 4,
            SHAPE((8, 96, 384), BF16),
        ),
        in_specs=[SMEM] * 2 + [VMEM] + [ANY] * 5 + [VMEM] * 10 + [ANY] + [VMEM] * 2,
        out_specs=(VMEM,) * 5,
        scratch_shapes=[
            pltpu.VMEM((CHUNKS, 3 * HEAD, CHUNK), BF16),
            pltpu.VMEM((CHUNKS, CHUNK, HEAD), F32),
            pltpu.VMEM((CHUNKS, CHUNK, HEAD), F32),
            pltpu.VMEM((CHUNKS, HEAD, CHUNK), BF16),
            pltpu.VMEM((CHUNKS, CHUNK, HEAD), BF16),
            pltpu.VMEM((384, WIDTH), F32),
            pltpu.VMEM((4, 4, 3 * HEAD, 2 * BLOCK), BF16),
            pltpu.VMEM((16, 128, WIDTH), BF16),
            pltpu.VMEM((2 * CHUNK, WIDTH), BF16),
            pltpu.SemaphoreType.DMA((10,)),
        ],
        compiler_params=pltpu.CompilerParams(vmem_limit_bytes=60 << 20),
        cost_estimate=cost(22.0),
        name="attention_backward",
    )(inverse, place, do, *blocks, wide, gain, *kept, cosine, sine, id_row, ob, *columns)


def pick(core, same, other):
    first = jnp.where(core == 0, same, other)
    return jnp.concatenate([first, jnp.where(core == 0, other, same)], 0)


def assemble(place, units_ref, sems, gu_ref=None, down_ref=None, wout_ref=None):
    copies = []
    parts = ((wout_ref, 144, 96), (gu_ref, 0, 96), (down_ref, 96, 48))
    for target, first, size in parts:
        if target is not None:
            for k in range(8):
                start = ((place[13] ^ (k % 2)) * 4 + k // 2) * size
                rows = target.at[pl.ds(pl.multiple_of(start, 16), size)]
                source = units_ref.at[k // 2, k % 2, first : first + size]
                copies.append(pltpu.make_async_copy(source, rows, sems.at[len(copies)]))
    for copy in copies:
        copy.start()

    def wait(first, last):
        for copy in copies[first:last]:
            copy.wait()

    return wait


def feed_kernel(
    place, own_ref, other_ref, n0_ref, n1_ref, f0_ref, f1_ref, gain_ref, units_ref,
    keep_ref, send_ref, h_ref, d_ref, a_ref, quad_ref, y_ref, wout_ref,
    own_v, other_v, x_v, z_v, gu_v, down_v, wout_v, ob_v, mid_v, h_v, d_v, a_v, keep_v, send_v, y_v,
    sems, unit_sems,
):
    core, member = place[8], place[9]
    started = []

    def copy(source, target):
        started.append(pltpu.make_async_copy(source, target, sems.at[len(started)]))
        started[-1].start()
        return started[-1]

    tiles_in = [copy(own_ref.at[:6], own_v), copy(other_ref.at[:6], other_v)]
    arrays = (n0_ref, n1_ref, f0_ref, f1_ref)
    x_in = [copy(ref.at[:2], x_v.at[k]) for k, ref in enumerate(arrays)]
    units_in = assemble(place, units_ref, unit_sems, gu_v, down_v, wout_v)
    z_in = [copy(ref.at[2:], z_v.at[k]) for k, ref in enumerate(arrays)]

    def rows(i):
        return slice(CHUNK * i, CHUNK * (i + 1))

    def block(ref, i):
        return pick(core, ref[2 * (i % 2), i // 2], ref[2 * (i % 2) + 1, i // 2])

    for part in tiles_in:
        part.wait()
    for i in range(4):
        at = (member // 2) ^ i
        for c in range(2):
            base = CHUNK * i + 128 * c
            for z in range(2):
                tiles = []
                for k in range(2):
                    for x in range(3):
                        mine, theirs = own_v[2 * x + z, 2 * at + c], other_v[2 * x + z, 2 * at + c]
                        tiles.append(jnp.where(core == k, mine, theirs))
                for pair in range(3):
                    left, right = tiles[2 * pair], tiles[2 * pair + 1]
                    lanes = slice(384 * z + 128 * pair, 384 * z + 128 * (pair + 1))
                    ob_v[base : base + BLOCK, lanes] = jnp.concatenate(
                        [left[:, :BLOCK], right[:, :BLOCK]], 1
                    )
                    ob_v[base + BLOCK : base + 128, lanes] = jnp.concatenate(
                        [left[:, BLOCK:], right[:, BLOCK:]], 1
                    )
    out = [copy(ob_v.at[: 2 * CHUNK], quad_ref)]
    for part in x_in:
        part.wait()
    units_in(0, 8)
    out.append(copy(wout_v, wout_ref))
    for i in range(4):
        middle = block(x_v, i).astype(F32) + dot(ob_v[rows(i)], wout_v[...])
        mid_v[rows(i)] = middle
        normal, _ = normalise(middle)
        h_v[rows(i)] = (normal * gain_ref[...]).astype(BF16)
        out.append(copy(h_v.at[rows(i)], h_ref.at[rows(i)]))
    y_v[...] = mid_v[pl.ds(pl.multiple_of(core * 128, 128), 128), :]
    out.append(copy(y_v, y_ref))
    for part in z_in:
        part.wait()
    units_in(8, 24)
    for i in range(4):
        gu = dot(h_v[rows(i)], gu_v[...])
        g, u = gu[:, :384], gu[:, 384:]
        da = dot(block(z_v, i), down_v[...], 1, 1)
        sigma = jax.nn.sigmoid(g)
        swish = g * sigma
        a_v[rows(i)] = (swish * u).astype(BF16)
        d_v[rows(i), :384] = (da * u * (sigma + swish * (1.0 - sigma))).astype(BF16)
        d_v[rows(i), 384:] = (da * swish).astype(BF16)
        out.append(copy(a_v.at[rows(i)], a_ref.at[rows(i)]))
        out.append(copy(d_v.at[rows(i)], d_ref.at[rows(i)]))
    for i in range(4):
        mid_v[rows(i)] = dot(d_v[rows(i)], gu_v[...], 1, 1)
        keep = pl.multiple_of(CHUNK * i + core * 128, 128)
        send = pl.multiple_of(CHUNK * i + 128 - core * 128, 128)
        keep_v[i] = mid_v[pl.ds(keep, 128), :].astype(BF16)
        send_v[i] = mid_v[pl.ds(send, 128), :].astype(BF16)
        out.append(copy(send_v.at[i], send_ref.at[i]))
        out.append(copy(keep_v.at[i], keep_ref.at[i]))
    for part in out:
        part.wait()


def run_feed(place, own, other, blocks, gain, units):
    rows = 4 * CHUNK
    scratch = [
        ((6, 8, BLOCK, 128), BF16),
        ((6, 8, BLOCK, 128), BF16),
        ((4, 2, 128, WIDTH), BF16),
        ((4, 2, 128, WIDTH), BF16),
        ((WIDTH, WIDTH), BF16),
        ((WIDTH // 2, WIDTH), BF16),
        ((WIDTH, WIDTH), BF16),
        ((rows, WIDTH), BF16),
        ((rows, WIDTH), F32),
        ((rows, WIDTH), BF16),
        ((rows, WIDTH), BF16),
        ((rows, WIDTH // 2), BF16),
        ((4, 128, WIDTH), BF16),
        ((4, 128, WIDTH), BF16),
        ((128, WIDTH), F32),
    ]
    return pl.pallas_call(
        feed_kernel,
        out_shape=(
            SHAPE((4, 128, WIDTH), BF16),
            SHAPE((4, 128, WIDTH), BF16),
            SHAPE((rows, WIDTH), BF16),
            SHAPE((rows, WIDTH), BF16),
            SHAPE((rows, WIDTH // 2), BF16),
            SHAPE((2 * CHUNK, WIDTH), BF16),
            SHAPE((128, WIDTH), F32),
            SHAPE((WIDTH, WIDTH), BF16),
        ),
        in_specs=[SMEM] + [ANY] * 6 + [VMEM, ANY],
        out_specs=(ANY,) * 8,
        scratch_shapes=[pltpu.VMEM(*shape) for shape in scratch]
        + [pltpu.SemaphoreType.DMA((40,)), pltpu.SemaphoreType.DMA((24,))],
        compiler_params=pltpu.CompilerParams(vmem_limit_bytes=60 << 20),
        cost_estimate=cost(40),
        name="feed",
    )(place, own, other, *blocks, gain, units)


def weights_kernel(
    place, h_ref, d_ref, a_ref, z0_ref, z1_ref, z2_ref, z3_ref, units_ref,
    out_ref, keep_ref, send_ref, gu_ref, gd_ref, z_ref, down_ref, sems,
):
    step = pl.program_id(0)

    @pl.when(step == 0)
    def _():
        assemble(place, units_ref, sems, down_ref=down_ref)(0, 8)

    core = place[8]
    dz = [pick(core, z0_ref[0], z1_ref[0]), pick(core, z2_ref[0], z3_ref[0])]
    gu = dot(h_ref[...], d_ref[...], 0, 0)
    gd = dot(a_ref[...], jnp.concatenate(dz, 0), 0, 0)

    @pl.when(step == 0)
    def _():
        gu_ref[...] = gu
        gd_ref[...] = gd

    @pl.when(step > 0)
    def _():
        gu_ref[...] += gu
        gd_ref[...] += gd

    z_ref[...] = dot(a_ref[...], down_ref[...])
    for i in range(2):
        keep = pl.multiple_of(256 * i + core * 128, 128)
        send = pl.multiple_of(256 * i + 128 - core * 128, 128)
        keep_ref[i] = z_ref[pl.ds(keep, 128), :].astype(BF16)
        send_ref[i] = z_ref[pl.ds(send, 128), :].astype(BF16)

    @pl.when(step == 1)
    def _():
        for f in range(8):
            base = (2 * (f % 4) + f // 4) * 144
            out_ref[base : base + 96] = gu_ref[96 * f : 96 * (f + 1)].astype(BF16)
            out_ref[base + 96 : base + 144] = gd_ref[48 * f : 48 * (f + 1)].astype(BF16)


def run_weights(place, h, d, a, blocks, units):
    return pl.pallas_call(
        weights_kernel,
        grid_spec=pltpu.PrefetchScalarGridSpec(
            num_scalar_prefetch=1,
            grid=(2,),
            in_specs=[
                pl.BlockSpec((2 * CHUNK, WIDTH), lambda i, s: (i, 0)),
                pl.BlockSpec((2 * CHUNK, WIDTH), lambda i, s: (i, 0)),
                pl.BlockSpec((2 * CHUNK, WIDTH // 2), lambda i, s: (i, 0)),
                *[pl.BlockSpec((1, 128, WIDTH), lambda i, s: (2 + i, 0, 0))] * 4,
                ANY,
            ],
            out_specs=[
                pl.BlockSpec((8 * 144, WIDTH), lambda i, s: (0, 0)),
                pl.BlockSpec((2, 128, WIDTH), lambda i, s: (i, 0, 0)),
                pl.BlockSpec((2, 128, WIDTH), lambda i, s: (i, 0, 0)),
            ],
            scratch_shapes=[
                pltpu.VMEM((WIDTH, WIDTH), F32),
                pltpu.VMEM((WIDTH // 2, WIDTH), F32),
                pltpu.VMEM((2 * CHUNK, WIDTH), F32),
                pltpu.VMEM((WIDTH // 2, WIDTH), BF16),
                pltpu.SemaphoreType.DMA((8,)),
            ],
        ),
        out_shape=(SHAPE((8 * 144, WIDTH), BF16),) + (SHAPE((4, 128, WIDTH), BF16),) * 2,
        compiler_params=pltpu.CompilerParams(vmem_limit_bytes=60 << 20),
        cost_estimate=cost(9),
        name="weights",
    )(place, h, d, a, *blocks, units)


def middle_kernel(
    place, p0_ref, p1_ref, p2_ref, p3_ref, y_ref, cot_ref, gain_ref, wout_ref,
    dy_ref, keep_ref, send_ref, do_ref, columns_ref,
):
    dh = sum(ref[...].astype(F32) for ref in (p0_ref, p1_ref, p2_ref, p3_ref))
    normal, scale = normalise(y_ref[...])
    dy = cot_ref[...].astype(F32) + norm_back(dh, normal, scale, gain_ref[...])
    dy_ref[...] = dy
    low = dy.astype(BF16)
    do = dot(wout_ref[...], low, 1, 1).astype(BF16)
    for t in range(4):
        for x in range(4):
            h = 3 * t + min(x, 2)
            do_ref[4 * x + t] = do[HEAD * h : HEAD * (h + 1)]
    for r in range(4):
        columns_ref[place[11] ^ r] = low[:, 192 * r : 192 * (r + 1)]
    keep_ref[...] = columns_ref[:2]
    send_ref[...] = columns_ref[2:]


def run_middle(place, parts, y, cotangent, gain, wout):
    return pl.pallas_call(
        middle_kernel,
        out_shape=(
            SHAPE((128, WIDTH), F32),
            *(SHAPE((2, 128, 192), BF16),) * 2,
            SHAPE((16, HEAD, 128), BF16),
        ),
        in_specs=[SMEM] + [VMEM] * 8,
        out_specs=(VMEM,) * 4,
        scratch_shapes=[
            pltpu.VMEM((4, 128, 192), BF16),
        ],
        compiler_params=pltpu.CompilerParams(vmem_limit_bytes=10 << 20),
        cost_estimate=cost(12.0),
        name="middle",
    )(place, *parts, y, cotangent, gain, wout)


def inputs_kernel(place, d0_ref, d1_ref, d2_ref, d3_ref, w_ref, keep_ref, send_ref, sum_ref):
    core, column = place[8], place[12]
    for c in range(4):
        for k, ref in enumerate((d0_ref, d1_ref, d2_ref, d3_ref)):
            x = (column - k) & 3
            at = jnp.minimum(x, 2) * HEAD
            w = jnp.concatenate(
                [w_ref[pl.ds(pl.multiple_of(base + at, HEAD), HEAD), :] for base in (0, 192, 384)],
                0,
            )
            part = jnp.where(x < 3, dot(ref[c], w, 0, 0), 0.0)
            sum_ref[c] = part if k == 0 else sum_ref[c] + part
    for z in range(2):
        keep_ref[z] = sum_ref[2 * z + core].astype(BF16)
        send_ref[z] = sum_ref[2 * z + 1 - core].astype(BF16)


def run_inputs(place, parts, w_rows):
    return pl.pallas_call(
        inputs_kernel,
        out_shape=(SHAPE((2, 128, WIDTH), BF16),) * 2,
        in_specs=[SMEM] + [VMEM] * 5,
        out_specs=(VMEM,) * 2,
        scratch_shapes=[pltpu.VMEM((4, 128, WIDTH), F32)],
        compiler_params=pltpu.CompilerParams(vmem_limit_bytes=12 << 20),
        cost_estimate=cost(3),
        name="inputs",
    )(place, *parts, w_rows)


def finish_feed_kernel(
    all_ref, gate_ref, up_ref, gain_ref, g_ref, u_ref, d_ref, n_ref
):
    total = jnp.zeros((96, 1), F32)
    for half, (w_ref, out_ref) in enumerate(((gate_ref, g_ref), (up_ref, u_ref))):
        tiles = []
        for m in range(8):
            part = all_ref[8 * half + m]
            d_ref[48 * m : 48 * (m + 1), 384 * half : 384 * (half + 1)] = part[96:].astype(F32)
            tiles.append(part[:96])
        for f in range(8):
            block = jnp.concatenate([t[:, 48 * f : 48 * (f + 1)] for t in tiles], 1).astype(F32)
            lanes = slice(384 * f, 384 * (f + 1))
            out_ref[:, lanes] = block
            total += jnp.sum(w_ref[:, lanes].astype(F32) * block, axis=1, keepdims=True)
    n_ref[...] = jnp.broadcast_to(total, (96, 128)).T[:1] / gain_ref[...].astype(F32)


def run_finish_feed(whole, gate, up, gain):
    return pl.pallas_call(
        finish_feed_kernel,
        out_shape=(
            SHAPE((96, 3072), F32),
            SHAPE((96, 3072), F32),
            SHAPE((384, WIDTH), F32),
            SHAPE((1, 96), F32),
        ),
        in_specs=[VMEM] * 4,
        out_specs=(VMEM,) * 4,
        compiler_params=pltpu.CompilerParams(vmem_limit_bytes=60 << 20),
        cost_estimate=cost(6),
        name="finish_feed",
    )(whole, gate, up, gain.reshape(1, 96))


def finish_heads_kernel(place, *refs):
    own_ref, other_ref = refs[:2]
    wq_ref, wk_ref, wv_ref, gain_ref, q_ref, k_ref, v_ref, o_ref, n_ref = refs[2:]
    core = place[8]
    tiles = {}
    for x in range(4):
        for z in range(2):
            mine, theirs = own_ref[2 * x + z], other_ref[2 * x + z]
            for k in range(2):
                tiles[x, 2 * z + k] = jnp.where(core == k, mine, theirs).astype(F32)
    total = jnp.zeros((96, 1), F32)
    for j, (w_ref, out_ref) in enumerate(((wq_ref, q_ref), (wk_ref, k_ref), (wv_ref, v_ref))):
        lanes = slice(HEAD * j, HEAD * (j + 1))
        whole = jnp.concatenate([tiles[h % 3, h // 3][:, lanes] for h in range(12)], 1)
        out_ref[...] = whole
        total += jnp.sum(w_ref[...].astype(F32) * whole, axis=1, keepdims=True)
    n_ref[...] = jnp.broadcast_to(total, (96, 128)).T[:1] / gain_ref[...].astype(F32)
    o_ref[...] = jnp.concatenate(
        [sum(tiles[x, t][:, 192:] for x in range(4)) for t in range(4)], 1
    )


def run_finish_heads(place, own, other, query, key, value, gain):
    return pl.pallas_call(
        finish_heads_kernel,
        out_shape=(SHAPE((96, WIDTH), F32),) * 4 + (SHAPE((1, 96), F32),),
        in_specs=[SMEM] + [VMEM] * 6,
        out_specs=(VMEM,) * 5,
        compiler_params=pltpu.CompilerParams(vmem_limit_bytes=12 << 20),
        cost_estimate=cost(8),
        name="finish_heads",
    )(place, own, other, query, key, value, gain.reshape(1, 96))


def fold_kernel(in_ref, out_ref):
    total = jnp.sum(in_ref[...].astype(F32), axis=0).astype(BF16)
    for k in range(8):
        out_ref[k] = total


def run_fold(parts):
    return pl.pallas_call(
        fold_kernel,
        out_shape=SHAPE(parts.shape, BF16),
        in_specs=[VMEM],
        out_specs=VMEM,
        compiler_params=pltpu.CompilerParams(vmem_limit_bytes=6 << 20),
        cost_estimate=cost(0.3),
        name="fold",
    )(parts)


def trade(value, distance):
    return lax.ppermute(value, "ctx", [(i, i ^ distance) for i in range(16)])


def pair_kernel(keep_ref, got_ref, *outs):
    for k, ref in enumerate(outs):
        ref[...] = (keep_ref[k].astype(F32) + got_ref[k].astype(F32)).astype(BF16)


def run_pair(keep, got):
    return pl.pallas_call(
        pair_kernel,
        out_shape=(SHAPE((128, WIDTH), BF16),) * 4,
        in_specs=[VMEM] * 2,
        out_specs=(VMEM,) * 4,
        compiler_params=pltpu.CompilerParams(vmem_limit_bytes=8 << 20),
        cost_estimate=cost(2),
        name="pair",
    )(keep, got)


def norm_back(grad_normed, normal_rows, inverse, gains):
    scaled = grad_normed * gains
    return inverse * (scaled - normal_rows * jnp.mean(scaled * normal_rows, axis=-1, keepdims=True))


def local(
    tokens, block_table, seq_ids, w_query, w_key, w_value, w_out, w_gate, w_up, w_down,
    gain_attn, gain_mlp, cotangent,
):
    index = lax.axis_index("ctx")
    shard = lax.axis_index("fsdp")
    rank, column = index % 4, index // 4
    core, member, group = index % 2, index % 8, index // 8

    rings = [[0, 1, 2, 3], [4, 5, 6, 7]]

    blocks = block_table.reshape(-1)
    numbers = jnp.arange(32, dtype=jnp.int32)
    inverse = jnp.sum(
        jnp.where(blocks[None, :] == numbers[:, None], numbers[None, :], 0), axis=1
    ).astype(jnp.int32)
    frequency = jnp.power(THETA, -(jnp.arange(HALF, dtype=F32) * 2.0) / HEAD)
    own_blocks = lax.dynamic_slice_in_dim(blocks, 8 * column, 8)
    places = (own_blocks[:, None] * BLOCK + jnp.arange(BLOCK, dtype=jnp.int32)).reshape(4, 1, 128)
    angles = places.astype(F32) * frequency[None, :, None]
    place = jnp.stack(
        [(shard // 4 ^ dz) * 4 + (shard + dy) % 4 for dz, dy in RING]
        + [core, member, group, rank, column, shard // 4, index]
    ).astype(jnp.int32)

    units = run_pack_heads(w_query, w_key, w_value, gain_attn, gain_mlp)
    w_heads = lax.all_to_all(units, "fsdp", 0, 0).reshape(WIDTH, 640)
    x_own = after(tokens[0], units)
    x_blocks = [tokens[0], trade(x_own, 1)]
    unit, both = run_pack_units(w_gate, w_up, w_down, w_out, x_blocks[1])
    x_blocks.append(trade(x_own, 2))
    across = lax.ppermute(after(unit, x_blocks[2]), "fsdp", [(i, i ^ 4) for i in range(8)])
    own = after(jnp.stack([x_own, cotangent[0]]), x_blocks[1])
    own = [own, trade(own, 4), trade(own[0], 8)]
    x_blocks.append(trade(after(x_blocks[2], own, unit), 1))
    w_heads, angles = lax.optimization_barrier((w_heads, (jnp.cos(angles), jnp.sin(angles))))
    *tiles, w_rows = run_project(place, w_heads, x_blocks, *angles)
    gains = w_rows[576:578].astype(F32)
    gain_one, gain_two = gains[:1], gains[1:]

    ids = after(seq_ids[0], w_rows).reshape(32, BLOCK)
    hits = (inverse[16:, None] == numbers[None, :]).astype(jnp.int32)
    ids = jnp.sum(hits[:, :, None] * ids[None], axis=1).reshape(HALF_SEQ)
    id_row = ids.reshape(1, HALF_SEQ)
    angles = after(jnp.arange(SEQ, dtype=F32), w_rows).reshape(CHUNKS, 1, CHUNK)
    angles = angles * frequency[None, :, None]
    cosine, sine = jnp.cos(angles), jnp.sin(angles)

    for k in range(1, 4):
        tiles[k] = lax.ppermute(
            tiles[k], "ctx", [(i, (i + 4 * k) % 16) for i in range(16)]
        )
    units = lax.all_gather(
        both.at[1].set(after(across, w_rows)), "fsdp", axis=0, axis_index_groups=rings
    )
    near = jnp.stack([own[0][0], own[1][0], own[0][1], own[1][1]])
    far = trade(after(near, w_rows), 2)
    tiles, cosine, sine = lax.optimization_barrier((tiles, cosine, sine))
    o_tiles, *kept = run_forward(inverse, place, tiles, id_row)
    o_own = lax.all_to_all(o_tiles, "ctx", 0, 0, axis_index_groups=SAME_CORE)
    blocks = [near, trade(near, 1), far, trade(far, 1)]
    o_other = trade(after(o_own, blocks), 1)
    eights = [list(range(8)), list(range(8, 16))]
    wide = lax.all_gather(after(own[2], o_tiles), "ctx", axis=0, axis_index_groups=eights)

    keep, send, h2, dgu, a, ob, middle, wout = run_feed(
        place, o_own, o_other, blocks, gain_two, units
    )
    pair = run_pair(keep, trade(send, 1))
    parts = [pair[0]] + [trade(pair[k], 2 * k) for k in (1, 2, 3)]

    ff, z_keep, z_send = run_weights(place, after(h2, pair), dgu, a, blocks, units)
    dy1, *columns, do = run_middle(place, after(parts, ff), middle, cotangent[0], gain_two, wout)
    ff = lax.psum_scatter(
        ff, "fsdp", scatter_dimension=0, tiled=True, axis_index_groups=rings
    )
    z = run_pair(z_keep, trade(after(z_send, do), 1))
    z = [z[0]] + [trade(z[k], 2 * k) for k in (1, 2, 3)]
    do = lax.all_to_all(do, "ctx", 0, 0)
    columns = jnp.stack([columns[0], trade(columns[1], 2)], 1)
    columns = [columns[0], trade(columns[1], 1)]
    *d_parts, small = run_backward(
        inverse, place, do, blocks, wide, gain_one, kept, cosine, sine, id_row, ob, columns
    )
    small, ff, z = lax.optimization_barrier((small, ff, z))
    small = lax.all_to_all(small, "fsdp", 0, 0)
    far = shard // 4 == 1
    away = jnp.where(far, ff[:144], ff[144:])
    ff = jnp.where(far, ff[144:], ff[:144])

    def half(value, flip):
        return jnp.where((group == 1) ^ flip, value[:, 384:], value[:, :384])

    def across(value, flip, shift):
        pairs = [(8 * c + f, 8 * (c ^ shift) + (f ^ flip)) for f in range(8) for c in range(16)]
        return lax.ppermute(value, ("ctx", "fsdp"), pairs)

    halves = half(ff, False), half(ff, True), half(away, False), half(away, True)
    parts = [
        halves[0], across(halves[1], 0, 8), across(halves[2], 4, 0), across(halves[3], 4, 8)
    ]
    ff = sum(part.astype(F32) for part in parts).astype(BF16)
    ff = lax.all_gather(ff, "ctx", axis=0)

    folded = run_fold(small)
    for k in range(1, 4):
        d_parts[k] = lax.ppermute(
            after(d_parts[k], folded), "ctx", [(i, (i + 4 * k) % 16) for i in range(16)]
        )
    small = lax.all_to_all(folded, "ctx", 0, 0, axis_index_groups=SAME_CORE)
    total_query, total_key, total_value, total_out, total_gain_one = run_finish_heads(
        place, small, trade(small, 1), w_query, w_key, w_value, gain_attn
    )

    keep, send = run_inputs(place, d_parts, w_rows)
    summed = keep.astype(F32) + trade(send, 1).astype(F32)
    low = rank // 2 == 0
    keep = jnp.where(low, summed[0], summed[1])
    send = jnp.where(low, summed[1], summed[0]).astype(BF16)
    dh1 = keep + trade(send, 2).astype(F32)
    normal_one, inverse_one = normalise(tokens[0].astype(F32))
    grad_stream = dy1 + norm_back(dh1, normal_one, inverse_one, gain_one)
    result = middle + sum(part.astype(F32) for part in z)
    grad_stream, result = grad_stream.astype(BF16), result.astype(BF16)
    ff, grad_stream, result, total_query = lax.optimization_barrier(
        (ff, grad_stream, result, total_query)
    )
    total_gate, total_up, total_down, total_gain_two = run_finish_feed(
        ff, w_gate, w_up, gain_mlp
    )

    return (
        result[None],
        grad_stream[None],
        total_query,
        total_key,
        total_value,
        total_out,
        total_gate,
        total_up,
        total_down,
        total_gain_one.reshape(96),
        total_gain_two.reshape(96),
    )


def solution(mesh):
    rows = P("fsdp", "ctx", None)
    weight = P("fsdp", None)
    return jax.shard_map(
        local,
        mesh=mesh,
        in_specs=(rows, P(), weight) + (weight,) * 7 + (P("fsdp"), P("fsdp"), rows),
        out_specs=(rows, rows) + (weight,) * 7 + (P("fsdp"), P("fsdp")),
        check_vma=False,
    )
```

```python
import jax
import jax.numpy as jnp
from jax import lax
from jax.experimental import pallas as pl
from jax.experimental.pallas import tpu as pltpu
from jax.sharding import PartitionSpec as P

EPS = 1e-05
THETA = 10000.0
WIDTH = 768
HEAD = 64
HALF = 32
SEQ = 2048
BLOCK = 64
CHUNK = 256
CHUNKS = SEQ // CHUNK
HALF_SEQ = SEQ // 2
F32 = jnp.float32
BF16 = jnp.bfloat16

QUADS = [[4 * i + j for j in range(4)] for i in range(4)]
COLUMNS = [[j + 4 * i for i in range(4)] for j in range(4)]
SAME_CORE = [[j + 2 * i for i in range(8)] for j in range(2)]
FOUR_CHIPS = [[8 * g + j + 2 * i for i in range(4)] for g in range(2) for j in range(2)]
RING = [(0, 0), (1, 0), (0, 3), (0, 1), (1, 3), (1, 1), (0, 2), (1, 2)]

VMEM = pl.BlockSpec(memory_space=pltpu.VMEM)
SMEM = pl.BlockSpec(memory_space=pltpu.SMEM)
ANY = pl.BlockSpec(memory_space=pl.ANY)
SHAPE = jax.ShapeDtypeStruct


def cost(microseconds):
    return pl.CostEstimate(
        flops=int(microseconds * 1.1e9), bytes_accessed=int(microseconds * 3.6e6), transcendentals=0
    )


def after(value, *others):
    return lax.optimization_barrier((value, others))[0]


def dot(left, right, left_dim=1, right_dim=0):
    return lax.dot_general(
        left, right, (((left_dim,), (right_dim,)), ((), ())), preferred_element_type=F32
    )


def turn(block, cosine, sine, backward):
    first, second = block[:HALF], block[HALF:]
    if backward:
        return jnp.concatenate([first * cosine + second * sine, second * cosine - first * sine], 0)
    return jnp.concatenate([first * cosine - second * sine, second * cosine + first * sine], 0)


def normalise(x):
    scale = lax.rsqrt(jnp.mean(x * x, axis=-1, keepdims=True) + EPS)
    return x * scale, scale


def document_starts(id_row):
    start = jnp.zeros_like(id_row)
    for number in (1, 2, 3):
        before = jnp.sum((id_row < number).astype(F32), axis=1, keepdims=True).astype(jnp.int32)
        start = jnp.where(id_row >= number, before, start)
    return start


def masked(scores, half, part, starts, other):
    keys = scores.shape[0]
    base = keys - CHUNK
    row = lax.broadcasted_iota(jnp.int32, (CHUNK, CHUNK), 0)
    column = lax.broadcasted_iota(jnp.int32, (CHUNK, CHUNK), 1)
    if half == 1:
        place = lax.broadcasted_iota(jnp.int32, scores.shape, 0)
        inside = place >= starts[:, part * CHUNK : (part + 1) * CHUNK]
        scores = jnp.where(inside, scores, other)
    last = jnp.where(row <= column, scores[base:], other)
    return last if base == 0 else jnp.concatenate([scores[:base], last], 0)


def swap_lanes(tile):
    return jnp.concatenate([tile[:, BLOCK:], tile[:, :BLOCK]], 1)


def sort_tiles(inverse, in_ref, out_ref):
    for b in range(16):
        flat = inverse[b]
        upper = 15 - b
        tile = in_ref[flat // 2].astype(F32)
        tile = jnp.where(flat % 2 == 0, tile, swap_lanes(tile)).astype(BF16)
        out_ref[b // 4, :, (b % 4) * BLOCK : (b % 4 + 1) * BLOCK] = tile[:, :BLOCK]
        out_ref[4 + upper // 4, :, (upper % 4) * BLOCK : (upper % 4 + 1) * BLOCK] = tile[:, BLOCK:]


def pack_heads_kernel(q_ref, k_ref, v_ref, one_ref, two_ref, out_ref):
    rank = lax.axis_index("ctx") & 3
    column = lax.broadcasted_iota(jnp.int32, (96, 64), 1)
    one = jnp.broadcast_to(one_ref[...].astype(F32), (128, 96)).T[:, :64]
    two = jnp.broadcast_to(two_ref[...].astype(F32), (128, 96)).T[:, :64]
    gains = jnp.where(column == 0, one, jnp.where(column == 1, two, 0.0)).astype(BF16)
    for r in range(4):

        @pl.when(rank == r)
        def _():
            lanes = slice(192 * r, 192 * (r + 1))
            unit = jnp.concatenate([q_ref[:, lanes], k_ref[:, lanes], v_ref[:, lanes], gains], 1)
            for f in range(8):
                out_ref[f] = unit


def run_pack_heads(query, key, value, gain_one, gain_two):
    return pl.pallas_call(
        pack_heads_kernel,
        out_shape=SHAPE((8, 96, 640), BF16),
        in_specs=[VMEM] * 5,
        out_specs=VMEM,
        compiler_params=pltpu.CompilerParams(vmem_limit_bytes=60 << 20),
        cost_estimate=cost(2),
        name="pack_heads",
    )(query, key, value, gain_one.reshape(1, 96), gain_two.reshape(1, 96))


def pack_units_kernel(gate_ref, up_ref, down_ref, wout_ref, _, out_ref, both_ref):
    index = lax.axis_index("ctx")
    member = index & 7
    for m in range(8):

        @pl.when(member == m)
        def _():
            parts = [
                ref[:, 384 * f + 48 * m : 384 * f + 48 * (m + 1)]
                for ref in (gate_ref, up_ref)
                for f in range(8)
            ]
            out_ref[:96] = jnp.concatenate(parts, 1)

    out_ref[96:144] = down_ref[pl.ds(pl.multiple_of(member * 48, 16), 48), :]
    out_ref[144:] = wout_ref[...]
    both_ref[0] = out_ref[...]


def run_pack_units(gate, up, down, wout, after):
    return pl.pallas_call(
        pack_units_kernel,
        out_shape=(SHAPE((240, WIDTH), BF16), SHAPE((2, 240, WIDTH), BF16)),
        in_specs=[VMEM] * 4 + [ANY],
        out_specs=(VMEM, VMEM),
        compiler_params=pltpu.CompilerParams(vmem_limit_bytes=60 << 20),
        cost_estimate=cost(2.4),
        name="pack_units",
    )(gate, up, down, wout, after)


def project_kernel(
    place, w_ref, x0_ref, x1_ref, x2_ref, x3_ref, cos_ref, sin_ref,
    out0_ref, out1_ref, out2_ref, out3_ref, wt_ref, out_ref,
):
    wt_ref[...] = w_ref[...].T
    gain = wt_ref[576:592].astype(F32)[:1]
    for d, block in enumerate((x0_ref, x1_ref, x2_ref, x3_ref)):
        c = place[11] ^ d
        normal, _ = normalise(block[...].astype(F32))
        h = (normal * gain).astype(BF16)
        qkv = dot(wt_ref[:576], h, 1, 1)
        cosine, sine = cos_ref[c], sin_ref[c]
        for j in range(3):
            at = HEAD * j
            q = (turn(qkv[at : at + HEAD], cosine, sine, False).astype(BF16) * 0.125).astype(BF16)
            k = turn(qkv[192 + at : 192 + at + HEAD], cosine, sine, False).astype(BF16)
            v = qkv[384 + at : 384 + at + HEAD].astype(BF16)
            for target in (2, 3) if j == 2 else (j,):
                away = (target - place[12]) & 3
                out_ref[away, c, :HEAD] = q
                out_ref[away, c, HEAD : 2 * HEAD] = k
                out_ref[away, c, 2 * HEAD :] = v
    for k, ref in enumerate((out0_ref, out1_ref, out2_ref, out3_ref)):
        ref[...] = out_ref[k]


def run_project(place, w, blocks, cosine, sine):
    return pl.pallas_call(
        project_kernel,
        out_shape=(SHAPE((4, 3 * HEAD, 128), BF16),) * 4 + (SHAPE((640, WIDTH), BF16),),
        in_specs=[SMEM] + [VMEM] * 7,
        out_specs=(VMEM,) * 5,
        scratch_shapes=[pltpu.VMEM((4, 4, 3 * HEAD, 128), BF16)],
        compiler_params=pltpu.CompilerParams(vmem_limit_bytes=14 << 20),
        cost_estimate=cost(40),
        name="project",
    )(place, w, *blocks, cosine, sine)


def forward_kernel(
    inverse, place, in0_ref, in1_ref, in2_ref, in3_ref, id_row,
    out_ref, q_ref, k_ref, v_ref, krow_ref, o_ref, lse_ref, all_ref, orow_ref, in_ref,
):
    for k, ref in enumerate((in0_ref, in1_ref, in2_ref, in3_ref)):
        in_ref[pl.ds(4 * ((place[12] - k) & 3), 4)] = ref[...]
    sort_tiles(inverse, in_ref, all_ref)
    starts = document_starts(id_row[...])
    for at in range(CHUNKS):
        q_ref[at] = all_ref[at, :HEAD]
        k_ref[at] = all_ref[at, HEAD : 2 * HEAD]
        v_ref[at] = all_ref[at, 2 * HEAD :]
        krow_ref[at] = all_ref[at, HEAD : 2 * HEAD].T
    for half in range(2):
        for part in range(4):
            at = 4 * half + part
            keys = (part + 1) * CHUNK
            k = krow_ref[4 * half : 4 * half + part + 1].reshape(keys, HEAD)
            s = dot(k, q_ref[at])
            s = masked(s, half, part, starts, -1e30)
            top = jnp.max(s, axis=0, keepdims=True)
            p = jnp.exp(s - top)
            total = jnp.sum(p, axis=0, keepdims=True)
            low = p.astype(BF16)
            o = dot(v_ref[4 * half], low[:CHUNK])
            for j in range(1, part + 1):
                o += dot(v_ref[4 * half + j], low[j * CHUNK : (j + 1) * CHUNK])
            o = o / total
            o_ref[at] = o
            orow_ref[at] = o.T
            lse_ref[at] = top + jnp.log(total)
    for b in range(16):
        flat = inverse[b]
        upper = 15 - b
        lo = orow_ref[b // 4, (b % 4) * BLOCK : (b % 4 + 1) * BLOCK, :]
        up = orow_ref[4 + upper // 4, (upper % 4) * BLOCK : (upper % 4 + 1) * BLOCK, :]
        tile = jnp.concatenate([lo, up], 1)
        turned = jnp.concatenate([up, lo], 1)
        tile = jnp.where(flat % 2 == 0, tile, turned).astype(BF16)
        group = flat // 16
        for chip in range(4):
            out_ref[4 * group + chip, (flat // 2) % 8] = tile


def run_forward(inverse, place, tiles, id_row):
    return pl.pallas_call(
        forward_kernel,
        out_shape=(
            SHAPE((8, 8, BLOCK, 128), BF16),
            SHAPE((CHUNKS, HEAD, CHUNK), BF16),
            SHAPE((CHUNKS, HEAD, CHUNK), BF16),
            SHAPE((CHUNKS, HEAD, CHUNK), BF16),
            SHAPE((CHUNKS, CHUNK, HEAD), BF16),
            SHAPE((CHUNKS, HEAD, CHUNK), F32),
            SHAPE((CHUNKS, 1, CHUNK), F32),
        ),
        in_specs=[SMEM] * 2 + [VMEM] * 5,
        out_specs=(VMEM,) * 7,
        scratch_shapes=[
            pltpu.VMEM((CHUNKS, 3 * HEAD, CHUNK), BF16),
            pltpu.VMEM((CHUNKS, CHUNK, HEAD), F32),
            pltpu.VMEM((16, 3 * HEAD, 128), BF16),
        ],
        compiler_params=pltpu.CompilerParams(vmem_limit_bytes=60 << 20),
        cost_estimate=cost(40),
        name="attention_forward",
    )(inverse, place, *tiles, id_row)


def backward_kernel(
    inverse, place, do_ref, b0_ref, b1_ref, b2_ref, b3_ref, wide_ref, gain_ref,
    q_ref, k_ref, v_ref, krow_ref, o_ref, lse_ref, cos_ref, sin_ref,
    id_row, ob_ref, near_ref, far_ref,
    out0_ref, out1_ref, out2_ref, out3_ref, grad_ref,
    d_ref, dk_ref, dv_ref, dot_ref, vrow_ref, wt_ref, all_ref, xv_ref, obv_ref, xsem,
):
    other = xv_ref.at[pl.ds(8 - 8 * place[10], 8)]
    copies = [
        pltpu.make_async_copy(ob_ref, obv_ref, xsem.at[8]),
        pltpu.make_async_copy(wide_ref, other, xsem.at[9]),
    ]
    for k, ref in enumerate((b0_ref, b1_ref, b2_ref, b3_ref)):
        for j in range(2):
            at = place[14] ^ (k + 4 * j)
            copies.append(pltpu.make_async_copy(ref.at[j], xv_ref.at[at], xsem.at[2 * k + j]))
    for copy in copies:
        copy.start()
    sort_tiles(inverse, do_ref, dot_ref)
    starts = document_starts(id_row[...])
    for half in range(2):
        for part in range(4):
            at = 4 * half + part
            vrow_ref[at] = v_ref[at].T
            keys = (part + 1) * CHUNK
            first = 4 * half
            k = krow_ref[first : first + part + 1].reshape(keys, HEAD)
            v = vrow_ref[first : first + part + 1].reshape(keys, HEAD)
            q = q_ref[at]
            do = dot_ref[at]
            delta = jnp.sum(do.astype(F32) * o_ref[at], axis=0, keepdims=True)
            s = dot(k, q) - lse_ref[at]
            p = jnp.exp(masked(s, half, part, starts, -1e30))
            ds = (p * (dot(v, do) - delta)).astype(BF16)
            dv = dot(p.astype(BF16), do.T).reshape(part + 1, CHUNK, HEAD)
            dk = dot(ds, q.T).reshape(part + 1, CHUNK, HEAD)
            if part:
                dv_ref[first : first + part] += dv[:part]
                dk_ref[first : first + part] += dk[:part]
            dv_ref[at] = dv[part]
            dk_ref[at] = dk[part]
            dq = dot(k_ref[first], ds[:CHUNK])
            for j in range(1, part + 1):
                dq += dot(k_ref[first + j], ds[j * CHUNK : (j + 1) * CHUNK])
            d_ref[at, :HEAD] = turn(dq * 0.125, cos_ref[at], sin_ref[at], True).astype(BF16)
    for copy in copies:
        copy.wait()
    for at in range(8):
        dk = turn(dk_ref[at].T, cos_ref[at], sin_ref[at], True)
        d_ref[at, HEAD : 2 * HEAD] = dk.astype(BF16)
        d_ref[at, 2 * HEAD :] = dv_ref[at].T.astype(BF16)
        rows = []
        for j in range(4):
            flat = inverse[4 * at + j]
            start = pl.multiple_of((flat & 1) * BLOCK, BLOCK)
            rows.append(xv_ref[flat // 2, pl.ds(start, BLOCK), :])
        normal, _ = normalise(jnp.concatenate(rows, 0).astype(F32))
        part = dot(d_ref[at], (normal * gain_ref[...]).astype(BF16))
        wt_ref[:192] = part if at == 0 else wt_ref[:192] + part
    for d in range(4):
        start = pl.multiple_of((d // 2) * 256 + ((place[9] ^ d) & 1) * 128, 128)
        columns = (near_ref if d % 2 == 0 else far_ref)[d // 2]
        part = dot(columns.T, obv_ref[pl.ds(start, 128), :])
        wt_ref[192:] = part if d == 0 else wt_ref[192:] + part
    grad_ref[...] = wt_ref[...].T.astype(BF16).reshape(8, 96, 384)
    for b in range(16):
        flat = inverse[b]
        upper = 15 - b
        lo = d_ref[b // 4, :, (b % 4) * BLOCK : (b % 4 + 1) * BLOCK].astype(F32)
        up = d_ref[4 + upper // 4, :, (upper % 4) * BLOCK : (upper % 4 + 1) * BLOCK].astype(F32)
        tile = jnp.concatenate([lo, up], 1)
        turned = jnp.concatenate([up, lo], 1)
        away = (flat // 8 - place[12]) & 3
        all_ref[away, (flat // 2) % 4] = jnp.where(flat % 2 == 0, tile, turned).astype(BF16)
    for k, ref in enumerate((out0_ref, out1_ref, out2_ref, out3_ref)):
        ref[...] = all_ref[k]


def run_backward(
    inverse, place, do, blocks, wide, gain, kept, cosine, sine, id_row, ob, columns
):
    return pl.pallas_call(
        backward_kernel,
        out_shape=(
            *(SHAPE((4, 3 * HEAD, 2 * BLOCK), BF16),) * 4,
            SHAPE((8, 96, 384), BF16),
        ),
        in_specs=[SMEM] * 2 + [VMEM] + [ANY] * 5 + [VMEM] * 10 + [ANY] + [VMEM] * 2,
        out_specs=(VMEM,) * 5,
        scratch_shapes=[
            pltpu.VMEM((CHUNKS, 3 * HEAD, CHUNK), BF16),
            pltpu.VMEM((CHUNKS, CHUNK, HEAD), F32),
            pltpu.VMEM((CHUNKS, CHUNK, HEAD), F32),
            pltpu.VMEM((CHUNKS, HEAD, CHUNK), BF16),
            pltpu.VMEM((CHUNKS, CHUNK, HEAD), BF16),
            pltpu.VMEM((384, WIDTH), F32),
            pltpu.VMEM((4, 4, 3 * HEAD, 2 * BLOCK), BF16),
            pltpu.VMEM((16, 128, WIDTH), BF16),
            pltpu.VMEM((2 * CHUNK, WIDTH), BF16),
            pltpu.SemaphoreType.DMA((10,)),
        ],
        compiler_params=pltpu.CompilerParams(vmem_limit_bytes=60 << 20),
        cost_estimate=cost(22.0),
        name="attention_backward",
    )(inverse, place, do, *blocks, wide, gain, *kept, cosine, sine, id_row, ob, *columns)


def pick(core, same, other):
    first = jnp.where(core == 0, same, other)
    return jnp.concatenate([first, jnp.where(core == 0, other, same)], 0)


def assemble(place, units_ref, sems, gu_ref=None, down_ref=None, wout_ref=None):
    copies = []
    parts = ((wout_ref, 144, 96), (gu_ref, 0, 96), (down_ref, 96, 48))
    for target, first, size in parts:
        if target is not None:
            for k in range(8):
                start = ((place[13] ^ (k % 2)) * 4 + k // 2) * size
                rows = target.at[pl.ds(pl.multiple_of(start, 16), size)]
                source = units_ref.at[k // 2, k % 2, first : first + size]
                copies.append(pltpu.make_async_copy(source, rows, sems.at[len(copies)]))
    for copy in copies:
        copy.start()

    def wait(first, last):
        for copy in copies[first:last]:
            copy.wait()

    return wait


def feed_kernel(
    place, own_ref, other_ref, n0_ref, n1_ref, f0_ref, f1_ref, gain_ref, units_ref,
    keep_ref, send_ref, h_ref, d_ref, a_ref, quad_ref, y_ref, wout_ref,
    own_v, other_v, x_v, z_v, gu_v, down_v, wout_v, ob_v, mid_v, h_v, d_v, a_v, keep_v, send_v, y_v,
    sems, unit_sems,
):
    core, member = place[8], place[9]
    started = []

    def copy(source, target):
        started.append(pltpu.make_async_copy(source, target, sems.at[len(started)]))
        started[-1].start()
        return started[-1]

    tiles_in = [copy(own_ref.at[:6], own_v), copy(other_ref.at[:6], other_v)]
    arrays = (n0_ref, n1_ref, f0_ref, f1_ref)
    x_in = [copy(ref.at[:2], x_v.at[k]) for k, ref in enumerate(arrays)]
    units_in = assemble(place, units_ref, unit_sems, gu_v, down_v, wout_v)
    z_in = [copy(ref.at[2:], z_v.at[k]) for k, ref in enumerate(arrays)]

    def rows(i):
        return slice(CHUNK * i, CHUNK * (i + 1))

    def block(ref, i):
        return pick(core, ref[2 * (i % 2), i // 2], ref[2 * (i % 2) + 1, i // 2])

    for part in tiles_in:
        part.wait()
    for i in range(4):
        at = (member // 2) ^ i
        for c in range(2):
            base = CHUNK * i + 128 * c
            for z in range(2):
                tiles = []
                for k in range(2):
                    for x in range(3):
                        mine, theirs = own_v[2 * x + z, 2 * at + c], other_v[2 * x + z, 2 * at + c]
                        tiles.append(jnp.where(core == k, mine, theirs))
                for pair in range(3):
                    left, right = tiles[2 * pair], tiles[2 * pair + 1]
                    lanes = slice(384 * z + 128 * pair, 384 * z + 128 * (pair + 1))
                    ob_v[base : base + BLOCK, lanes] = jnp.concatenate(
                        [left[:, :BLOCK], right[:, :BLOCK]], 1
                    )
                    ob_v[base + BLOCK : base + 128, lanes] = jnp.concatenate(
                        [left[:, BLOCK:], right[:, BLOCK:]], 1
                    )
    out = [copy(ob_v.at[: 2 * CHUNK], quad_ref)]
    for part in x_in:
        part.wait()
    units_in(0, 8)
    out.append(copy(wout_v, wout_ref))
    for i in range(4):
        middle = block(x_v, i).astype(F32) + dot(ob_v[rows(i)], wout_v[...])
        mid_v[rows(i)] = middle
        normal, _ = normalise(middle)
        h_v[rows(i)] = (normal * gain_ref[...]).astype(BF16)
        out.append(copy(h_v.at[rows(i)], h_ref.at[rows(i)]))
    y_v[...] = mid_v[pl.ds(pl.multiple_of(core * 128, 128), 128), :]
    out.append(copy(y_v, y_ref))
    for part in z_in:
        part.wait()
    units_in(8, 24)
    for i in range(4):
        gu = dot(h_v[rows(i)], gu_v[...])
        g, u = gu[:, :384], gu[:, 384:]
        da = dot(block(z_v, i), down_v[...], 1, 1)
        sigma = jax.nn.sigmoid(g)
        swish = g * sigma
        a_v[rows(i)] = (swish * u).astype(BF16)
        d_v[rows(i), :384] = (da * u * (sigma + swish * (1.0 - sigma))).astype(BF16)
        d_v[rows(i), 384:] = (da * swish).astype(BF16)
        out.append(copy(a_v.at[rows(i)], a_ref.at[rows(i)]))
        out.append(copy(d_v.at[rows(i)], d_ref.at[rows(i)]))
    for i in range(4):
        mid_v[rows(i)] = dot(d_v[rows(i)], gu_v[...], 1, 1)
        keep = pl.multiple_of(CHUNK * i + core * 128, 128)
        send = pl.multiple_of(CHUNK * i + 128 - core * 128, 128)
        keep_v[i] = mid_v[pl.ds(keep, 128), :].astype(BF16)
        send_v[i] = mid_v[pl.ds(send, 128), :].astype(BF16)
        out.append(copy(send_v.at[i], send_ref.at[i]))
        out.append(copy(keep_v.at[i], keep_ref.at[i]))
    for part in out:
        part.wait()


def run_feed(place, own, other, blocks, gain, units):
    rows = 4 * CHUNK
    scratch = [
        ((6, 8, BLOCK, 128), BF16),
        ((6, 8, BLOCK, 128), BF16),
        ((4, 2, 128, WIDTH), BF16),
        ((4, 2, 128, WIDTH), BF16),
        ((WIDTH, WIDTH), BF16),
        ((WIDTH // 2, WIDTH), BF16),
        ((WIDTH, WIDTH), BF16),
        ((rows, WIDTH), BF16),
        ((rows, WIDTH), F32),
        ((rows, WIDTH), BF16),
        ((rows, WIDTH), BF16),
        ((rows, WIDTH // 2), BF16),
        ((4, 128, WIDTH), BF16),
        ((4, 128, WIDTH), BF16),
        ((128, WIDTH), F32),
    ]
    return pl.pallas_call(
        feed_kernel,
        out_shape=(
            SHAPE((4, 128, WIDTH), BF16),
            SHAPE((4, 128, WIDTH), BF16),
            SHAPE((rows, WIDTH), BF16),
            SHAPE((rows, WIDTH), BF16),
            SHAPE((rows, WIDTH // 2), BF16),
            SHAPE((2 * CHUNK, WIDTH), BF16),
            SHAPE((128, WIDTH), F32),
            SHAPE((WIDTH, WIDTH), BF16),
        ),
        in_specs=[SMEM] + [ANY] * 6 + [VMEM, ANY],
        out_specs=(ANY,) * 8,
        scratch_shapes=[pltpu.VMEM(*shape) for shape in scratch]
        + [pltpu.SemaphoreType.DMA((40,)), pltpu.SemaphoreType.DMA((24,))],
        compiler_params=pltpu.CompilerParams(vmem_limit_bytes=60 << 20),
        cost_estimate=cost(40),
        name="feed",
    )(place, own, other, *blocks, gain, units)


def weights_kernel(
    place, h_ref, d_ref, a_ref, z0_ref, z1_ref, z2_ref, z3_ref, units_ref,
    out_ref, keep_ref, send_ref,
    h_v, d_v, a_v, dz_v, gu_v, gd_v, z_v, down_v, out_v, keep_v, send_v, sems, unit_sems,
):
    core = place[8]
    started = []

    def copy(source, target):
        started.append(pltpu.make_async_copy(source, target, sems.at[len(started)]))
        started[-1].start()
        return started[-1]

    def rows(i):
        return slice(2 * CHUNK * i, 2 * CHUNK * (i + 1))

    parts = []
    for i in range(2):
        parts.append([copy(h_ref.at[rows(i)], h_v.at[rows(i)]), copy(d_ref.at[rows(i)], d_v.at[rows(i)])])
        if i == 0:
            dz_in = [
                copy(ref.at[2:], dz_v.at[k]) for k, ref in enumerate((z0_ref, z1_ref, z2_ref, z3_ref))
            ]
            units_in = assemble(place, units_ref, unit_sems, down_ref=down_v)
        parts[i].append(copy(a_ref.at[rows(i)], a_v.at[rows(i)]))
    out = []
    for i in range(2):
        parts[i][0].wait()
        parts[i][1].wait()
        gu = dot(h_v[rows(i)], d_v[rows(i)], 0, 0)
        gu_v[...] = gu if i == 0 else gu_v[...] + gu
    for part in dz_in + [parts[0][2], parts[1][2]]:
        part.wait()
    units_in(0, 8)
    for i in range(2):
        dz = [pick(core, dz_v[0, i], dz_v[1, i]), pick(core, dz_v[2, i], dz_v[3, i])]
        gd = dot(a_v[rows(i)], jnp.concatenate(dz, 0), 0, 0)
        gd_v[...] = gd if i == 0 else gd_v[...] + gd
    for f in range(8):
        base = (2 * (f % 4) + f // 4) * 144
        out_v[base : base + 96] = gu_v[96 * f : 96 * (f + 1)].astype(BF16)
        out_v[base + 96 : base + 144] = gd_v[48 * f : 48 * (f + 1)].astype(BF16)
    out.append(copy(out_v, out_ref))
    for i in range(2):
        z_v[...] = dot(a_v[rows(i)], down_v[...])
        for j in range(2):
            keep = pl.multiple_of(256 * j + core * 128, 128)
            send = pl.multiple_of(256 * j + 128 - core * 128, 128)
            keep_v[2 * i + j] = z_v[pl.ds(keep, 128), :].astype(BF16)
            send_v[2 * i + j] = z_v[pl.ds(send, 128), :].astype(BF16)
    out += [copy(keep_v, keep_ref), copy(send_v, send_ref)]
    for part in out:
        part.wait()


def run_weights(place, h, d, a, blocks, units):
    rows = 4 * CHUNK
    scratch = [
        ((rows, WIDTH), BF16),
        ((rows, WIDTH), BF16),
        ((rows, WIDTH // 2), BF16),
        ((4, 2, 128, WIDTH), BF16),
        ((WIDTH, WIDTH), F32),
        ((WIDTH // 2, WIDTH), F32),
        ((2 * CHUNK, WIDTH), F32),
        ((WIDTH // 2, WIDTH), BF16),
        ((8 * 144, WIDTH), BF16),
        ((4, 128, WIDTH), BF16),
        ((4, 128, WIDTH), BF16),
    ]
    return pl.pallas_call(
        weights_kernel,
        out_shape=(SHAPE((8 * 144, WIDTH), BF16),) + (SHAPE((4, 128, WIDTH), BF16),) * 2,
        in_specs=[SMEM] + [ANY] * 8,
        out_specs=(ANY,) * 3,
        scratch_shapes=[pltpu.VMEM(*shape) for shape in scratch]
        + [pltpu.SemaphoreType.DMA((16,)), pltpu.SemaphoreType.DMA((8,))],
        compiler_params=pltpu.CompilerParams(vmem_limit_bytes=60 << 20),
        cost_estimate=cost(9),
        name="weights",
    )(place, h, d, a, *blocks, units)


def middle_kernel(
    place, p0_ref, p1_ref, p2_ref, p3_ref, y_ref, cot_ref, gain_ref, wout_ref,
    dy_ref, keep_ref, send_ref, do_ref, columns_ref,
):
    dh = sum(ref[...].astype(F32) for ref in (p0_ref, p1_ref, p2_ref, p3_ref))
    normal, scale = normalise(y_ref[...])
    dy = cot_ref[...].astype(F32) + norm_back(dh, normal, scale, gain_ref[...])
    dy_ref[...] = dy
    low = dy.astype(BF16)
    do = dot(wout_ref[...], low, 1, 1).astype(BF16)
    for t in range(4):
        for x in range(4):
            h = 3 * t + min(x, 2)
            do_ref[4 * x + t] = do[HEAD * h : HEAD * (h + 1)]
    for r in range(4):
        columns_ref[place[11] ^ r] = low[:, 192 * r : 192 * (r + 1)]
    keep_ref[...] = columns_ref[:2]
    send_ref[...] = columns_ref[2:]


def run_middle(place, parts, y, cotangent, gain, wout):
    return pl.pallas_call(
        middle_kernel,
        out_shape=(
            SHAPE((128, WIDTH), F32),
            *(SHAPE((2, 128, 192), BF16),) * 2,
            SHAPE((16, HEAD, 128), BF16),
        ),
        in_specs=[SMEM] + [VMEM] * 8,
        out_specs=(VMEM,) * 4,
        scratch_shapes=[
            pltpu.VMEM((4, 128, 192), BF16),
        ],
        compiler_params=pltpu.CompilerParams(vmem_limit_bytes=10 << 20),
        cost_estimate=cost(12.0),
        name="middle",
    )(place, *parts, y, cotangent, gain, wout)


def inputs_kernel(place, d0_ref, d1_ref, d2_ref, d3_ref, w_ref, keep_ref, send_ref, sum_ref):
    core, column = place[8], place[12]
    for c in range(4):
        for k, ref in enumerate((d0_ref, d1_ref, d2_ref, d3_ref)):
            x = (column - k) & 3
            at = jnp.minimum(x, 2) * HEAD
            w = jnp.concatenate(
                [w_ref[pl.ds(pl.multiple_of(base + at, HEAD), HEAD), :] for base in (0, 192, 384)],
                0,
            )
            part = jnp.where(x < 3, dot(ref[c], w, 0, 0), 0.0)
            sum_ref[c] = part if k == 0 else sum_ref[c] + part
    for z in range(2):
        keep_ref[z] = sum_ref[2 * z + core].astype(BF16)
        send_ref[z] = sum_ref[2 * z + 1 - core].astype(BF16)


def run_inputs(place, parts, w_rows):
    return pl.pallas_call(
        inputs_kernel,
        out_shape=(SHAPE((2, 128, WIDTH), BF16),) * 2,
        in_specs=[SMEM] + [VMEM] * 5,
        out_specs=(VMEM,) * 2,
        scratch_shapes=[pltpu.VMEM((4, 128, WIDTH), F32)],
        compiler_params=pltpu.CompilerParams(vmem_limit_bytes=12 << 20),
        cost_estimate=cost(3),
        name="inputs",
    )(place, *parts, w_rows)


def finish_feed_kernel(
    all_ref, gate_ref, up_ref, gain_ref, g_ref, u_ref, d_ref, n_ref
):
    total = jnp.zeros((96, 1), F32)
    for half, (w_ref, out_ref) in enumerate(((gate_ref, g_ref), (up_ref, u_ref))):
        tiles = []
        for m in range(8):
            part = all_ref[8 * half + m]
            d_ref[48 * m : 48 * (m + 1), 384 * half : 384 * (half + 1)] = part[96:].astype(F32)
            tiles.append(part[:96])
        for f in range(8):
            block = jnp.concatenate([t[:, 48 * f : 48 * (f + 1)] for t in tiles], 1).astype(F32)
            lanes = slice(384 * f, 384 * (f + 1))
            out_ref[:, lanes] = block
            total += jnp.sum(w_ref[:, lanes].astype(F32) * block, axis=1, keepdims=True)
    n_ref[...] = jnp.broadcast_to(total, (96, 128)).T[:1] / gain_ref[...].astype(F32)


def run_finish_feed(whole, gate, up, gain):
    return pl.pallas_call(
        finish_feed_kernel,
        out_shape=(
            SHAPE((96, 3072), F32),
            SHAPE((96, 3072), F32),
            SHAPE((384, WIDTH), F32),
            SHAPE((1, 96), F32),
        ),
        in_specs=[VMEM] * 4,
        out_specs=(VMEM,) * 4,
        compiler_params=pltpu.CompilerParams(vmem_limit_bytes=60 << 20),
        cost_estimate=cost(6),
        name="finish_feed",
    )(whole, gate, up, gain.reshape(1, 96))


def finish_heads_kernel(place, *refs):
    own_ref, other_ref = refs[:2]
    wq_ref, wk_ref, wv_ref, gain_ref, q_ref, k_ref, v_ref, o_ref, n_ref = refs[2:]
    core = place[8]
    tiles = {}
    for x in range(4):
        for z in range(2):
            mine, theirs = own_ref[2 * x + z], other_ref[2 * x + z]
            for k in range(2):
                tiles[x, 2 * z + k] = jnp.where(core == k, mine, theirs).astype(F32)
    total = jnp.zeros((96, 1), F32)
    for j, (w_ref, out_ref) in enumerate(((wq_ref, q_ref), (wk_ref, k_ref), (wv_ref, v_ref))):
        lanes = slice(HEAD * j, HEAD * (j + 1))
        whole = jnp.concatenate([tiles[h % 3, h // 3][:, lanes] for h in range(12)], 1)
        out_ref[...] = whole
        total += jnp.sum(w_ref[...].astype(F32) * whole, axis=1, keepdims=True)
    n_ref[...] = jnp.broadcast_to(total, (96, 128)).T[:1] / gain_ref[...].astype(F32)
    o_ref[...] = jnp.concatenate(
        [sum(tiles[x, t][:, 192:] for x in range(4)) for t in range(4)], 1
    )


def run_finish_heads(place, own, other, query, key, value, gain):
    return pl.pallas_call(
        finish_heads_kernel,
        out_shape=(SHAPE((96, WIDTH), F32),) * 4 + (SHAPE((1, 96), F32),),
        in_specs=[SMEM] + [VMEM] * 6,
        out_specs=(VMEM,) * 5,
        compiler_params=pltpu.CompilerParams(vmem_limit_bytes=12 << 20),
        cost_estimate=cost(8),
        name="finish_heads",
    )(place, own, other, query, key, value, gain.reshape(1, 96))


def fold_kernel(in_ref, out_ref):
    total = jnp.sum(in_ref[...].astype(F32), axis=0).astype(BF16)
    for k in range(8):
        out_ref[k] = total


def run_fold(parts):
    return pl.pallas_call(
        fold_kernel,
        out_shape=SHAPE(parts.shape, BF16),
        in_specs=[VMEM],
        out_specs=VMEM,
        compiler_params=pltpu.CompilerParams(vmem_limit_bytes=6 << 20),
        cost_estimate=cost(0.3),
        name="fold",
    )(parts)


def trade(value, distance):
    return lax.ppermute(value, "ctx", [(i, i ^ distance) for i in range(16)])


def pair_kernel(keep_ref, got_ref, *outs):
    for k, ref in enumerate(outs):
        ref[...] = (keep_ref[k].astype(F32) + got_ref[k].astype(F32)).astype(BF16)


def run_pair(keep, got):
    return pl.pallas_call(
        pair_kernel,
        out_shape=(SHAPE((128, WIDTH), BF16),) * 4,
        in_specs=[VMEM] * 2,
        out_specs=(VMEM,) * 4,
        compiler_params=pltpu.CompilerParams(vmem_limit_bytes=8 << 20),
        cost_estimate=cost(2),
        name="pair",
    )(keep, got)


def norm_back(grad_normed, normal_rows, inverse, gains):
    scaled = grad_normed * gains
    return inverse * (scaled - normal_rows * jnp.mean(scaled * normal_rows, axis=-1, keepdims=True))


def local(
    tokens, block_table, seq_ids, w_query, w_key, w_value, w_out, w_gate, w_up, w_down,
    gain_attn, gain_mlp, cotangent,
):
    index = lax.axis_index("ctx")
    shard = lax.axis_index("fsdp")
    rank, column = index % 4, index // 4
    core, member, group = index % 2, index % 8, index // 8

    rings = [[0, 1, 2, 3], [4, 5, 6, 7]]

    blocks = block_table.reshape(-1)
    numbers = jnp.arange(32, dtype=jnp.int32)
    inverse = jnp.sum(
        jnp.where(blocks[None, :] == numbers[:, None], numbers[None, :], 0), axis=1
    ).astype(jnp.int32)
    frequency = jnp.power(THETA, -(jnp.arange(HALF, dtype=F32) * 2.0) / HEAD)
    own_blocks = lax.dynamic_slice_in_dim(blocks, 8 * column, 8)
    places = (own_blocks[:, None] * BLOCK + jnp.arange(BLOCK, dtype=jnp.int32)).reshape(4, 1, 128)
    angles = places.astype(F32) * frequency[None, :, None]
    place = jnp.stack(
        [(shard // 4 ^ dz) * 4 + (shard + dy) % 4 for dz, dy in RING]
        + [core, member, group, rank, column, shard // 4, index]
    ).astype(jnp.int32)

    units = run_pack_heads(w_query, w_key, w_value, gain_attn, gain_mlp)
    w_heads = lax.all_to_all(units, "fsdp", 0, 0).reshape(WIDTH, 640)
    x_own = after(tokens[0], units)
    x_blocks = [tokens[0], trade(x_own, 1)]
    unit, both = run_pack_units(w_gate, w_up, w_down, w_out, x_blocks[1])
    x_blocks.append(trade(x_own, 2))
    across = lax.ppermute(after(unit, x_blocks[2]), "fsdp", [(i, i ^ 4) for i in range(8)])
    own = after(jnp.stack([x_own, cotangent[0]]), x_blocks[1])
    own = [own, trade(own, 4), trade(own[0], 8)]
    x_blocks.append(trade(after(x_blocks[2], own, unit), 1))
    w_heads, angles = lax.optimization_barrier((w_heads, (jnp.cos(angles), jnp.sin(angles))))
    *tiles, w_rows = run_project(place, w_heads, x_blocks, *angles)
    gains = w_rows[576:578].astype(F32)
    gain_one, gain_two = gains[:1], gains[1:]

    ids = after(seq_ids[0], w_rows).reshape(32, BLOCK)
    hits = (inverse[16:, None] == numbers[None, :]).astype(jnp.int32)
    ids = jnp.sum(hits[:, :, None] * ids[None], axis=1).reshape(HALF_SEQ)
    id_row = ids.reshape(1, HALF_SEQ)
    angles = after(jnp.arange(SEQ, dtype=F32), w_rows).reshape(CHUNKS, 1, CHUNK)
    angles = angles * frequency[None, :, None]
    cosine, sine = jnp.cos(angles), jnp.sin(angles)

    for k in range(1, 4):
        tiles[k] = lax.ppermute(
            tiles[k], "ctx", [(i, (i + 4 * k) % 16) for i in range(16)]
        )
    units = lax.all_gather(
        both.at[1].set(after(across, w_rows)), "fsdp", axis=0, axis_index_groups=rings
    )
    near = jnp.stack([own[0][0], own[1][0], own[0][1], own[1][1]])
    far = trade(after(near, w_rows), 2)
    tiles, cosine, sine = lax.optimization_barrier((tiles, cosine, sine))
    o_tiles, *kept = run_forward(inverse, place, tiles, id_row)
    o_own = lax.all_to_all(o_tiles, "ctx", 0, 0, axis_index_groups=SAME_CORE)
    blocks = [near, trade(near, 1), far, trade(far, 1)]
    o_other = trade(after(o_own, blocks), 1)
    eights = [list(range(8)), list(range(8, 16))]
    wide = lax.all_gather(after(own[2], o_tiles), "ctx", axis=0, axis_index_groups=eights)

    keep, send, h2, dgu, a, ob, middle, wout = run_feed(
        place, o_own, o_other, blocks, gain_two, units
    )
    pair = run_pair(keep, trade(send, 1))
    parts = [pair[0]] + [trade(pair[k], 2 * k) for k in (1, 2, 3)]

    ff, z_keep, z_send = run_weights(place, after(h2, pair), dgu, a, blocks, units)
    dy1, *columns, do = run_middle(place, after(parts, ff), middle, cotangent[0], gain_two, wout)
    ff = lax.psum_scatter(
        ff, "fsdp", scatter_dimension=0, tiled=True, axis_index_groups=rings
    )
    z = run_pair(z_keep, trade(after(z_send, do), 1))
    z = [z[0]] + [trade(z[k], 2 * k) for k in (1, 2, 3)]
    do = lax.all_to_all(do, "ctx", 0, 0)
    columns = jnp.stack([columns[0], trade(columns[1], 2)], 1)
    columns = [columns[0], trade(columns[1], 1)]
    *d_parts, small = run_backward(
        inverse, place, do, blocks, wide, gain_one, kept, cosine, sine, id_row, ob, columns
    )
    small, ff, z = lax.optimization_barrier((small, ff, z))
    small = lax.all_to_all(small, "fsdp", 0, 0)
    far = shard // 4 == 1
    away = jnp.where(far, ff[:144], ff[144:])
    ff = jnp.where(far, ff[144:], ff[:144])

    def half(value, flip):
        return jnp.where((group == 1) ^ flip, value[:, 384:], value[:, :384])

    def across(value, flip, shift):
        pairs = [(8 * c + f, 8 * (c ^ shift) + (f ^ flip)) for f in range(8) for c in range(16)]
        return lax.ppermute(value, ("ctx", "fsdp"), pairs)

    halves = half(ff, False), half(ff, True), half(away, False), half(away, True)
    parts = [
        halves[0], across(halves[1], 0, 8), across(halves[2], 4, 0), across(halves[3], 4, 8)
    ]
    ff = sum(part.astype(F32) for part in parts).astype(BF16)
    ff = lax.all_gather(ff, "ctx", axis=0)

    folded = run_fold(small)
    for k in range(1, 4):
        d_parts[k] = lax.ppermute(
            after(d_parts[k], folded), "ctx", [(i, (i + 4 * k) % 16) for i in range(16)]
        )
    small = lax.all_to_all(folded, "ctx", 0, 0, axis_index_groups=SAME_CORE)
    total_query, total_key, total_value, total_out, total_gain_one = run_finish_heads(
        place, small, trade(small, 1), w_query, w_key, w_value, gain_attn
    )

    keep, send = run_inputs(place, d_parts, w_rows)
    summed = keep.astype(F32) + trade(send, 1).astype(F32)
    low = rank // 2 == 0
    keep = jnp.where(low, summed[0], summed[1])
    send = jnp.where(low, summed[1], summed[0]).astype(BF16)
    dh1 = keep + trade(send, 2).astype(F32)
    normal_one, inverse_one = normalise(tokens[0].astype(F32))
    grad_stream = dy1 + norm_back(dh1, normal_one, inverse_one, gain_one)
    result = middle + sum(part.astype(F32) for part in z)
    grad_stream, result = grad_stream.astype(BF16), result.astype(BF16)
    ff, grad_stream, result, total_query = lax.optimization_barrier(
        (ff, grad_stream, result, total_query)
    )
    total_gate, total_up, total_down, total_gain_two = run_finish_feed(
        ff, w_gate, w_up, gain_mlp
    )

    return (
        result[None],
        grad_stream[None],
        total_query,
        total_key,
        total_value,
        total_out,
        total_gate,
        total_up,
        total_down,
        total_gain_one.reshape(96),
        total_gain_two.reshape(96),
    )


def solution(mesh):
    rows = P("fsdp", "ctx", None)
    weight = P("fsdp", None)
    return jax.shard_map(
        local,
        mesh=mesh,
        in_specs=(rows, P(), weight) + (weight,) * 7 + (P("fsdp"), P("fsdp"), rows),
        out_specs=(rows, rows) + (weight,) * 7 + (P("fsdp"), P("fsdp")),
        check_vma=False,
    )
```

```python
import jax
import jax.numpy as jnp
from jax import lax
from jax.experimental import pallas as pl
from jax.experimental.pallas import tpu as pltpu
from jax.sharding import PartitionSpec as P

EPS = 1e-05
THETA = 10000.0
WIDTH = 768
HEAD = 64
HALF = 32
SEQ = 2048
BLOCK = 64
CHUNK = 256
CHUNKS = SEQ // CHUNK
HALF_SEQ = SEQ // 2
F32 = jnp.float32
BF16 = jnp.bfloat16

QUADS = [[4 * i + j for j in range(4)] for i in range(4)]
COLUMNS = [[j + 4 * i for i in range(4)] for j in range(4)]
SAME_CORE = [[j + 2 * i for i in range(8)] for j in range(2)]
FOUR_CHIPS = [[8 * g + j + 2 * i for i in range(4)] for g in range(2) for j in range(2)]
RING = [(0, 0), (1, 0), (0, 3), (0, 1), (1, 3), (1, 1), (0, 2), (1, 2)]

VMEM = pl.BlockSpec(memory_space=pltpu.VMEM)
SMEM = pl.BlockSpec(memory_space=pltpu.SMEM)
ANY = pl.BlockSpec(memory_space=pl.ANY)
SHAPE = jax.ShapeDtypeStruct


def cost(microseconds):
    return pl.CostEstimate(
        flops=int(microseconds * 1.1e9), bytes_accessed=int(microseconds * 3.6e6), transcendentals=0
    )


def after(value, *others):
    return lax.optimization_barrier((value, others))[0]


def dot(left, right, left_dim=1, right_dim=0):
    return lax.dot_general(
        left, right, (((left_dim,), (right_dim,)), ((), ())), preferred_element_type=F32
    )


def turn(block, cosine, sine, backward):
    first, second = block[:HALF], block[HALF:]
    if backward:
        return jnp.concatenate([first * cosine + second * sine, second * cosine - first * sine], 0)
    return jnp.concatenate([first * cosine - second * sine, second * cosine + first * sine], 0)


def normalise(x):
    scale = lax.rsqrt(jnp.mean(x * x, axis=-1, keepdims=True) + EPS)
    return x * scale, scale


def document_starts(id_row):
    start = jnp.zeros_like(id_row)
    for number in (1, 2, 3):
        before = jnp.sum((id_row < number).astype(F32), axis=1, keepdims=True).astype(jnp.int32)
        start = jnp.where(id_row >= number, before, start)
    return start


def masked(scores, half, part, starts, other):
    keys = scores.shape[0]
    base = keys - CHUNK
    row = lax.broadcasted_iota(jnp.int32, (CHUNK, CHUNK), 0)
    column = lax.broadcasted_iota(jnp.int32, (CHUNK, CHUNK), 1)
    if half == 1:
        place = lax.broadcasted_iota(jnp.int32, scores.shape, 0)
        inside = place >= starts[:, part * CHUNK : (part + 1) * CHUNK]
        scores = jnp.where(inside, scores, other)
    last = jnp.where(row <= column, scores[base:], other)
    return last if base == 0 else jnp.concatenate([scores[:base], last], 0)


def swap_lanes(tile):
    return jnp.concatenate([tile[:, BLOCK:], tile[:, :BLOCK]], 1)


def sort_tiles(inverse, in_ref, out_ref):
    for b in range(16):
        flat = inverse[b]
        upper = 15 - b
        tile = in_ref[flat // 2].astype(F32)
        tile = jnp.where(flat % 2 == 0, tile, swap_lanes(tile)).astype(BF16)
        out_ref[b // 4, :, (b % 4) * BLOCK : (b % 4 + 1) * BLOCK] = tile[:, :BLOCK]
        out_ref[4 + upper // 4, :, (upper % 4) * BLOCK : (upper % 4 + 1) * BLOCK] = tile[:, BLOCK:]


def pack_heads_kernel(q_ref, k_ref, v_ref, one_ref, two_ref, out_ref):
    rank = lax.axis_index("ctx") & 3
    column = lax.broadcasted_iota(jnp.int32, (96, 64), 1)
    one = jnp.broadcast_to(one_ref[...].astype(F32), (128, 96)).T[:, :64]
    two = jnp.broadcast_to(two_ref[...].astype(F32), (128, 96)).T[:, :64]
    gains = jnp.where(column == 0, one, jnp.where(column == 1, two, 0.0)).astype(BF16)
    for r in range(4):

        @pl.when(rank == r)
        def _():
            lanes = slice(192 * r, 192 * (r + 1))
            unit = jnp.concatenate([q_ref[:, lanes], k_ref[:, lanes], v_ref[:, lanes], gains], 1)
            for f in range(8):
                out_ref[f] = unit


def run_pack_heads(query, key, value, gain_one, gain_two):
    return pl.pallas_call(
        pack_heads_kernel,
        out_shape=SHAPE((8, 96, 640), BF16),
        in_specs=[VMEM] * 5,
        out_specs=VMEM,
        compiler_params=pltpu.CompilerParams(vmem_limit_bytes=60 << 20),
        cost_estimate=cost(2),
        name="pack_heads",
    )(query, key, value, gain_one.reshape(1, 96), gain_two.reshape(1, 96))


def pack_units_kernel(gate_ref, up_ref, down_ref, wout_ref, _, out_ref, both_ref):
    index = lax.axis_index("ctx")
    member = index & 7
    for m in range(8):

        @pl.when(member == m)
        def _():
            parts = [
                ref[:, 384 * f + 48 * m : 384 * f + 48 * (m + 1)]
                for ref in (gate_ref, up_ref)
                for f in range(8)
            ]
            out_ref[:96] = jnp.concatenate(parts, 1)

    out_ref[96:144] = down_ref[pl.ds(pl.multiple_of(member * 48, 16), 48), :]
    out_ref[144:] = wout_ref[...]
    both_ref[0] = out_ref[...]


def run_pack_units(gate, up, down, wout, after):
    return pl.pallas_call(
        pack_units_kernel,
        out_shape=(SHAPE((240, WIDTH), BF16), SHAPE((2, 240, WIDTH), BF16)),
        in_specs=[VMEM] * 4 + [ANY],
        out_specs=(VMEM, VMEM),
        compiler_params=pltpu.CompilerParams(vmem_limit_bytes=60 << 20),
        cost_estimate=cost(2.4),
        name="pack_units",
    )(gate, up, down, wout, after)


def project_kernel(
    place, w_ref, x0_ref, x1_ref, x2_ref, x3_ref, cos_ref, sin_ref,
    out0_ref, out1_ref, out2_ref, out3_ref, wt_ref, out_ref,
):
    wt_ref[...] = w_ref[...].T
    gain = wt_ref[576:592].astype(F32)[:1]
    for d, block in enumerate((x0_ref, x1_ref, x2_ref, x3_ref)):
        c = place[11] ^ d
        normal, _ = normalise(block[...].astype(F32))
        h = (normal * gain).astype(BF16)
        qkv = dot(wt_ref[:576], h, 1, 1)
        cosine, sine = cos_ref[c], sin_ref[c]
        for j in range(3):
            at = HEAD * j
            q = (turn(qkv[at : at + HEAD], cosine, sine, False).astype(BF16) * 0.125).astype(BF16)
            k = turn(qkv[192 + at : 192 + at + HEAD], cosine, sine, False).astype(BF16)
            v = qkv[384 + at : 384 + at + HEAD].astype(BF16)
            for target in (2, 3) if j == 2 else (j,):
                away = (target - place[12]) & 3
                out_ref[away, c, :HEAD] = q
                out_ref[away, c, HEAD : 2 * HEAD] = k
                out_ref[away, c, 2 * HEAD :] = v
    for k, ref in enumerate((out0_ref, out1_ref, out2_ref, out3_ref)):
        ref[...] = out_ref[k]


def run_project(place, w, blocks, cosine, sine):
    return pl.pallas_call(
        project_kernel,
        out_shape=(SHAPE((4, 3 * HEAD, 128), BF16),) * 4 + (SHAPE((640, WIDTH), BF16),),
        in_specs=[SMEM] + [VMEM] * 7,
        out_specs=(VMEM,) * 5,
        scratch_shapes=[pltpu.VMEM((4, 4, 3 * HEAD, 128), BF16)],
        compiler_params=pltpu.CompilerParams(vmem_limit_bytes=14 << 20),
        cost_estimate=cost(40),
        name="project",
    )(place, w, *blocks, cosine, sine)


def forward_kernel(
    inverse, place, in0_ref, in1_ref, in2_ref, in3_ref, id_row,
    out_ref, q_ref, k_ref, v_ref, krow_ref, o_ref, lse_ref, all_ref, orow_ref, in_ref,
):
    for k, ref in enumerate((in0_ref, in1_ref, in2_ref, in3_ref)):
        in_ref[pl.ds(4 * ((place[12] - k) & 3), 4)] = ref[...]
    sort_tiles(inverse, in_ref, all_ref)
    starts = document_starts(id_row[...])
    for at in range(CHUNKS):
        q_ref[at] = all_ref[at, :HEAD]
        k_ref[at] = all_ref[at, HEAD : 2 * HEAD]
        v_ref[at] = all_ref[at, 2 * HEAD :]
        krow_ref[at] = all_ref[at, HEAD : 2 * HEAD].T
    for half in range(2):
        for part in range(4):
            at = 4 * half + part
            keys = (part + 1) * CHUNK
            k = krow_ref[4 * half : 4 * half + part + 1].reshape(keys, HEAD)
            s = dot(k, q_ref[at])
            s = masked(s, half, part, starts, -1e30)
            top = jnp.max(s, axis=0, keepdims=True)
            p = jnp.exp(s - top)
            total = jnp.sum(p, axis=0, keepdims=True)
            low = p.astype(BF16)
            o = dot(v_ref[4 * half], low[:CHUNK])
            for j in range(1, part + 1):
                o += dot(v_ref[4 * half + j], low[j * CHUNK : (j + 1) * CHUNK])
            o = o / total
            o_ref[at] = o
            orow_ref[at] = o.T
            lse_ref[at] = top + jnp.log(total)
    for b in range(16):
        flat = inverse[b]
        upper = 15 - b
        lo = orow_ref[b // 4, (b % 4) * BLOCK : (b % 4 + 1) * BLOCK, :]
        up = orow_ref[4 + upper // 4, (upper % 4) * BLOCK : (upper % 4 + 1) * BLOCK, :]
        tile = jnp.concatenate([lo, up], 1)
        turned = jnp.concatenate([up, lo], 1)
        tile = jnp.where(flat % 2 == 0, tile, turned).astype(BF16)
        group = flat // 16
        for chip in range(4):
            out_ref[4 * group + chip, (flat // 2) % 8] = tile


def run_forward(inverse, place, tiles, id_row):
    return pl.pallas_call(
        forward_kernel,
        out_shape=(
            SHAPE((8, 8, BLOCK, 128), BF16),
            SHAPE((CHUNKS, HEAD, CHUNK), BF16),
            SHAPE((CHUNKS, HEAD, CHUNK), BF16),
            SHAPE((CHUNKS, HEAD, CHUNK), BF16),
            SHAPE((CHUNKS, CHUNK, HEAD), BF16),
            SHAPE((CHUNKS, HEAD, CHUNK), F32),
            SHAPE((CHUNKS, 1, CHUNK), F32),
        ),
        in_specs=[SMEM] * 2 + [VMEM] * 5,
        out_specs=(VMEM,) * 7,
        scratch_shapes=[
            pltpu.VMEM((CHUNKS, 3 * HEAD, CHUNK), BF16),
            pltpu.VMEM((CHUNKS, CHUNK, HEAD), F32),
            pltpu.VMEM((16, 3 * HEAD, 128), BF16),
        ],
        compiler_params=pltpu.CompilerParams(vmem_limit_bytes=60 << 20),
        cost_estimate=cost(40),
        name="attention_forward",
    )(inverse, place, *tiles, id_row)


def backward_kernel(
    inverse, place, do_ref, b0_ref, b1_ref, b2_ref, b3_ref, wide_ref, gain_ref,
    q_ref, k_ref, v_ref, krow_ref, o_ref, lse_ref, cos_ref, sin_ref,
    id_row, ob_ref, near_ref, far_ref,
    out0_ref, out1_ref, out2_ref, out3_ref, grad_ref,
    d_ref, dk_ref, dv_ref, dot_ref, vrow_ref, wt_ref, all_ref, xv_ref, obv_ref, xsem,
):
    other = xv_ref.at[pl.ds(8 - 8 * place[10], 8)]
    copies = [
        pltpu.make_async_copy(ob_ref, obv_ref, xsem.at[8]),
        pltpu.make_async_copy(wide_ref, other, xsem.at[9]),
    ]
    for k, ref in enumerate((b0_ref, b1_ref, b2_ref, b3_ref)):
        for j in range(2):
            at = place[14] ^ (k + 4 * j)
            copies.append(pltpu.make_async_copy(ref.at[j], xv_ref.at[at], xsem.at[2 * k + j]))
    for copy in copies:
        copy.start()
    sort_tiles(inverse, do_ref, dot_ref)
    starts = document_starts(id_row[...])
    for half in range(2):
        for part in range(4):
            at = 4 * half + part
            vrow_ref[at] = v_ref[at].T
            keys = (part + 1) * CHUNK
            first = 4 * half
            k = krow_ref[first : first + part + 1].reshape(keys, HEAD)
            v = vrow_ref[first : first + part + 1].reshape(keys, HEAD)
            q = q_ref[at]
            do = dot_ref[at]
            delta = jnp.sum(do.astype(F32) * o_ref[at], axis=0, keepdims=True)
            s = dot(k, q) - lse_ref[at]
            p = jnp.exp(masked(s, half, part, starts, -1e30))
            ds = (p * (dot(v, do) - delta)).astype(BF16)
            dv = dot(p.astype(BF16), do.T).reshape(part + 1, CHUNK, HEAD)
            dk = dot(ds, q.T).reshape(part + 1, CHUNK, HEAD)
            if part:
                dv_ref[first : first + part] += dv[:part]
                dk_ref[first : first + part] += dk[:part]
            dv_ref[at] = dv[part]
            dk_ref[at] = dk[part]
            dq = dot(k_ref[first], ds[:CHUNK])
            for j in range(1, part + 1):
                dq += dot(k_ref[first + j], ds[j * CHUNK : (j + 1) * CHUNK])
            d_ref[at, :HEAD] = turn(dq * 0.125, cos_ref[at], sin_ref[at], True).astype(BF16)
    for copy in copies:
        copy.wait()
    for at in range(8):
        dk = turn(dk_ref[at].T, cos_ref[at], sin_ref[at], True)
        d_ref[at, HEAD : 2 * HEAD] = dk.astype(BF16)
        d_ref[at, 2 * HEAD :] = dv_ref[at].T.astype(BF16)
        rows = []
        for j in range(4):
            flat = inverse[4 * at + j]
            start = pl.multiple_of((flat & 1) * BLOCK, BLOCK)
            rows.append(xv_ref[flat // 2, pl.ds(start, BLOCK), :])
        normal, _ = normalise(jnp.concatenate(rows, 0).astype(F32))
        part = dot(d_ref[at], (normal * gain_ref[...]).astype(BF16))
        wt_ref[:192] = part if at == 0 else wt_ref[:192] + part
    for d in range(4):
        start = pl.multiple_of((d // 2) * 256 + ((place[9] ^ d) & 1) * 128, 128)
        columns = (near_ref if d % 2 == 0 else far_ref)[d // 2]
        part = dot(columns.T, obv_ref[pl.ds(start, 128), :])
        wt_ref[192:] = part if d == 0 else wt_ref[192:] + part
    grad_ref[...] = wt_ref[...].T.astype(BF16).reshape(8, 96, 384)
    for b in range(16):
        flat = inverse[b]
        upper = 15 - b
        lo = d_ref[b // 4, :, (b % 4) * BLOCK : (b % 4 + 1) * BLOCK].astype(F32)
        up = d_ref[4 + upper // 4, :, (upper % 4) * BLOCK : (upper % 4 + 1) * BLOCK].astype(F32)
        tile = jnp.concatenate([lo, up], 1)
        turned = jnp.concatenate([up, lo], 1)
        away = (flat // 8 - place[12]) & 3
        all_ref[away, (flat // 2) % 4] = jnp.where(flat % 2 == 0, tile, turned).astype(BF16)
    for k, ref in enumerate((out0_ref, out1_ref, out2_ref, out3_ref)):
        ref[...] = all_ref[k]


def run_backward(
    inverse, place, do, blocks, wide, gain, kept, cosine, sine, id_row, ob, columns
):
    return pl.pallas_call(
        backward_kernel,
        out_shape=(
            *(SHAPE((4, 3 * HEAD, 2 * BLOCK), BF16),) * 4,
            SHAPE((8, 96, 384), BF16),
        ),
        in_specs=[SMEM] * 2 + [VMEM] + [ANY] * 5 + [VMEM] * 10 + [ANY] + [VMEM] * 2,
        out_specs=(VMEM,) * 5,
        scratch_shapes=[
            pltpu.VMEM((CHUNKS, 3 * HEAD, CHUNK), BF16),
            pltpu.VMEM((CHUNKS, CHUNK, HEAD), F32),
            pltpu.VMEM((CHUNKS, CHUNK, HEAD), F32),
            pltpu.VMEM((CHUNKS, HEAD, CHUNK), BF16),
            pltpu.VMEM((CHUNKS, CHUNK, HEAD), BF16),
            pltpu.VMEM((384, WIDTH), F32),
            pltpu.VMEM((4, 4, 3 * HEAD, 2 * BLOCK), BF16),
            pltpu.VMEM((16, 128, WIDTH), BF16),
            pltpu.VMEM((2 * CHUNK, WIDTH), BF16),
            pltpu.SemaphoreType.DMA((10,)),
        ],
        compiler_params=pltpu.CompilerParams(vmem_limit_bytes=60 << 20),
        cost_estimate=cost(22.0),
        name="attention_backward",
    )(inverse, place, do, *blocks, wide, gain, *kept, cosine, sine, id_row, ob, *columns)


def pick(core, same, other):
    first = jnp.where(core == 0, same, other)
    return jnp.concatenate([first, jnp.where(core == 0, other, same)], 0)


def assemble(place, units_ref, sems, gu_ref=None, down_ref=None, wout_ref=None):
    copies = []
    parts = ((wout_ref, 144, 96), (gu_ref, 0, 96), (down_ref, 96, 48))
    for target, first, size in parts:
        if target is not None:
            for k in range(8):
                start = ((place[13] ^ (k % 2)) * 4 + k // 2) * size
                rows = target.at[pl.ds(pl.multiple_of(start, 16), size)]
                source = units_ref.at[k // 2, k % 2, first : first + size]
                copies.append(pltpu.make_async_copy(source, rows, sems.at[len(copies)]))
    for copy in copies:
        copy.start()

    def wait(first, last):
        for copy in copies[first:last]:
            copy.wait()

    return wait


def feed_kernel(
    place, own_ref, other_ref, n0_ref, n1_ref, f0_ref, f1_ref, gain_ref, units_ref,
    keep_ref, send_ref, h_ref, d_ref, a_ref, quad_ref, y_ref, wout_ref,
    own_v, other_v, x_v, z_v, gu_v, down_v, wout_v, ob_v, mid_v, h_v, d_v, a_v, keep_v, send_v, y_v,
    sems, unit_sems,
):
    core, member = place[8], place[9]
    started = []

    def copy(source, target):
        started.append(pltpu.make_async_copy(source, target, sems.at[len(started)]))
        started[-1].start()
        return started[-1]

    tiles_in = [copy(own_ref.at[:6], own_v), copy(other_ref.at[:6], other_v)]
    arrays = (n0_ref, n1_ref, f0_ref, f1_ref)
    x_in = [copy(ref.at[:2], x_v.at[k]) for k, ref in enumerate(arrays)]
    units_in = assemble(place, units_ref, unit_sems, gu_v, down_v, wout_v)
    z_in = [copy(ref.at[2:], z_v.at[k]) for k, ref in enumerate(arrays)]

    def rows(i):
        return slice(CHUNK * i, CHUNK * (i + 1))

    def block(ref, i):
        return pick(core, ref[2 * (i % 2), i // 2], ref[2 * (i % 2) + 1, i // 2])

    for part in tiles_in:
        part.wait()
    for i in range(4):
        at = (member // 2) ^ i
        for c in range(2):
            base = CHUNK * i + 128 * c
            for z in range(2):
                tiles = []
                for k in range(2):
                    for x in range(3):
                        mine, theirs = own_v[2 * x + z, 2 * at + c], other_v[2 * x + z, 2 * at + c]
                        tiles.append(jnp.where(core == k, mine, theirs))
                for pair in range(3):
                    left, right = tiles[2 * pair], tiles[2 * pair + 1]
                    lanes = slice(384 * z + 128 * pair, 384 * z + 128 * (pair + 1))
                    ob_v[base : base + BLOCK, lanes] = jnp.concatenate(
                        [left[:, :BLOCK], right[:, :BLOCK]], 1
                    )
                    ob_v[base + BLOCK : base + 128, lanes] = jnp.concatenate(
                        [left[:, BLOCK:], right[:, BLOCK:]], 1
                    )
    out = [copy(ob_v.at[: 2 * CHUNK], quad_ref)]
    for part in x_in:
        part.wait()
    units_in(0, 8)
    out.append(copy(wout_v, wout_ref))
    for i in range(4):
        middle = block(x_v, i).astype(F32) + dot(ob_v[rows(i)], wout_v[...])
        mid_v[rows(i)] = middle
        normal, _ = normalise(middle)
        h_v[rows(i)] = (normal * gain_ref[...]).astype(BF16)
        out.append(copy(h_v.at[rows(i)], h_ref.at[rows(i)]))
    y_v[...] = mid_v[pl.ds(pl.multiple_of(core * 128, 128), 128), :]
    out.append(copy(y_v, y_ref))
    for part in z_in:
        part.wait()
    units_in(8, 24)
    for i in range(4):
        gu = dot(h_v[rows(i)], gu_v[...])
        g, u = gu[:, :384], gu[:, 384:]
        da = dot(block(z_v, i), down_v[...], 1, 1)
        sigma = jax.nn.sigmoid(g)
        swish = g * sigma
        a_v[rows(i)] = (swish * u).astype(BF16)
        d_v[rows(i), :384] = (da * u * (sigma + swish * (1.0 - sigma))).astype(BF16)
        d_v[rows(i), 384:] = (da * swish).astype(BF16)
        out.append(copy(a_v.at[rows(i)], a_ref.at[rows(i)]))
        out.append(copy(d_v.at[rows(i)], d_ref.at[rows(i)]))
    for i in range(4):
        mid_v[rows(i)] = dot(d_v[rows(i)], gu_v[...], 1, 1)
        keep = pl.multiple_of(CHUNK * i + core * 128, 128)
        send = pl.multiple_of(CHUNK * i + 128 - core * 128, 128)
        keep_v[i] = mid_v[pl.ds(keep, 128), :].astype(BF16)
        send_v[i] = mid_v[pl.ds(send, 128), :].astype(BF16)
        out.append(copy(send_v.at[i], send_ref.at[i]))
        out.append(copy(keep_v.at[i], keep_ref.at[i]))
    for part in out:
        part.wait()


def run_feed(place, own, other, blocks, gain, units):
    rows = 4 * CHUNK
    scratch = [
        ((6, 8, BLOCK, 128), BF16),
        ((6, 8, BLOCK, 128), BF16),
        ((4, 2, 128, WIDTH), BF16),
        ((4, 2, 128, WIDTH), BF16),
        ((WIDTH, WIDTH), BF16),
        ((WIDTH // 2, WIDTH), BF16),
        ((WIDTH, WIDTH), BF16),
        ((rows, WIDTH), BF16),
        ((rows, WIDTH), F32),
        ((rows, WIDTH), BF16),
        ((rows, WIDTH), BF16),
        ((rows, WIDTH // 2), BF16),
        ((4, 128, WIDTH), BF16),
        ((4, 128, WIDTH), BF16),
        ((128, WIDTH), F32),
    ]
    return pl.pallas_call(
        feed_kernel,
        out_shape=(
            SHAPE((4, 128, WIDTH), BF16),
            SHAPE((4, 128, WIDTH), BF16),
            SHAPE((rows, WIDTH), BF16),
            SHAPE((rows, WIDTH), BF16),
            SHAPE((rows, WIDTH // 2), BF16),
            SHAPE((2 * CHUNK, WIDTH), BF16),
            SHAPE((128, WIDTH), F32),
            SHAPE((WIDTH, WIDTH), BF16),
        ),
        in_specs=[SMEM] + [ANY] * 6 + [VMEM, ANY],
        out_specs=(ANY,) * 8,
        scratch_shapes=[pltpu.VMEM(*shape) for shape in scratch]
        + [pltpu.SemaphoreType.DMA((40,)), pltpu.SemaphoreType.DMA((24,))],
        compiler_params=pltpu.CompilerParams(vmem_limit_bytes=60 << 20),
        cost_estimate=cost(40),
        name="feed",
    )(place, own, other, *blocks, gain, units)


def weights_kernel(
    place, h_ref, d_ref, a_ref, z0_ref, z1_ref, z2_ref, z3_ref, units_ref,
    out_ref, keep_ref, send_ref,
    h_v, d_v, a_v, dz_v, gu_v, gd_v, z_v, down_v, out_v, keep_v, send_v, sems, unit_sems,
):
    core = place[8]
    started = []

    def copy(source, target):
        started.append(pltpu.make_async_copy(source, target, sems.at[len(started)]))
        started[-1].start()
        return started[-1]

    def rows(i):
        return slice(2 * CHUNK * i, 2 * CHUNK * (i + 1))

    parts = []
    for i in range(2):
        parts.append([copy(h_ref.at[rows(i)], h_v.at[rows(i)]), copy(d_ref.at[rows(i)], d_v.at[rows(i)])])
        if i == 0:
            dz_in = [
                copy(ref.at[2:], dz_v.at[k]) for k, ref in enumerate((z0_ref, z1_ref, z2_ref, z3_ref))
            ]
            units_in = assemble(place, units_ref, unit_sems, down_ref=down_v)
        parts[i].append(copy(a_ref.at[rows(i)], a_v.at[rows(i)]))
    out = []
    for i in range(2):
        parts[i][0].wait()
        parts[i][1].wait()
        gu = dot(h_v[rows(i)], d_v[rows(i)], 0, 0)
        gu_v[...] = gu if i == 0 else gu_v[...] + gu
    for part in dz_in + [parts[0][2], parts[1][2]]:
        part.wait()
    units_in(0, 8)
    for i in range(2):
        dz = [pick(core, dz_v[0, i], dz_v[1, i]), pick(core, dz_v[2, i], dz_v[3, i])]
        gd = dot(a_v[rows(i)], jnp.concatenate(dz, 0), 0, 0)
        gd_v[...] = gd if i == 0 else gd_v[...] + gd
    for f in range(8):
        base = (2 * (f % 4) + f // 4) * 144
        out_v[base : base + 96] = gu_v[96 * f : 96 * (f + 1)].astype(BF16)
        out_v[base + 96 : base + 144] = gd_v[48 * f : 48 * (f + 1)].astype(BF16)
    out.append(copy(out_v, out_ref))
    for i in range(2):
        z_v[...] = dot(a_v[rows(i)], down_v[...])
        for j in range(2):
            keep = pl.multiple_of(256 * j + core * 128, 128)
            send = pl.multiple_of(256 * j + 128 - core * 128, 128)
            keep_v[2 * i + j] = z_v[pl.ds(keep, 128), :].astype(BF16)
            send_v[2 * i + j] = z_v[pl.ds(send, 128), :].astype(BF16)
    out += [copy(keep_v, keep_ref), copy(send_v, send_ref)]
    for part in out:
        part.wait()


def run_weights(place, h, d, a, blocks, units):
    rows = 4 * CHUNK
    scratch = [
        ((rows, WIDTH), BF16),
        ((rows, WIDTH), BF16),
        ((rows, WIDTH // 2), BF16),
        ((4, 2, 128, WIDTH), BF16),
        ((WIDTH, WIDTH), F32),
        ((WIDTH // 2, WIDTH), F32),
        ((2 * CHUNK, WIDTH), F32),
        ((WIDTH // 2, WIDTH), BF16),
        ((8 * 144, WIDTH), BF16),
        ((4, 128, WIDTH), BF16),
        ((4, 128, WIDTH), BF16),
    ]
    return pl.pallas_call(
        weights_kernel,
        out_shape=(SHAPE((8 * 144, WIDTH), BF16),) + (SHAPE((4, 128, WIDTH), BF16),) * 2,
        in_specs=[SMEM] + [ANY] * 8,
        out_specs=(ANY,) * 3,
        scratch_shapes=[pltpu.VMEM(*shape) for shape in scratch]
        + [pltpu.SemaphoreType.DMA((16,)), pltpu.SemaphoreType.DMA((8,))],
        compiler_params=pltpu.CompilerParams(vmem_limit_bytes=60 << 20),
        cost_estimate=cost(9),
        name="weights",
    )(place, h, d, a, *blocks, units)


def middle_kernel(
    place, p0_ref, p1_ref, p2_ref, p3_ref, y_ref, cot_ref, gain_ref, wout_ref,
    dy_ref, keep_ref, send_ref, do_ref, columns_ref,
):
    dh = sum(ref[...].astype(F32) for ref in (p0_ref, p1_ref, p2_ref, p3_ref))
    normal, scale = normalise(y_ref[...])
    dy = cot_ref[...].astype(F32) + norm_back(dh, normal, scale, gain_ref[...])
    dy_ref[...] = dy
    low = dy.astype(BF16)
    do = dot(wout_ref[...], low, 1, 1).astype(BF16)
    for t in range(4):
        for x in range(4):
            h = 3 * t + min(x, 2)
            do_ref[4 * x + t] = do[HEAD * h : HEAD * (h + 1)]
    for r in range(4):
        columns_ref[place[11] ^ r] = low[:, 192 * r : 192 * (r + 1)]
    keep_ref[...] = columns_ref[:2]
    send_ref[...] = columns_ref[2:]


def run_middle(place, parts, y, cotangent, gain, wout):
    return pl.pallas_call(
        middle_kernel,
        out_shape=(
            SHAPE((128, WIDTH), F32),
            *(SHAPE((2, 128, 192), BF16),) * 2,
            SHAPE((16, HEAD, 128), BF16),
        ),
        in_specs=[SMEM] + [VMEM] * 8,
        out_specs=(VMEM,) * 4,
        scratch_shapes=[
            pltpu.VMEM((4, 128, 192), BF16),
        ],
        compiler_params=pltpu.CompilerParams(vmem_limit_bytes=10 << 20),
        cost_estimate=cost(12.0),
        name="middle",
    )(place, *parts, y, cotangent, gain, wout)


def inputs_kernel(place, d0_ref, d1_ref, d2_ref, d3_ref, w_ref, keep_ref, send_ref, sum_ref):
    core, column = place[8], place[12]
    for c in range(4):
        for k, ref in enumerate((d0_ref, d1_ref, d2_ref, d3_ref)):
            x = (column - k) & 3
            at = jnp.minimum(x, 2) * HEAD
            w = jnp.concatenate(
                [w_ref[pl.ds(pl.multiple_of(base + at, HEAD), HEAD), :] for base in (0, 192, 384)],
                0,
            )
            part = jnp.where(x < 3, dot(ref[c], w, 0, 0), 0.0)
            sum_ref[c] = part if k == 0 else sum_ref[c] + part
    for z in range(2):
        keep_ref[z] = sum_ref[2 * z + core].astype(BF16)
        send_ref[z] = sum_ref[2 * z + 1 - core].astype(BF16)


def run_inputs(place, parts, w_rows):
    return pl.pallas_call(
        inputs_kernel,
        out_shape=(SHAPE((2, 128, WIDTH), BF16),) * 2,
        in_specs=[SMEM] + [VMEM] * 5,
        out_specs=(VMEM,) * 2,
        scratch_shapes=[pltpu.VMEM((4, 128, WIDTH), F32)],
        compiler_params=pltpu.CompilerParams(vmem_limit_bytes=12 << 20),
        cost_estimate=cost(3),
        name="inputs",
    )(place, *parts, w_rows)


def finish_feed_kernel(
    all_ref, gate_ref, up_ref, gain_ref, g_ref, u_ref, d_ref, n_ref,
    all_v, w_v, o_v, d_v, sems,
):
    started = []

    def copy(source, target):
        started.append(pltpu.make_async_copy(source, target, sems.at[len(started)]))
        started[-1].start()
        return started[-1]

    halves = [copy(all_ref.at[8 * h : 8 * h + 8], all_v.at[8 * h : 8 * h + 8]) for h in range(2)]
    weights = [copy(gate_ref, w_v.at[0]), copy(up_ref, w_v.at[1])]
    total = jnp.zeros((96, 1), F32)
    out = []
    for half, out_ref in enumerate((g_ref, u_ref)):
        halves[half].wait()
        tiles = [all_v[8 * half + m, :96] for m in range(8)]
        for f in range(8):
            block = jnp.concatenate([t[:, 48 * f : 48 * (f + 1)] for t in tiles], 1)
            lanes = slice(384 * f, 384 * (f + 1))
            o_v[half, :, lanes] = block.astype(F32)
        out.append(copy(o_v.at[half], out_ref))
        side = slice(384 * half, 384 * (half + 1))
        for m in range(8):
            d_v[48 * m : 48 * (m + 1), side] = all_v[8 * half + m, 96:].astype(F32)
    out.append(copy(d_v, d_ref))
    for half in range(2):
        weights[half].wait()
        total += jnp.sum(w_v[half].astype(F32) * o_v[half], axis=1, keepdims=True)
    n_ref[...] = jnp.broadcast_to(total, (96, 128)).T[:1] / gain_ref[...].astype(F32)
    for part in out:
        part.wait()


def run_finish_feed(whole, gate, up, gain):
    return pl.pallas_call(
        finish_feed_kernel,
        out_shape=(
            SHAPE((96, 3072), F32),
            SHAPE((96, 3072), F32),
            SHAPE((384, WIDTH), F32),
            SHAPE((1, 96), F32),
        ),
        in_specs=[ANY] * 3 + [VMEM],
        out_specs=(ANY,) * 3 + (VMEM,),
        scratch_shapes=[
            pltpu.VMEM((16, 144, 384), BF16),
            pltpu.VMEM((2, 96, 3072), BF16),
            pltpu.VMEM((2, 96, 3072), F32),
            pltpu.VMEM((384, WIDTH), F32),
            pltpu.SemaphoreType.DMA((8,)),
        ],
        compiler_params=pltpu.CompilerParams(vmem_limit_bytes=60 << 20),
        cost_estimate=cost(6),
        name="finish_feed",
    )(whole, gate, up, gain.reshape(1, 96))


def finish_heads_kernel(place, *refs):
    own_ref, other_ref = refs[:2]
    wq_ref, wk_ref, wv_ref, gain_ref, q_ref, k_ref, v_ref, o_ref, n_ref = refs[2:]
    core = place[8]
    tiles = {}
    for x in range(4):
        for z in range(2):
            mine, theirs = own_ref[2 * x + z], other_ref[2 * x + z]
            for k in range(2):
                tiles[x, 2 * z + k] = jnp.where(core == k, mine, theirs).astype(F32)
    total = jnp.zeros((96, 1), F32)
    for j, (w_ref, out_ref) in enumerate(((wq_ref, q_ref), (wk_ref, k_ref), (wv_ref, v_ref))):
        lanes = slice(HEAD * j, HEAD * (j + 1))
        whole = jnp.concatenate([tiles[h % 3, h // 3][:, lanes] for h in range(12)], 1)
        out_ref[...] = whole
        total += jnp.sum(w_ref[...].astype(F32) * whole, axis=1, keepdims=True)
    n_ref[...] = jnp.broadcast_to(total, (96, 128)).T[:1] / gain_ref[...].astype(F32)
    o_ref[...] = jnp.concatenate(
        [sum(tiles[x, t][:, 192:] for x in range(4)) for t in range(4)], 1
    )


def run_finish_heads(place, own, other, query, key, value, gain):
    return pl.pallas_call(
        finish_heads_kernel,
        out_shape=(SHAPE((96, WIDTH), F32),) * 4 + (SHAPE((1, 96), F32),),
        in_specs=[SMEM] + [VMEM] * 6,
        out_specs=(VMEM,) * 5,
        compiler_params=pltpu.CompilerParams(vmem_limit_bytes=12 << 20),
        cost_estimate=cost(8),
        name="finish_heads",
    )(place, own, other, query, key, value, gain.reshape(1, 96))


def fold_kernel(in_ref, out_ref):
    total = jnp.sum(in_ref[...].astype(F32), axis=0).astype(BF16)
    for k in range(8):
        out_ref[k] = total


def run_fold(parts):
    return pl.pallas_call(
        fold_kernel,
        out_shape=SHAPE(parts.shape, BF16),
        in_specs=[VMEM],
        out_specs=VMEM,
        compiler_params=pltpu.CompilerParams(vmem_limit_bytes=6 << 20),
        cost_estimate=cost(0.3),
        name="fold",
    )(parts)


def trade(value, distance):
    return lax.ppermute(value, "ctx", [(i, i ^ distance) for i in range(16)])


def pair_kernel(keep_ref, got_ref, *outs):
    for k, ref in enumerate(outs):
        ref[...] = (keep_ref[k].astype(F32) + got_ref[k].astype(F32)).astype(BF16)


def run_pair(keep, got):
    return pl.pallas_call(
        pair_kernel,
        out_shape=(SHAPE((128, WIDTH), BF16),) * 4,
        in_specs=[VMEM] * 2,
        out_specs=(VMEM,) * 4,
        compiler_params=pltpu.CompilerParams(vmem_limit_bytes=8 << 20),
        cost_estimate=cost(2),
        name="pair",
    )(keep, got)


def norm_back(grad_normed, normal_rows, inverse, gains):
    scaled = grad_normed * gains
    return inverse * (scaled - normal_rows * jnp.mean(scaled * normal_rows, axis=-1, keepdims=True))


def local(
    tokens, block_table, seq_ids, w_query, w_key, w_value, w_out, w_gate, w_up, w_down,
    gain_attn, gain_mlp, cotangent,
):
    index = lax.axis_index("ctx")
    shard = lax.axis_index("fsdp")
    rank, column = index % 4, index // 4
    core, member, group = index % 2, index % 8, index // 8

    rings = [[0, 1, 2, 3], [4, 5, 6, 7]]

    blocks = block_table.reshape(-1)
    numbers = jnp.arange(32, dtype=jnp.int32)
    inverse = jnp.sum(
        jnp.where(blocks[None, :] == numbers[:, None], numbers[None, :], 0), axis=1
    ).astype(jnp.int32)
    frequency = jnp.power(THETA, -(jnp.arange(HALF, dtype=F32) * 2.0) / HEAD)
    own_blocks = lax.dynamic_slice_in_dim(blocks, 8 * column, 8)
    places = (own_blocks[:, None] * BLOCK + jnp.arange(BLOCK, dtype=jnp.int32)).reshape(4, 1, 128)
    angles = places.astype(F32) * frequency[None, :, None]
    place = jnp.stack(
        [(shard // 4 ^ dz) * 4 + (shard + dy) % 4 for dz, dy in RING]
        + [core, member, group, rank, column, shard // 4, index]
    ).astype(jnp.int32)

    units = run_pack_heads(w_query, w_key, w_value, gain_attn, gain_mlp)
    w_heads = lax.all_to_all(units, "fsdp", 0, 0).reshape(WIDTH, 640)
    x_own = after(tokens[0], units)
    x_blocks = [tokens[0], trade(x_own, 1)]
    unit, both = run_pack_units(w_gate, w_up, w_down, w_out, x_blocks[1])
    x_blocks.append(trade(x_own, 2))
    across = lax.ppermute(after(unit, x_blocks[2]), "fsdp", [(i, i ^ 4) for i in range(8)])
    own = after(jnp.stack([x_own, cotangent[0]]), x_blocks[1])
    own = [own, trade(own, 4), trade(own[0], 8)]
    x_blocks.append(trade(after(x_blocks[2], own, unit), 1))
    w_heads, angles = lax.optimization_barrier((w_heads, (jnp.cos(angles), jnp.sin(angles))))
    *tiles, w_rows = run_project(place, w_heads, x_blocks, *angles)
    gains = w_rows[576:578].astype(F32)
    gain_one, gain_two = gains[:1], gains[1:]

    ids = after(seq_ids[0], w_rows).reshape(32, BLOCK)
    hits = (inverse[16:, None] == numbers[None, :]).astype(jnp.int32)
    ids = jnp.sum(hits[:, :, None] * ids[None], axis=1).reshape(HALF_SEQ)
    id_row = ids.reshape(1, HALF_SEQ)
    angles = after(jnp.arange(SEQ, dtype=F32), w_rows).reshape(CHUNKS, 1, CHUNK)
    angles = angles * frequency[None, :, None]
    cosine, sine = jnp.cos(angles), jnp.sin(angles)

    for k in range(1, 4):
        tiles[k] = lax.ppermute(
            tiles[k], "ctx", [(i, (i + 4 * k) % 16) for i in range(16)]
        )
    units = lax.all_gather(
        both.at[1].set(after(across, w_rows)), "fsdp", axis=0, axis_index_groups=rings
    )
    near = jnp.stack([own[0][0], own[1][0], own[0][1], own[1][1]])
    far = trade(after(near, w_rows), 2)
    tiles, cosine, sine = lax.optimization_barrier((tiles, cosine, sine))
    o_tiles, *kept = run_forward(inverse, place, tiles, id_row)
    o_own = lax.all_to_all(o_tiles, "ctx", 0, 0, axis_index_groups=SAME_CORE)
    blocks = [near, trade(near, 1), far, trade(far, 1)]
    o_other = trade(after(o_own, blocks), 1)
    eights = [list(range(8)), list(range(8, 16))]
    wide = lax.all_gather(after(own[2], o_tiles), "ctx", axis=0, axis_index_groups=eights)

    keep, send, h2, dgu, a, ob, middle, wout = run_feed(
        place, o_own, o_other, blocks, gain_two, units
    )
    pair = run_pair(keep, trade(send, 1))
    parts = [pair[0]] + [trade(pair[k], 2 * k) for k in (1, 2, 3)]

    ff, z_keep, z_send = run_weights(place, after(h2, pair), dgu, a, blocks, units)
    dy1, *columns, do = run_middle(place, after(parts, ff), middle, cotangent[0], gain_two, wout)
    ff = lax.psum_scatter(
        ff, "fsdp", scatter_dimension=0, tiled=True, axis_index_groups=rings
    )
    z = run_pair(z_keep, trade(after(z_send, do), 1))
    z = [z[0]] + [trade(z[k], 2 * k) for k in (1, 2, 3)]
    do = lax.all_to_all(do, "ctx", 0, 0)
    columns = jnp.stack([columns[0], trade(columns[1], 2)], 1)
    columns = [columns[0], trade(columns[1], 1)]
    *d_parts, small = run_backward(
        inverse, place, do, blocks, wide, gain_one, kept, cosine, sine, id_row, ob, columns
    )
    small, ff, z = lax.optimization_barrier((small, ff, z))
    small = lax.all_to_all(small, "fsdp", 0, 0)
    far = shard // 4 == 1
    away = jnp.where(far, ff[:144], ff[144:])
    ff = jnp.where(far, ff[144:], ff[:144])

    def half(value, flip):
        return jnp.where((group == 1) ^ flip, value[:, 384:], value[:, :384])

    def across(value, flip, shift):
        pairs = [(8 * c + f, 8 * (c ^ shift) + (f ^ flip)) for f in range(8) for c in range(16)]
        return lax.ppermute(value, ("ctx", "fsdp"), pairs)

    halves = half(ff, False), half(ff, True), half(away, False), half(away, True)
    parts = [
        halves[0], across(halves[1], 0, 8), across(halves[2], 4, 0), across(halves[3], 4, 8)
    ]
    ff = sum(part.astype(F32) for part in parts).astype(BF16)
    ff = lax.all_gather(ff, "ctx", axis=0)

    folded = run_fold(small)
    for k in range(1, 4):
        d_parts[k] = lax.ppermute(
            after(d_parts[k], folded), "ctx", [(i, (i + 4 * k) % 16) for i in range(16)]
        )
    small = lax.all_to_all(folded, "ctx", 0, 0, axis_index_groups=SAME_CORE)
    total_query, total_key, total_value, total_out, total_gain_one = run_finish_heads(
        place, small, trade(small, 1), w_query, w_key, w_value, gain_attn
    )

    keep, send = run_inputs(place, d_parts, w_rows)
    summed = keep.astype(F32) + trade(send, 1).astype(F32)
    low = rank // 2 == 0
    keep = jnp.where(low, summed[0], summed[1])
    send = jnp.where(low, summed[1], summed[0]).astype(BF16)
    dh1 = keep + trade(send, 2).astype(F32)
    normal_one, inverse_one = normalise(tokens[0].astype(F32))
    grad_stream = dy1 + norm_back(dh1, normal_one, inverse_one, gain_one)
    result = middle + sum(part.astype(F32) for part in z)
    grad_stream, result = grad_stream.astype(BF16), result.astype(BF16)
    ff, grad_stream, result, total_query = lax.optimization_barrier(
        (ff, grad_stream, result, total_query)
    )
    total_gate, total_up, total_down, total_gain_two = run_finish_feed(
        ff, w_gate, w_up, gain_mlp
    )

    return (
        result[None],
        grad_stream[None],
        total_query,
        total_key,
        total_value,
        total_out,
        total_gate,
        total_up,
        total_down,
        total_gain_one.reshape(96),
        total_gain_two.reshape(96),
    )


def solution(mesh):
    rows = P("fsdp", "ctx", None)
    weight = P("fsdp", None)
    return jax.shard_map(
        local,
        mesh=mesh,
        in_specs=(rows, P(), weight) + (weight,) * 7 + (P("fsdp"), P("fsdp"), rows),
        out_specs=(rows, rows) + (weight,) * 7 + (P("fsdp"), P("fsdp")),
        check_vma=False,
    )
```

```python
import jax
import jax.numpy as jnp
from jax import lax
from jax.experimental import pallas as pl
from jax.experimental.pallas import tpu as pltpu
from jax.sharding import PartitionSpec as P

EPS = 1e-05
THETA = 10000.0
WIDTH = 768
HEAD = 64
HALF = 32
SEQ = 2048
BLOCK = 64
CHUNK = 256
CHUNKS = SEQ // CHUNK
HALF_SEQ = SEQ // 2
F32 = jnp.float32
BF16 = jnp.bfloat16

QUADS = [[4 * i + j for j in range(4)] for i in range(4)]
COLUMNS = [[j + 4 * i for i in range(4)] for j in range(4)]
SAME_CORE = [[j + 2 * i for i in range(8)] for j in range(2)]
FOUR_CHIPS = [[8 * g + j + 2 * i for i in range(4)] for g in range(2) for j in range(2)]
RING = [(0, 0), (1, 0), (0, 3), (0, 1), (1, 3), (1, 1), (0, 2), (1, 2)]

VMEM = pl.BlockSpec(memory_space=pltpu.VMEM)
SMEM = pl.BlockSpec(memory_space=pltpu.SMEM)
ANY = pl.BlockSpec(memory_space=pl.ANY)
SHAPE = jax.ShapeDtypeStruct


def cost(microseconds):
    return pl.CostEstimate(
        flops=int(microseconds * 1.1e9), bytes_accessed=int(microseconds * 3.6e6), transcendentals=0
    )


def after(value, *others):
    return lax.optimization_barrier((value, others))[0]


def dot(left, right, left_dim=1, right_dim=0):
    return lax.dot_general(
        left, right, (((left_dim,), (right_dim,)), ((), ())), preferred_element_type=F32
    )


def turn(block, cosine, sine, backward):
    first, second = block[:HALF], block[HALF:]
    if backward:
        return jnp.concatenate([first * cosine + second * sine, second * cosine - first * sine], 0)
    return jnp.concatenate([first * cosine - second * sine, second * cosine + first * sine], 0)


def normalise(x):
    scale = lax.rsqrt(jnp.mean(x * x, axis=-1, keepdims=True) + EPS)
    return x * scale, scale


def document_starts(id_row):
    start = jnp.zeros_like(id_row)
    for number in (1, 2, 3):
        before = jnp.sum((id_row < number).astype(F32), axis=1, keepdims=True).astype(jnp.int32)
        start = jnp.where(id_row >= number, before, start)
    return start


def masked(scores, half, part, starts, other):
    keys = scores.shape[0]
    base = keys - CHUNK
    row = lax.broadcasted_iota(jnp.int32, (CHUNK, CHUNK), 0)
    column = lax.broadcasted_iota(jnp.int32, (CHUNK, CHUNK), 1)
    if half == 1:
        place = lax.broadcasted_iota(jnp.int32, scores.shape, 0)
        inside = place >= starts[:, part * CHUNK : (part + 1) * CHUNK]
        scores = jnp.where(inside, scores, other)
    last = jnp.where(row <= column, scores[base:], other)
    return last if base == 0 else jnp.concatenate([scores[:base], last], 0)


def swap_lanes(tile):
    return jnp.concatenate([tile[:, BLOCK:], tile[:, :BLOCK]], 1)


def sort_tiles(inverse, in_ref, out_ref):
    for b in range(16):
        flat = inverse[b]
        upper = 15 - b
        tile = in_ref[flat // 2].astype(F32)
        tile = jnp.where(flat % 2 == 0, tile, swap_lanes(tile)).astype(BF16)
        out_ref[b // 4, :, (b % 4) * BLOCK : (b % 4 + 1) * BLOCK] = tile[:, :BLOCK]
        out_ref[4 + upper // 4, :, (upper % 4) * BLOCK : (upper % 4 + 1) * BLOCK] = tile[:, BLOCK:]


def pack_heads_kernel(q_ref, k_ref, v_ref, one_ref, two_ref, out_ref):
    rank = lax.axis_index("ctx") & 3
    column = lax.broadcasted_iota(jnp.int32, (96, 64), 1)
    one = jnp.broadcast_to(one_ref[...].astype(F32), (128, 96)).T[:, :64]
    two = jnp.broadcast_to(two_ref[...].astype(F32), (128, 96)).T[:, :64]
    gains = jnp.where(column == 0, one, jnp.where(column == 1, two, 0.0)).astype(BF16)
    for r in range(4):

        @pl.when(rank == r)
        def _():
            lanes = slice(192 * r, 192 * (r + 1))
            unit = jnp.concatenate([q_ref[:, lanes], k_ref[:, lanes], v_ref[:, lanes], gains], 1)
            for f in range(8):
                out_ref[f] = unit


def run_pack_heads(query, key, value, gain_one, gain_two):
    return pl.pallas_call(
        pack_heads_kernel,
        out_shape=SHAPE((8, 96, 640), BF16),
        in_specs=[VMEM] * 5,
        out_specs=VMEM,
        compiler_params=pltpu.CompilerParams(vmem_limit_bytes=60 << 20),
        cost_estimate=cost(2),
        name="pack_heads",
    )(query, key, value, gain_one.reshape(1, 96), gain_two.reshape(1, 96))


def pack_units_kernel(gate_ref, up_ref, down_ref, wout_ref, _, out_ref, both_ref):
    index = lax.axis_index("ctx")
    member = index & 7
    for m in range(8):

        @pl.when(member == m)
        def _():
            parts = [
                ref[:, 384 * f + 48 * m : 384 * f + 48 * (m + 1)]
                for ref in (gate_ref, up_ref)
                for f in range(8)
            ]
            out_ref[:96] = jnp.concatenate(parts, 1)

    out_ref[96:144] = down_ref[pl.ds(pl.multiple_of(member * 48, 16), 48), :]
    out_ref[144:] = wout_ref[...]
    both_ref[0] = out_ref[...]


def run_pack_units(gate, up, down, wout, after):
    return pl.pallas_call(
        pack_units_kernel,
        out_shape=(SHAPE((240, WIDTH), BF16), SHAPE((2, 240, WIDTH), BF16)),
        in_specs=[VMEM] * 4 + [ANY],
        out_specs=(VMEM, VMEM),
        compiler_params=pltpu.CompilerParams(vmem_limit_bytes=60 << 20),
        cost_estimate=cost(2.4),
        name="pack_units",
    )(gate, up, down, wout, after)


def project_kernel(
    place, w_ref, x0_ref, x1_ref, x2_ref, x3_ref, cos_ref, sin_ref,
    out0_ref, out1_ref, out2_ref, out3_ref, wt_ref, out_ref,
):
    wt_ref[...] = w_ref[...].T
    gain = wt_ref[576:592].astype(F32)[:1]
    for d, block in enumerate((x0_ref, x1_ref, x2_ref, x3_ref)):
        c = place[11] ^ d
        normal, _ = normalise(block[...].astype(F32))
        h = (normal * gain).astype(BF16)
        qkv = dot(wt_ref[:576], h, 1, 1)
        cosine, sine = cos_ref[c], sin_ref[c]
        for j in range(3):
            at = HEAD * j
            q = (turn(qkv[at : at + HEAD], cosine, sine, False).astype(BF16) * 0.125).astype(BF16)
            k = turn(qkv[192 + at : 192 + at + HEAD], cosine, sine, False).astype(BF16)
            v = qkv[384 + at : 384 + at + HEAD].astype(BF16)
            for target in (2, 3) if j == 2 else (j,):
                away = (target - place[12]) & 3
                out_ref[away, c, :HEAD] = q
                out_ref[away, c, HEAD : 2 * HEAD] = k
                out_ref[away, c, 2 * HEAD :] = v
    for k, ref in enumerate((out0_ref, out1_ref, out2_ref, out3_ref)):
        ref[...] = out_ref[k]


def run_project(place, w, blocks, cosine, sine):
    return pl.pallas_call(
        project_kernel,
        out_shape=(SHAPE((4, 3 * HEAD, 128), BF16),) * 4 + (SHAPE((640, WIDTH), BF16),),
        in_specs=[SMEM] + [VMEM] * 7,
        out_specs=(VMEM,) * 5,
        scratch_shapes=[pltpu.VMEM((4, 4, 3 * HEAD, 128), BF16)],
        compiler_params=pltpu.CompilerParams(vmem_limit_bytes=14 << 20),
        cost_estimate=cost(40),
        name="project",
    )(place, w, *blocks, cosine, sine)


def forward_kernel(
    inverse, place, in0_ref, in1_ref, in2_ref, in3_ref, id_row,
    out_ref, q_ref, k_ref, v_ref, krow_ref, o_ref, lse_ref, all_ref, orow_ref, in_ref,
):
    for k, ref in enumerate((in0_ref, in1_ref, in2_ref, in3_ref)):
        in_ref[pl.ds(4 * ((place[12] - k) & 3), 4)] = ref[...]
    sort_tiles(inverse, in_ref, all_ref)
    starts = document_starts(id_row[...])
    for at in range(CHUNKS):
        q_ref[at] = all_ref[at, :HEAD]
        k_ref[at] = all_ref[at, HEAD : 2 * HEAD]
        v_ref[at] = all_ref[at, 2 * HEAD :]
        krow_ref[at] = all_ref[at, HEAD : 2 * HEAD].T
    for half in range(2):
        for part in range(4):
            at = 4 * half + part
            keys = (part + 1) * CHUNK
            k = krow_ref[4 * half : 4 * half + part + 1].reshape(keys, HEAD)
            s = dot(k, q_ref[at])
            s = masked(s, half, part, starts, -1e30)
            top = jnp.max(s, axis=0, keepdims=True)
            p = jnp.exp(s - top)
            total = jnp.sum(p, axis=0, keepdims=True)
            low = p.astype(BF16)
            o = dot(v_ref[4 * half], low[:CHUNK])
            for j in range(1, part + 1):
                o += dot(v_ref[4 * half + j], low[j * CHUNK : (j + 1) * CHUNK])
            o = o / total
            o_ref[at] = o
            orow_ref[at] = o.T
            lse_ref[at] = top + jnp.log(total)
    for b in range(16):
        flat = inverse[b]
        upper = 15 - b
        lo = orow_ref[b // 4, (b % 4) * BLOCK : (b % 4 + 1) * BLOCK, :]
        up = orow_ref[4 + upper // 4, (upper % 4) * BLOCK : (upper % 4 + 1) * BLOCK, :]
        tile = jnp.concatenate([lo, up], 1)
        turned = jnp.concatenate([up, lo], 1)
        tile = jnp.where(flat % 2 == 0, tile, turned).astype(BF16)
        group = flat // 16
        for chip in range(4):
            out_ref[4 * group + chip, (flat // 2) % 8] = tile


def run_forward(inverse, place, tiles, id_row):
    return pl.pallas_call(
        forward_kernel,
        out_shape=(
            SHAPE((8, 8, BLOCK, 128), BF16),
            SHAPE((CHUNKS, HEAD, CHUNK), BF16),
            SHAPE((CHUNKS, HEAD, CHUNK), BF16),
            SHAPE((CHUNKS, HEAD, CHUNK), BF16),
            SHAPE((CHUNKS, CHUNK, HEAD), BF16),
            SHAPE((CHUNKS, HEAD, CHUNK), F32),
            SHAPE((CHUNKS, 1, CHUNK), F32),
        ),
        in_specs=[SMEM] * 2 + [VMEM] * 5,
        out_specs=(VMEM,) * 7,
        scratch_shapes=[
            pltpu.VMEM((CHUNKS, 3 * HEAD, CHUNK), BF16),
            pltpu.VMEM((CHUNKS, CHUNK, HEAD), F32),
            pltpu.VMEM((16, 3 * HEAD, 128), BF16),
        ],
        compiler_params=pltpu.CompilerParams(vmem_limit_bytes=24 << 20),
        cost_estimate=cost(40),
        name="attention_forward",
    )(inverse, place, *tiles, id_row)


def backward_kernel(
    inverse, place, do_ref, b0_ref, b1_ref, b2_ref, b3_ref, wide_ref, gain_ref,
    q_ref, k_ref, v_ref, krow_ref, o_ref, lse_ref, cos_ref, sin_ref,
    id_row, ob_ref, near_ref, far_ref,
    out0_ref, out1_ref, out2_ref, out3_ref, grad_ref,
    d_ref, dk_ref, dv_ref, dot_ref, vrow_ref, wt_ref, all_ref, xv_ref, obv_ref, xsem,
):
    other = xv_ref.at[pl.ds(8 - 8 * place[10], 8)]
    copies = [
        pltpu.make_async_copy(ob_ref, obv_ref, xsem.at[8]),
        pltpu.make_async_copy(wide_ref, other, xsem.at[9]),
    ]
    for k, ref in enumerate((b0_ref, b1_ref, b2_ref, b3_ref)):
        for j in range(2):
            at = place[14] ^ (k + 4 * j)
            copies.append(pltpu.make_async_copy(ref.at[j], xv_ref.at[at], xsem.at[2 * k + j]))
    for copy in copies:
        copy.start()
    sort_tiles(inverse, do_ref, dot_ref)
    starts = document_starts(id_row[...])
    for half in range(2):
        for part in range(4):
            at = 4 * half + part
            vrow_ref[at] = v_ref[at].T
            keys = (part + 1) * CHUNK
            first = 4 * half
            k = krow_ref[first : first + part + 1].reshape(keys, HEAD)
            v = vrow_ref[first : first + part + 1].reshape(keys, HEAD)
            q = q_ref[at]
            do = dot_ref[at]
            delta = jnp.sum(do.astype(F32) * o_ref[at], axis=0, keepdims=True)
            s = dot(k, q) - lse_ref[at]
            p = jnp.exp(masked(s, half, part, starts, -1e30))
            ds = (p * (dot(v, do) - delta)).astype(BF16)
            dv = dot(p.astype(BF16), do.T).reshape(part + 1, CHUNK, HEAD)
            dk = dot(ds, q.T).reshape(part + 1, CHUNK, HEAD)
            if part:
                dv_ref[first : first + part] += dv[:part]
                dk_ref[first : first + part] += dk[:part]
            dv_ref[at] = dv[part]
            dk_ref[at] = dk[part]
            dq = dot(k_ref[first], ds[:CHUNK])
            for j in range(1, part + 1):
                dq += dot(k_ref[first + j], ds[j * CHUNK : (j + 1) * CHUNK])
            d_ref[at, :HEAD] = turn(dq * 0.125, cos_ref[at], sin_ref[at], True).astype(BF16)
    for copy in copies:
        copy.wait()
    for at in range(8):
        dk = turn(dk_ref[at].T, cos_ref[at], sin_ref[at], True)
        d_ref[at, HEAD : 2 * HEAD] = dk.astype(BF16)
        d_ref[at, 2 * HEAD :] = dv_ref[at].T.astype(BF16)
        rows = []
        for j in range(4):
            flat = inverse[4 * at + j]
            start = pl.multiple_of((flat & 1) * BLOCK, BLOCK)
            rows.append(xv_ref[flat // 2, pl.ds(start, BLOCK), :])
        normal, _ = normalise(jnp.concatenate(rows, 0).astype(F32))
        part = dot(d_ref[at], (normal * gain_ref[...]).astype(BF16))
        wt_ref[:192] = part if at == 0 else wt_ref[:192] + part
    for d in range(4):
        start = pl.multiple_of((d // 2) * 256 + ((place[9] ^ d) & 1) * 128, 128)
        columns = (near_ref if d % 2 == 0 else far_ref)[d // 2]
        part = dot(columns.T, obv_ref[pl.ds(start, 128), :])
        wt_ref[192:] = part if d == 0 else wt_ref[192:] + part
    grad_ref[...] = wt_ref[...].T.astype(BF16).reshape(8, 96, 384)
    for b in range(16):
        flat = inverse[b]
        upper = 15 - b
        lo = d_ref[b // 4, :, (b % 4) * BLOCK : (b % 4 + 1) * BLOCK].astype(F32)
        up = d_ref[4 + upper // 4, :, (upper % 4) * BLOCK : (upper % 4 + 1) * BLOCK].astype(F32)
        tile = jnp.concatenate([lo, up], 1)
        turned = jnp.concatenate([up, lo], 1)
        away = (flat // 8 - place[12]) & 3
        all_ref[away, (flat // 2) % 4] = jnp.where(flat % 2 == 0, tile, turned).astype(BF16)
    for k, ref in enumerate((out0_ref, out1_ref, out2_ref, out3_ref)):
        ref[...] = all_ref[k]


def run_backward(
    inverse, place, do, blocks, wide, gain, kept, cosine, sine, id_row, ob, columns
):
    return pl.pallas_call(
        backward_kernel,
        out_shape=(
            *(SHAPE((4, 3 * HEAD, 2 * BLOCK), BF16),) * 4,
            SHAPE((8, 96, 384), BF16),
        ),
        in_specs=[SMEM] * 2 + [VMEM] + [ANY] * 5 + [VMEM] * 10 + [ANY] + [VMEM] * 2,
        out_specs=(VMEM,) * 5,
        scratch_shapes=[
            pltpu.VMEM((CHUNKS, 3 * HEAD, CHUNK), BF16),
            pltpu.VMEM((CHUNKS, CHUNK, HEAD), F32),
            pltpu.VMEM((CHUNKS, CHUNK, HEAD), F32),
            pltpu.VMEM((CHUNKS, HEAD, CHUNK), BF16),
            pltpu.VMEM((CHUNKS, CHUNK, HEAD), BF16),
            pltpu.VMEM((384, WIDTH), F32),
            pltpu.VMEM((4, 4, 3 * HEAD, 2 * BLOCK), BF16),
            pltpu.VMEM((16, 128, WIDTH), BF16),
            pltpu.VMEM((2 * CHUNK, WIDTH), BF16),
            pltpu.SemaphoreType.DMA((10,)),
        ],
        compiler_params=pltpu.CompilerParams(vmem_limit_bytes=60 << 20),
        cost_estimate=cost(22.0),
        name="attention_backward",
    )(inverse, place, do, *blocks, wide, gain, *kept, cosine, sine, id_row, ob, *columns)


def pick(core, same, other):
    first = jnp.where(core == 0, same, other)
    return jnp.concatenate([first, jnp.where(core == 0, other, same)], 0)


def assemble(place, units_ref, sems, gu_ref=None, down_ref=None, wout_ref=None):
    copies = []
    parts = ((wout_ref, 144, 96), (gu_ref, 0, 96), (down_ref, 96, 48))
    for target, first, size in parts:
        if target is not None:
            for k in range(8):
                start = ((place[13] ^ (k % 2)) * 4 + k // 2) * size
                rows = target.at[pl.ds(pl.multiple_of(start, 16), size)]
                source = units_ref.at[k // 2, k % 2, first : first + size]
                copies.append(pltpu.make_async_copy(source, rows, sems.at[len(copies)]))
    for copy in copies:
        copy.start()

    def wait(first, last):
        for copy in copies[first:last]:
            copy.wait()

    return wait


def feed_kernel(
    place, own_ref, other_ref, n0_ref, n1_ref, f0_ref, f1_ref, gain_ref, units_ref,
    keep_ref, send_ref, h_ref, d_ref, a_ref, quad_ref, y_ref, wout_ref,
    own_v, other_v, x_v, z_v, gu_v, down_v, wout_v, ob_v, mid_v, h_v, d_v, a_v, keep_v, send_v, y_v,
    sems, unit_sems,
):
    core, member = place[8], place[9]
    started = []

    def copy(source, target):
        started.append(pltpu.make_async_copy(source, target, sems.at[len(started)]))
        started[-1].start()
        return started[-1]

    tiles_in = [copy(own_ref.at[:6], own_v), copy(other_ref.at[:6], other_v)]
    arrays = (n0_ref, n1_ref, f0_ref, f1_ref)
    x_in = [copy(ref.at[:2], x_v.at[k]) for k, ref in enumerate(arrays)]
    units_in = assemble(place, units_ref, unit_sems, gu_v, down_v, wout_v)
    z_in = [copy(ref.at[2:], z_v.at[k]) for k, ref in enumerate(arrays)]

    def rows(i):
        return slice(CHUNK * i, CHUNK * (i + 1))

    def block(ref, i):
        return pick(core, ref[2 * (i % 2), i // 2], ref[2 * (i % 2) + 1, i // 2])

    for part in tiles_in:
        part.wait()
    for i in range(4):
        at = (member // 2) ^ i
        for c in range(2):
            base = CHUNK * i + 128 * c
            for z in range(2):
                tiles = []
                for k in range(2):
                    for x in range(3):
                        mine, theirs = own_v[2 * x + z, 2 * at + c], other_v[2 * x + z, 2 * at + c]
                        tiles.append(jnp.where(core == k, mine, theirs))
                for pair in range(3):
                    left, right = tiles[2 * pair], tiles[2 * pair + 1]
                    lanes = slice(384 * z + 128 * pair, 384 * z + 128 * (pair + 1))
                    ob_v[base : base + BLOCK, lanes] = jnp.concatenate(
                        [left[:, :BLOCK], right[:, :BLOCK]], 1
                    )
                    ob_v[base + BLOCK : base + 128, lanes] = jnp.concatenate(
                        [left[:, BLOCK:], right[:, BLOCK:]], 1
                    )
    out = [copy(ob_v.at[: 2 * CHUNK], quad_ref)]
    for part in x_in:
        part.wait()
    units_in(0, 8)
    out.append(copy(wout_v, wout_ref))
    for i in range(4):
        middle = block(x_v, i).astype(F32) + dot(ob_v[rows(i)], wout_v[...])
        mid_v[rows(i)] = middle
        normal, _ = normalise(middle)
        h_v[rows(i)] = (normal * gain_ref[...]).astype(BF16)
        out.append(copy(h_v.at[rows(i)], h_ref.at[rows(i)]))
    y_v[...] = mid_v[pl.ds(pl.multiple_of(core * 128, 128), 128), :]
    out.append(copy(y_v, y_ref))
    for part in z_in:
        part.wait()
    units_in(8, 24)
    for i in range(4):
        gu = dot(h_v[rows(i)], gu_v[...])
        g, u = gu[:, :384], gu[:, 384:]
        da = dot(block(z_v, i), down_v[...], 1, 1)
        sigma = jax.nn.sigmoid(g)
        swish = g * sigma
        a_v[rows(i)] = (swish * u).astype(BF16)
        d_v[rows(i), :384] = (da * u * (sigma + swish * (1.0 - sigma))).astype(BF16)
        d_v[rows(i), 384:] = (da * swish).astype(BF16)
        out.append(copy(a_v.at[rows(i)], a_ref.at[rows(i)]))
        out.append(copy(d_v.at[rows(i)], d_ref.at[rows(i)]))
    for i in range(4):
        mid_v[rows(i)] = dot(d_v[rows(i)], gu_v[...], 1, 1)
        keep = pl.multiple_of(CHUNK * i + core * 128, 128)
        send = pl.multiple_of(CHUNK * i + 128 - core * 128, 128)
        keep_v[i] = mid_v[pl.ds(keep, 128), :].astype(BF16)
        send_v[i] = mid_v[pl.ds(send, 128), :].astype(BF16)
        out.append(copy(send_v.at[i], send_ref.at[i]))
        out.append(copy(keep_v.at[i], keep_ref.at[i]))
    for part in out:
        part.wait()


def run_feed(place, own, other, blocks, gain, units):
    rows = 4 * CHUNK
    scratch = [
        ((6, 8, BLOCK, 128), BF16),
        ((6, 8, BLOCK, 128), BF16),
        ((4, 2, 128, WIDTH), BF16),
        ((4, 2, 128, WIDTH), BF16),
        ((WIDTH, WIDTH), BF16),
        ((WIDTH // 2, WIDTH), BF16),
        ((WIDTH, WIDTH), BF16),
        ((rows, WIDTH), BF16),
        ((rows, WIDTH), F32),
        ((rows, WIDTH), BF16),
        ((rows, WIDTH), BF16),
        ((rows, WIDTH // 2), BF16),
        ((4, 128, WIDTH), BF16),
        ((4, 128, WIDTH), BF16),
        ((128, WIDTH), F32),
    ]
    return pl.pallas_call(
        feed_kernel,
        out_shape=(
            SHAPE((4, 128, WIDTH), BF16),
            SHAPE((4, 128, WIDTH), BF16),
            SHAPE((rows, WIDTH), BF16),
            SHAPE((rows, WIDTH), BF16),
            SHAPE((rows, WIDTH // 2), BF16),
            SHAPE((2 * CHUNK, WIDTH), BF16),
            SHAPE((128, WIDTH), F32),
            SHAPE((WIDTH, WIDTH), BF16),
        ),
        in_specs=[SMEM] + [ANY] * 6 + [VMEM, ANY],
        out_specs=(ANY,) * 8,
        scratch_shapes=[pltpu.VMEM(*shape) for shape in scratch]
        + [pltpu.SemaphoreType.DMA((40,)), pltpu.SemaphoreType.DMA((24,))],
        compiler_params=pltpu.CompilerParams(vmem_limit_bytes=60 << 20),
        cost_estimate=cost(40),
        name="feed",
    )(place, own, other, *blocks, gain, units)


def weights_kernel(
    place, h_ref, d_ref, a_ref, z0_ref, z1_ref, z2_ref, z3_ref, units_ref,
    out_ref, keep_ref, send_ref,
    h_v, d_v, a_v, dz_v, gu_v, gd_v, z_v, down_v, out_v, keep_v, send_v, sems, unit_sems,
):
    core = place[8]
    started = []

    def copy(source, target):
        started.append(pltpu.make_async_copy(source, target, sems.at[len(started)]))
        started[-1].start()
        return started[-1]

    def rows(i):
        return slice(2 * CHUNK * i, 2 * CHUNK * (i + 1))

    parts = []
    for i in range(2):
        parts.append([copy(h_ref.at[rows(i)], h_v.at[rows(i)]), copy(d_ref.at[rows(i)], d_v.at[rows(i)])])
        if i == 0:
            dz_in = [
                copy(ref.at[2:], dz_v.at[k]) for k, ref in enumerate((z0_ref, z1_ref, z2_ref, z3_ref))
            ]
            units_in = assemble(place, units_ref, unit_sems, down_ref=down_v)
        parts[i].append(copy(a_ref.at[rows(i)], a_v.at[rows(i)]))
    out = []
    for i in range(2):
        parts[i][0].wait()
        parts[i][1].wait()
        gu = dot(h_v[rows(i)], d_v[rows(i)], 0, 0)
        gu_v[...] = gu if i == 0 else gu_v[...] + gu
    for part in dz_in + [parts[0][2], parts[1][2]]:
        part.wait()
    units_in(0, 8)
    for i in range(2):
        dz = [pick(core, dz_v[0, i], dz_v[1, i]), pick(core, dz_v[2, i], dz_v[3, i])]
        gd = dot(a_v[rows(i)], jnp.concatenate(dz, 0), 0, 0)
        gd_v[...] = gd if i == 0 else gd_v[...] + gd
    for f in range(8):
        base = (2 * (f % 4) + f // 4) * 144
        out_v[base : base + 96] = gu_v[96 * f : 96 * (f + 1)].astype(BF16)
        out_v[base + 96 : base + 144] = gd_v[48 * f : 48 * (f + 1)].astype(BF16)
    out.append(copy(out_v, out_ref))
    for i in range(2):
        z_v[...] = dot(a_v[rows(i)], down_v[...])
        for j in range(2):
            keep = pl.multiple_of(256 * j + core * 128, 128)
            send = pl.multiple_of(256 * j + 128 - core * 128, 128)
            keep_v[2 * i + j] = z_v[pl.ds(keep, 128), :].astype(BF16)
            send_v[2 * i + j] = z_v[pl.ds(send, 128), :].astype(BF16)
    out += [copy(keep_v, keep_ref), copy(send_v, send_ref)]
    for part in out:
        part.wait()


def run_weights(place, h, d, a, blocks, units):
    rows = 4 * CHUNK
    scratch = [
        ((rows, WIDTH), BF16),
        ((rows, WIDTH), BF16),
        ((rows, WIDTH // 2), BF16),
        ((4, 2, 128, WIDTH), BF16),
        ((WIDTH, WIDTH), F32),
        ((WIDTH // 2, WIDTH), F32),
        ((2 * CHUNK, WIDTH), F32),
        ((WIDTH // 2, WIDTH), BF16),
        ((8 * 144, WIDTH), BF16),
        ((4, 128, WIDTH), BF16),
        ((4, 128, WIDTH), BF16),
    ]
    return pl.pallas_call(
        weights_kernel,
        out_shape=(SHAPE((8 * 144, WIDTH), BF16),) + (SHAPE((4, 128, WIDTH), BF16),) * 2,
        in_specs=[SMEM] + [ANY] * 8,
        out_specs=(ANY,) * 3,
        scratch_shapes=[pltpu.VMEM(*shape) for shape in scratch]
        + [pltpu.SemaphoreType.DMA((16,)), pltpu.SemaphoreType.DMA((8,))],
        compiler_params=pltpu.CompilerParams(vmem_limit_bytes=60 << 20),
        cost_estimate=cost(9),
        name="weights",
    )(place, h, d, a, *blocks, units)


def middle_kernel(
    place, p0_ref, p1_ref, p2_ref, p3_ref, y_ref, cot_ref, gain_ref, wout_ref,
    dy_ref, keep_ref, send_ref, do_ref, columns_ref,
):
    dh = sum(ref[...].astype(F32) for ref in (p0_ref, p1_ref, p2_ref, p3_ref))
    normal, scale = normalise(y_ref[...])
    dy = cot_ref[...].astype(F32) + norm_back(dh, normal, scale, gain_ref[...])
    dy_ref[...] = dy
    low = dy.astype(BF16)
    do = dot(wout_ref[...], low, 1, 1).astype(BF16)
    for t in range(4):
        for x in range(4):
            h = 3 * t + min(x, 2)
            do_ref[4 * x + t] = do[HEAD * h : HEAD * (h + 1)]
    for r in range(4):
        columns_ref[place[11] ^ r] = low[:, 192 * r : 192 * (r + 1)]
    keep_ref[...] = columns_ref[:2]
    send_ref[...] = columns_ref[2:]


def run_middle(place, parts, y, cotangent, gain, wout):
    return pl.pallas_call(
        middle_kernel,
        out_shape=(
            SHAPE((128, WIDTH), F32),
            *(SHAPE((2, 128, 192), BF16),) * 2,
            SHAPE((16, HEAD, 128), BF16),
        ),
        in_specs=[SMEM] + [VMEM] * 8,
        out_specs=(VMEM,) * 4,
        scratch_shapes=[
            pltpu.VMEM((4, 128, 192), BF16),
        ],
        compiler_params=pltpu.CompilerParams(vmem_limit_bytes=10 << 20),
        cost_estimate=cost(12.0),
        name="middle",
    )(place, *parts, y, cotangent, gain, wout)


def inputs_kernel(place, d0_ref, d1_ref, d2_ref, d3_ref, w_ref, keep_ref, send_ref, sum_ref):
    core, column = place[8], place[12]
    for c in range(4):
        for k, ref in enumerate((d0_ref, d1_ref, d2_ref, d3_ref)):
            x = (column - k) & 3
            at = jnp.minimum(x, 2) * HEAD
            w = jnp.concatenate(
                [w_ref[pl.ds(pl.multiple_of(base + at, HEAD), HEAD), :] for base in (0, 192, 384)],
                0,
            )
            part = jnp.where(x < 3, dot(ref[c], w, 0, 0), 0.0)
            sum_ref[c] = part if k == 0 else sum_ref[c] + part
    for z in range(2):
        keep_ref[z] = sum_ref[2 * z + core].astype(BF16)
        send_ref[z] = sum_ref[2 * z + 1 - core].astype(BF16)


def run_inputs(place, parts, w_rows):
    return pl.pallas_call(
        inputs_kernel,
        out_shape=(SHAPE((2, 128, WIDTH), BF16),) * 2,
        in_specs=[SMEM] + [VMEM] * 5,
        out_specs=(VMEM,) * 2,
        scratch_shapes=[pltpu.VMEM((4, 128, WIDTH), F32)],
        compiler_params=pltpu.CompilerParams(vmem_limit_bytes=12 << 20),
        cost_estimate=cost(3),
        name="inputs",
    )(place, *parts, w_rows)


def finish_feed_kernel(
    all_ref, gate_ref, up_ref, gain_ref, g_ref, u_ref, d_ref, n_ref,
    all_v, w_v, o_v, d_v, sems,
):
    started = []

    def copy(source, target):
        started.append(pltpu.make_async_copy(source, target, sems.at[len(started)]))
        started[-1].start()
        return started[-1]

    halves = [copy(all_ref.at[8 * h : 8 * h + 8], all_v.at[8 * h : 8 * h + 8]) for h in range(2)]
    weights = [copy(gate_ref, w_v.at[0]), copy(up_ref, w_v.at[1])]
    total = jnp.zeros((96, 1), F32)
    out = []
    for half, out_ref in enumerate((g_ref, u_ref)):
        halves[half].wait()
        tiles = [all_v[8 * half + m, :96] for m in range(8)]
        for f in range(8):
            block = jnp.concatenate([t[:, 48 * f : 48 * (f + 1)] for t in tiles], 1)
            lanes = slice(384 * f, 384 * (f + 1))
            o_v[half, :, lanes] = block.astype(F32)
        out.append(copy(o_v.at[half], out_ref))
        side = slice(384 * half, 384 * (half + 1))
        for m in range(8):
            d_v[48 * m : 48 * (m + 1), side] = all_v[8 * half + m, 96:].astype(F32)
    out.append(copy(d_v, d_ref))
    for half in range(2):
        weights[half].wait()
        total += jnp.sum(w_v[half].astype(F32) * o_v[half], axis=1, keepdims=True)
    n_ref[...] = jnp.broadcast_to(total, (96, 128)).T[:1] / gain_ref[...].astype(F32)
    for part in out:
        part.wait()


def run_finish_feed(whole, gate, up, gain):
    return pl.pallas_call(
        finish_feed_kernel,
        out_shape=(
            SHAPE((96, 3072), F32),
            SHAPE((96, 3072), F32),
            SHAPE((384, WIDTH), F32),
            SHAPE((1, 96), F32),
        ),
        in_specs=[ANY] * 3 + [VMEM],
        out_specs=(ANY,) * 3 + (VMEM,),
        scratch_shapes=[
            pltpu.VMEM((16, 144, 384), BF16),
            pltpu.VMEM((2, 96, 3072), BF16),
            pltpu.VMEM((2, 96, 3072), F32),
            pltpu.VMEM((384, WIDTH), F32),
            pltpu.SemaphoreType.DMA((8,)),
        ],
        compiler_params=pltpu.CompilerParams(vmem_limit_bytes=60 << 20),
        cost_estimate=cost(6),
        name="finish_feed",
    )(whole, gate, up, gain.reshape(1, 96))


def finish_heads_kernel(place, *refs):
    own_ref, other_ref = refs[:2]
    wq_ref, wk_ref, wv_ref, gain_ref, q_ref, k_ref, v_ref, o_ref, n_ref = refs[2:]
    core = place[8]
    tiles = {}
    for x in range(4):
        for z in range(2):
            mine, theirs = own_ref[2 * x + z], other_ref[2 * x + z]
            for k in range(2):
                tiles[x, 2 * z + k] = jnp.where(core == k, mine, theirs).astype(F32)
    total = jnp.zeros((96, 1), F32)
    for j, (w_ref, out_ref) in enumerate(((wq_ref, q_ref), (wk_ref, k_ref), (wv_ref, v_ref))):
        lanes = slice(HEAD * j, HEAD * (j + 1))
        whole = jnp.concatenate([tiles[h % 3, h // 3][:, lanes] for h in range(12)], 1)
        out_ref[...] = whole
        total += jnp.sum(w_ref[...].astype(F32) * whole, axis=1, keepdims=True)
    n_ref[...] = jnp.broadcast_to(total, (96, 128)).T[:1] / gain_ref[...].astype(F32)
    o_ref[...] = jnp.concatenate(
        [sum(tiles[x, t][:, 192:] for x in range(4)) for t in range(4)], 1
    )


def run_finish_heads(place, own, other, query, key, value, gain):
    return pl.pallas_call(
        finish_heads_kernel,
        out_shape=(SHAPE((96, WIDTH), F32),) * 4 + (SHAPE((1, 96), F32),),
        in_specs=[SMEM] + [VMEM] * 6,
        out_specs=(VMEM,) * 5,
        compiler_params=pltpu.CompilerParams(vmem_limit_bytes=12 << 20),
        cost_estimate=cost(8),
        name="finish_heads",
    )(place, own, other, query, key, value, gain.reshape(1, 96))


def fold_kernel(in_ref, out_ref):
    total = jnp.sum(in_ref[...].astype(F32), axis=0).astype(BF16)
    for k in range(8):
        out_ref[k] = total


def run_fold(parts):
    return pl.pallas_call(
        fold_kernel,
        out_shape=SHAPE(parts.shape, BF16),
        in_specs=[VMEM],
        out_specs=VMEM,
        compiler_params=pltpu.CompilerParams(vmem_limit_bytes=6 << 20),
        cost_estimate=cost(0.3),
        name="fold",
    )(parts)


def trade(value, distance):
    return lax.ppermute(value, "ctx", [(i, i ^ distance) for i in range(16)])


def pair_kernel(keep_ref, got_ref, *outs):
    for k, ref in enumerate(outs):
        ref[...] = (keep_ref[k].astype(F32) + got_ref[k].astype(F32)).astype(BF16)


def run_pair(keep, got):
    return pl.pallas_call(
        pair_kernel,
        out_shape=(SHAPE((128, WIDTH), BF16),) * 4,
        in_specs=[VMEM] * 2,
        out_specs=(VMEM,) * 4,
        compiler_params=pltpu.CompilerParams(vmem_limit_bytes=8 << 20),
        cost_estimate=cost(2),
        name="pair",
    )(keep, got)


def norm_back(grad_normed, normal_rows, inverse, gains):
    scaled = grad_normed * gains
    return inverse * (scaled - normal_rows * jnp.mean(scaled * normal_rows, axis=-1, keepdims=True))


def local(
    tokens, block_table, seq_ids, w_query, w_key, w_value, w_out, w_gate, w_up, w_down,
    gain_attn, gain_mlp, cotangent,
):
    index = lax.axis_index("ctx")
    shard = lax.axis_index("fsdp")
    rank, column = index % 4, index // 4
    core, member, group = index % 2, index % 8, index // 8

    rings = [[0, 1, 2, 3], [4, 5, 6, 7]]

    blocks = block_table.reshape(-1)
    numbers = jnp.arange(32, dtype=jnp.int32)
    inverse = jnp.sum(
        jnp.where(blocks[None, :] == numbers[:, None], numbers[None, :], 0), axis=1
    ).astype(jnp.int32)
    frequency = jnp.power(THETA, -(jnp.arange(HALF, dtype=F32) * 2.0) / HEAD)
    own_blocks = lax.dynamic_slice_in_dim(blocks, 8 * column, 8)
    places = (own_blocks[:, None] * BLOCK + jnp.arange(BLOCK, dtype=jnp.int32)).reshape(4, 1, 128)
    angles = places.astype(F32) * frequency[None, :, None]
    place = jnp.stack(
        [(shard // 4 ^ dz) * 4 + (shard + dy) % 4 for dz, dy in RING]
        + [core, member, group, rank, column, shard // 4, index]
    ).astype(jnp.int32)

    units = run_pack_heads(w_query, w_key, w_value, gain_attn, gain_mlp)
    w_heads = lax.all_to_all(units, "fsdp", 0, 0).reshape(WIDTH, 640)
    x_own = after(tokens[0], units)
    x_blocks = [tokens[0], trade(x_own, 1)]
    unit, both = run_pack_units(w_gate, w_up, w_down, w_out, x_blocks[1])
    x_blocks.append(trade(x_own, 2))
    across = lax.ppermute(after(unit, x_blocks[2]), "fsdp", [(i, i ^ 4) for i in range(8)])
    own = after(jnp.stack([x_own, cotangent[0]]), x_blocks[1])
    own = [own, trade(own, 4), trade(own[0], 8)]
    x_blocks.append(trade(after(x_blocks[2], own, unit), 1))
    w_heads, angles = lax.optimization_barrier((w_heads, (jnp.cos(angles), jnp.sin(angles))))
    *tiles, w_rows = run_project(place, w_heads, x_blocks, *angles)
    gains = w_rows[576:578].astype(F32)
    gain_one, gain_two = gains[:1], gains[1:]

    ids = after(seq_ids[0], w_rows).reshape(32, BLOCK)
    hits = (inverse[16:, None] == numbers[None, :]).astype(jnp.int32)
    ids = jnp.sum(hits[:, :, None] * ids[None], axis=1).reshape(HALF_SEQ)
    id_row = ids.reshape(1, HALF_SEQ)
    angles = after(jnp.arange(SEQ, dtype=F32), w_rows).reshape(CHUNKS, 1, CHUNK)
    angles = angles * frequency[None, :, None]
    cosine, sine = jnp.cos(angles), jnp.sin(angles)

    for k in range(1, 4):
        tiles[k] = lax.ppermute(
            tiles[k], "ctx", [(i, (i + 4 * k) % 16) for i in range(16)]
        )
    units = lax.all_gather(
        both.at[1].set(after(across, w_rows)), "fsdp", axis=0, axis_index_groups=rings
    )
    near = jnp.stack([own[0][0], own[1][0], own[0][1], own[1][1]])
    far = trade(after(near, w_rows), 2)
    tiles, cosine, sine = lax.optimization_barrier((tiles, cosine, sine))
    o_tiles, *kept = run_forward(inverse, place, tiles, id_row)
    o_own = lax.all_to_all(o_tiles, "ctx", 0, 0, axis_index_groups=SAME_CORE)
    blocks = [near, trade(near, 1), far, trade(far, 1)]
    o_other = trade(after(o_own, blocks), 1)
    eights = [list(range(8)), list(range(8, 16))]
    wide = lax.all_gather(after(own[2], o_tiles), "ctx", axis=0, axis_index_groups=eights)

    keep, send, h2, dgu, a, ob, middle, wout = run_feed(
        place, o_own, o_other, blocks, gain_two, units
    )
    pair = run_pair(keep, trade(send, 1))
    parts = [pair[0]] + [trade(pair[k], 2 * k) for k in (1, 2, 3)]

    ff, z_keep, z_send = run_weights(place, after(h2, pair), dgu, a, blocks, units)
    dy1, *columns, do = run_middle(place, after(parts, ff), middle, cotangent[0], gain_two, wout)
    ff = lax.psum_scatter(
        ff, "fsdp", scatter_dimension=0, tiled=True, axis_index_groups=rings
    )
    z = run_pair(z_keep, trade(after(z_send, do), 1))
    z = [z[0]] + [trade(z[k], 2 * k) for k in (1, 2, 3)]
    do = lax.all_to_all(do, "ctx", 0, 0)
    columns = jnp.stack([columns[0], trade(columns[1], 2)], 1)
    columns = [columns[0], trade(columns[1], 1)]
    *d_parts, small = run_backward(
        inverse, place, do, blocks, wide, gain_one, kept, cosine, sine, id_row, ob, columns
    )
    small, ff, z = lax.optimization_barrier((small, ff, z))
    small = lax.all_to_all(small, "fsdp", 0, 0)
    far = shard // 4 == 1
    away = jnp.where(far, ff[:144], ff[144:])
    ff = jnp.where(far, ff[144:], ff[:144])

    def half(value, flip):
        return jnp.where((group == 1) ^ flip, value[:, 384:], value[:, :384])

    def across(value, flip, shift):
        pairs = [(8 * c + f, 8 * (c ^ shift) + (f ^ flip)) for f in range(8) for c in range(16)]
        return lax.ppermute(value, ("ctx", "fsdp"), pairs)

    halves = half(ff, False), half(ff, True), half(away, False), half(away, True)
    parts = [
        halves[0], across(halves[1], 0, 8), across(halves[2], 4, 0), across(halves[3], 4, 8)
    ]
    ff = sum(part.astype(F32) for part in parts).astype(BF16)
    ff = lax.all_gather(ff, "ctx", axis=0)

    folded = run_fold(small)
    for k in range(1, 4):
        d_parts[k] = lax.ppermute(
            after(d_parts[k], folded), "ctx", [(i, (i + 4 * k) % 16) for i in range(16)]
        )
    small = lax.all_to_all(folded, "ctx", 0, 0, axis_index_groups=SAME_CORE)
    total_query, total_key, total_value, total_out, total_gain_one = run_finish_heads(
        place, small, trade(small, 1), w_query, w_key, w_value, gain_attn
    )

    keep, send = run_inputs(place, d_parts, w_rows)
    summed = keep.astype(F32) + trade(send, 1).astype(F32)
    low = rank // 2 == 0
    keep = jnp.where(low, summed[0], summed[1])
    send = jnp.where(low, summed[1], summed[0]).astype(BF16)
    dh1 = keep + trade(send, 2).astype(F32)
    normal_one, inverse_one = normalise(tokens[0].astype(F32))
    grad_stream = dy1 + norm_back(dh1, normal_one, inverse_one, gain_one)
    result = middle + sum(part.astype(F32) for part in z)
    grad_stream, result = grad_stream.astype(BF16), result.astype(BF16)
    ff, grad_stream, result, total_query = lax.optimization_barrier(
        (ff, grad_stream, result, total_query)
    )
    total_gate, total_up, total_down, total_gain_two = run_finish_feed(
        ff, w_gate, w_up, gain_mlp
    )

    return (
        result[None],
        grad_stream[None],
        total_query,
        total_key,
        total_value,
        total_out,
        total_gate,
        total_up,
        total_down,
        total_gain_one.reshape(96),
        total_gain_two.reshape(96),
    )


def solution(mesh):
    rows = P("fsdp", "ctx", None)
    weight = P("fsdp", None)
    return jax.shard_map(
        local,
        mesh=mesh,
        in_specs=(rows, P(), weight) + (weight,) * 7 + (P("fsdp"), P("fsdp"), rows),
        out_specs=(rows, rows) + (weight,) * 7 + (P("fsdp"), P("fsdp")),
        check_vma=False,
    )
```
